32 devices in a mesh: lat: 4 (over y, core), lon: 8 (over z, x).
Axes of the slice: x: 2, y: 2, z: 4, core: 2. Of those that a mesh axis runs over, the one named last changes fastest.
Arguments:
- tendency: bfloat16 [2, 16, 512, 2048], P(None, None, 'lat', 'lon'), may hold values from -6 to 6
- thickness: float32 [16], replicated, may hold values from 0.03 to 0.3
- level_count: int32 [512, 2048], P('lat', 'lon'), may hold values from 0 to 16, as said below
- block_mask: int32 [32, 8], P('lat', 'lon'), may hold values from 0 to 1, as said below
- owner: int32 [32, 8], P('lat', 'lon'), may hold values from -1 to 7, as said below
- inertia: float32 [512, 2048], P('lat', 'lon'), may hold values from 0.2 to 2
Outputs:
- barotropic_forcing: float32 [4, 8, 8, 2, 16, 256], P('lat', 'lon')
- pressure: float32 [512, 2048], P('lat', 'lon')
- residual: float32 [512, 2048], P('lat', 'lon')
The draws below stay inside these ranges and needn't reach their ends.
Inputs may be any that keep to these rules, and one draw needn't show every extreme that they name: `block_mask`: each latitude index holds exactly 48 ocean blocks among its 64. -1 exactly on land blocks; on ocean blocks the owner's longitude index within the same latitude index. A device's ocean blocks go to distinct owners, and every owner receives exactly 6 blocks. `level_count`: 0 exactly on the cells of land blocks, 1 to 16 on ocean cells; 16 is reached on every ocean block.
All inputs are finite; a program needn't handle non-finite values.
Results may differ from the reference program's by a relative error of at most 0.0003.
Values may be sent and summed in bfloat16 or wider, within the bound.
No kernel may reach another device: no remote copies, remote signals or barrier semaphores. Data moves between devices by JAX's collectives and lax.ppermute only.
A program may use at most 64 MiB of HBM per device.

```python
import math
import jax
import jax.numpy as jnp
from jax import lax

CX = 256
LEVELS = 16
ITERS = 4
SUB = 8
BROWS = 16
CAP = 6
NY = 512
NX = 2048
BLOCK_ROWS = 32
BLOCK_COLS = 8
N_LAT = 4
N_LON = 8


def ocean_blocks(key):
    groups = BLOCK_ROWS // SUB
    subkeys = jax.random.split(key, groups)
    orders = jax.vmap(lambda subkey: jax.random.permutation(subkey, BLOCK_COLS * SUB))(subkeys)
    ocean_flag = (orders < BLOCK_COLS * CAP).astype(jnp.int32)
    rank_index = jnp.cumsum(ocean_flag, axis=1) - 1
    return (ocean_flag, rank_index)


def to_grid(values):
    groups = BLOCK_ROWS // SUB
    return values.reshape(groups, BLOCK_COLS, SUB).transpose(0, 2, 1).reshape(BLOCK_ROWS, BLOCK_COLS)


def draw_block_mask(key, part):
    ocean_flag, rank_index = ocean_blocks(key)
    return to_grid(ocean_flag).astype(jnp.int32)


def draw_owner(key, part):
    ocean_flag, rank_index = ocean_blocks(key)
    key = jax.random.fold_in(key, 11)
    groups = BLOCK_ROWS // SUB
    offset = jax.random.randint(key, (groups, 1), 0, BLOCK_COLS)
    target = jnp.where(ocean_flag == 1, (rank_index + offset) % BLOCK_COLS, -1)
    return to_grid(target).astype(jnp.int32)


def draw_level_count(key, part):
    ocean_flag, rank_index = ocean_blocks(key)
    key = jax.random.fold_in(key, 13)
    grid = to_grid(ocean_flag)
    ocean_cells = jnp.repeat(jnp.repeat(grid, BROWS, axis=0), CX, axis=1)
    depth = jax.random.randint(key, (NY, NX), 1, LEVELS + 1)
    columns = jnp.arange(NX)[None, :]
    depth = jnp.where(columns % CX == 0, LEVELS, depth)
    return (depth * ocean_cells).astype(jnp.int32)


def block_scale(stream_key, dims, cuts, low, largest):
    factor_of, own = 1.0, jax.random.fold_in(stream_key, 6)
    for dim, parts in cuts:
        draws = jnp.exp(jax.random.uniform(jax.random.fold_in(own, dim), (parts,), jnp.float32, low / len(cuts), largest / len(cuts)))
        factor_of = factor_of * jnp.repeat(draws, dims[dim] // parts).reshape([-1 if axis == dim else 1 for axis in range(len(dims))])
    return factor_of


def gaussian(key, shape, scale, most, shards=(), dtype=jnp.bfloat16):
    drawn = jax.random.normal(key, shape, jnp.float32) * scale
    if len(shards) > 0:
        drawn = block_scale(key, shape, shards, -0.22, 0.18) * drawn
    return jnp.clip(drawn, min=-most, max=most).astype(dtype)


def setup_inputs(seed: int = 0) -> dict:
    seeds = jax.random.split(jax.random.key(seed), 7)
    return {
        "tendency": gaussian(seeds[0], (2, LEVELS, NY, NX), 1.0, 6.0, ((2, 4), (3, 8))),
        "thickness": jnp.clip(jnp.exp(jax.random.uniform(seeds[1], (LEVELS,), jnp.float32, math.log(0.03), math.log(0.3))), 0.03, 0.3),
        "level_count": draw_level_count(jax.random.fold_in(seeds[6], 71), 0),
        "block_mask": draw_block_mask(jax.random.fold_in(seeds[6], 71), 0),
        "owner": draw_owner(jax.random.fold_in(seeds[6], 71), 0),
        "inertia": jnp.clip(jnp.exp(math.log(2.0) - 2.3025851 * jax.random.uniform(seeds[5], (NY, NX), jnp.float32) ** block_scale(seeds[5], (NY, NX), ((0, 4), (1, 8)), -0.2, 0.2)), 0.2, 2.0),
    }


OFFSETS = [(-1, -1), (-1, 0), (-1, 1), (0, -1), (0, 1), (1, -1), (1, 0), (1, 1)]


def wrap_pad(field):
    padded = jnp.pad(field, ((1, 1), (0, 0)))
    return jnp.concatenate([padded[:, -1:], padded, padded[:, :1]], axis=1)


def neighbour(padded, row_step, col_step, total_rows, total_cols):
    return padded[1 + row_step:1 + row_step + total_rows, 1 + col_step:1 + col_step + total_cols]


def stencil(column_depth):
    total_rows, total_cols = column_depth.shape
    padded = wrap_pad(column_depth)
    weights = []
    for row_step, col_step in OFFSETS:
        factor = 1.0 if row_step * col_step == 0 else 0.5
        beside = neighbour(padded, row_step, col_step, total_rows, total_cols)
        weights.append(0.5 * factor * (column_depth + beside))
    return weights


def operate(field, weights, inertia):
    total_rows, total_cols = field.shape
    padded = wrap_pad(field)
    result = inertia * field
    for weight_map, (row_step, col_step) in zip(weights, OFFSETS):
        result = result + weight_map * (field - neighbour(padded, row_step, col_step, total_rows, total_cols))
    return result


def reference(tendency, thickness, level_count, block_mask, owner, inertia):
    forcing = jnp.zeros(tendency.shape[:1] + tendency.shape[2:], jnp.float32)
    column_depth = jnp.zeros(level_count.shape, jnp.float32)
    for level in range(LEVELS):
        live = level < level_count
        forcing = forcing + jnp.where(live[None], thickness[level] * tendency[:, level].astype(jnp.float32), 0.0)
        column_depth = column_depth + jnp.where(live, thickness[level], 0.0)
    blocked = forcing.reshape(2, N_LAT, SUB, BROWS, N_LON, CX)
    owner_grid = owner.reshape(N_LAT, SUB, N_LON)
    targets = jnp.arange(N_LON).astype(jnp.int32)
    holds = (owner_grid[:, None] == targets[None, :, None, None]).astype(jnp.float32)
    barotropic_forcing = jnp.einsum("iobs,cibrsx->ioscrx", holds, blocked, precision=lax.Precision.HIGHEST)
    ocean_cells = jnp.repeat(jnp.repeat(block_mask.astype(jnp.float32), BROWS, axis=0), CX, axis=1)
    east_west = jnp.roll(forcing[0], -1, axis=1) - jnp.roll(forcing[0], 1, axis=1)
    northward = jnp.pad(forcing[1], ((1, 1), (0, 0)))
    source = 0.5 * (east_west + northward[2:] - northward[:-2]) * ocean_cells
    weights = stencil(column_depth)
    diag = inertia + sum(weights)
    pressure = jnp.zeros_like(source)
    residual = source
    scaled = residual / diag
    direction = scaled
    norm_now = jnp.sum(residual * scaled)
    for iteration in range(ITERS):
        image = operate(direction, weights, inertia)
        alpha = norm_now / jnp.sum(direction * image)
        pressure = pressure + alpha * direction
        residual = residual - alpha * image
        scaled = residual / diag
        norm_next = jnp.sum(residual * scaled)
        direction = scaled + (norm_next / norm_now) * direction
        norm_now = norm_next
    return barotropic_forcing, pressure, residual
```

```python
import functools

import jax
import jax.numpy as jnp
from jax import lax
from jax.experimental import pallas as pl
from jax.experimental.pallas import tpu as pltpu
from jax.sharding import PartitionSpec as P

STEPS = 4
RIM = STEPS + 1
ROWS = 8
LANES = 128
CHUNK = 32
FIELDS = 4
SUMS = 16
VMEM_BYTES = 16 * 1024 * 1024


def integrate_kernel(
    thick_ref, owner_ref, count_ref, inertia_ref, tend_ref, fields_ref, head_ref, tail_ref, sent_ref
):
    step = pl.program_id(0)
    levels = tend_ref.shape[1]
    chunk = count_ref.shape[0]
    span = sent_ref.shape[2]
    count = count_ref[...]
    first = jnp.zeros(count.shape, jnp.float32)
    second = jnp.zeros(count.shape, jnp.float32)
    depth = jnp.zeros(count.shape, jnp.float32)
    for level in range(levels):
        layer = jnp.where(count > level, thick_ref[level], 0.0)
        depth = depth + layer
        first = first + layer * tend_ref[0, level].astype(jnp.float32)
        second = second + layer * tend_ref[1, level].astype(jnp.float32)
    inertia = inertia_ref[...]
    for place, values in enumerate((first, second, depth, inertia)):
        fields_ref[place] = values

    @pl.when(step == 0)
    def _():
        sent_ref[...] = jnp.zeros(sent_ref.shape, jnp.float32)
        for place, values in enumerate((first, second, depth, inertia)):
            head_ref[place] = values[:ROWS]

    @pl.when(step == pl.num_programs(0) - 1)
    def _():
        for place, values in enumerate((first, second, depth, inertia)):
            tail_ref[place] = values[chunk - ROWS :]

    for part in range(chunk // span):
        target = owner_ref[step * (chunk // span) + part]

        @pl.when(target >= 0)
        def _(target=target, part=part):
            rows = slice(part * span, (part + 1) * span)
            sent_ref[target, 0] = first[rows]
            sent_ref[target, 1] = second[rows]


def integrate(tendency, thickness, level_count, owner, inertia, lon_count):
    components, levels, rows, cols = tendency.shape
    span = rows // owner.shape[0]
    chunk = max(CHUNK, span)
    whole = lambda step: (0, 0, 0)
    f32 = jnp.float32
    return pl.pallas_call(
        integrate_kernel,
        grid=(rows // chunk,),
        in_specs=[
            pl.BlockSpec(memory_space=pltpu.SMEM),
            pl.BlockSpec(memory_space=pltpu.SMEM),
            pl.BlockSpec((chunk, cols), lambda step: (step, 0)),
            pl.BlockSpec((chunk, cols), lambda step: (step, 0)),
            pl.BlockSpec((components, levels, chunk, cols), lambda step: (0, 0, step, 0)),
        ],
        out_specs=[
            pl.BlockSpec((FIELDS, chunk, cols), lambda step: (0, step, 0)),
            pl.BlockSpec((FIELDS, ROWS, cols), whole),
            pl.BlockSpec((FIELDS, ROWS, cols), whole),
            pl.BlockSpec((lon_count, components, span, cols), lambda step: (0, 0, 0, 0)),
        ],
        out_shape=[
            jax.ShapeDtypeStruct((FIELDS, rows, cols), f32),
            jax.ShapeDtypeStruct((FIELDS, ROWS, cols), f32),
            jax.ShapeDtypeStruct((FIELDS, ROWS, cols), f32),
            jax.ShapeDtypeStruct((lon_count, components, span, cols), f32),
        ],
        compiler_params=pltpu.CompilerParams(vmem_limit_bytes=VMEM_BYTES),
        cost_estimate=pl.CostEstimate(
            flops=6 * components * levels * rows * cols,
            bytes_accessed=2 * components * levels * rows * cols,
            transcendentals=0,
        ),
        name="integrate",
    )(thickness, owner, level_count, inertia, tendency)


def edges_kernel(fields_ref, north_ref, south_ref, out_ref):
    rows = fields_ref.shape[1]
    cols = fields_ref.shape[2]
    half = LANES // 2
    for top, size, ref in ((0, ROWS, north_ref), (ROWS, rows, fields_ref), (ROWS + rows, ROWS, south_ref)):
        lane = lax.broadcasted_iota(jnp.int32, (size, LANES), 1)
        packed = jnp.zeros((size, LANES), jnp.float32)
        for place in range(FIELDS):
            west = ref[place, :, :LANES]
            east = ref[place, :, cols - LANES :]
            at = place * RIM
            west = pltpu.roll(west, at, 1) if at else west
            packed = jnp.where((lane >= at) & (lane < at + RIM), west, packed)
            at = half + place * RIM
            east = pltpu.roll(east, (at + RIM) % LANES, 1)
            packed = jnp.where((lane >= at) & (lane < at + RIM), east, packed)
        out_ref[top : top + size] = packed


def edges(fields, north, south):
    rows = fields.shape[1] + 2 * ROWS
    return pl.pallas_call(
        edges_kernel,
        out_shape=jax.ShapeDtypeStruct((rows, LANES), jnp.float32),
        compiler_params=pltpu.CompilerParams(vmem_limit_bytes=VMEM_BYTES),
        name="edges",
    )(fields, north, south)


def smooth(field):
    rows, cols = field.shape
    tall = field + 0.5 * (pltpu.roll(field, 1, 0) + pltpu.roll(field, rows - 1, 0))
    return tall + 0.5 * (pltpu.roll(tall, 1, 1) + pltpu.roll(tall, cols - 1, 1))


def krylov_kernel(fields_ref, north_ref, south_ref, east_ref, west_ref, w_ref, mw_ref, sums_ref):
    rows = fields_ref.shape[1]
    cols = fields_ref.shape[2]
    tall = rows + 2 * ROWS
    wide = cols + LANES
    half = LANES // 2
    lane = lax.broadcasted_iota(jnp.int32, (tall, LANES), 1)
    from_east = east_ref[...]
    from_west = west_ref[...]
    padded = []
    for place in range(FIELDS):
        middle = jnp.concatenate([north_ref[place], fields_ref[place], south_ref[place]], axis=0)
        at = place * RIM
        high = pltpu.roll(from_east, LANES - at, 1) if at else from_east
        low = pltpu.roll(from_west, half - RIM - at, 1)
        side = jnp.where(lane < RIM, high, jnp.where(lane >= LANES - RIM, low, 0.0))
        padded.append(jnp.concatenate([middle, side], axis=1))
    first, second, depth, inertia = padded
    inside = inertia > 0.0
    east_west = pltpu.roll(first, wide - 1, 1) - pltpu.roll(first, 1, 1)
    north_south = pltpu.roll(second, tall - 1, 0) - pltpu.roll(second, 1, 0)
    source = jnp.where(depth > 0.0, 0.5 * (east_west + north_south), 0.0)
    diag = inertia + 2.0 * depth + smooth(depth)
    inverse = jnp.where(inside, 1.0 / jnp.where(inside, diag, 1.0), 0.0)
    own = (slice(ROWS, ROWS + rows), slice(0, cols))
    scaled = source
    mws = [scaled[own]]
    ws = []
    vector = scaled * inverse
    for step in range(STEPS):
        ws.append(vector[own])
        weighed = depth * vector
        scaled = depth * smooth(vector) + smooth(weighed) - 2.0 * weighed
        mws.append(scaled[own])
        vector = scaled * inverse
    for place, values in enumerate(ws):
        w_ref[place] = values
    for place, values in enumerate(mws):
        mw_ref[place] = values
    images = [mws[place] - mws[place + 1] for place in range(STEPS)]
    pairs = [ws[place] * mws[0] for place in range(STEPS)]
    for low in range(STEPS):
        for high in range(low, STEPS):
            pairs.append(ws[low] * images[high])
    sums_ref[...] = jnp.zeros(sums_ref.shape, jnp.float32)
    for place, product in enumerate(pairs):
        line = jnp.sum(product, axis=0, keepdims=True)
        total = line[:, :LANES]
        for start in range(LANES, cols, LANES):
            total = total + line[:, start : start + LANES]
        sums_ref[place : place + 1, :] = total


def krylov(fields, north, south, east, west):
    _, rows, cols = fields.shape
    f32 = jnp.float32
    return pl.pallas_call(
        krylov_kernel,
        out_shape=[
            jax.ShapeDtypeStruct((STEPS, rows, cols), f32),
            jax.ShapeDtypeStruct((STEPS + 1, rows, cols), f32),
            jax.ShapeDtypeStruct((SUMS, LANES), f32),
        ],
        compiler_params=pltpu.CompilerParams(vmem_limit_bytes=VMEM_BYTES),
        name="krylov",
    )(fields, north, south, east, west)


def combine_kernel(sums_ref, w_ref, mw_ref, pressure_ref, residual_ref):
    totals = jnp.sum(sums_ref[...], axis=1, keepdims=True)
    entry = lambda place: totals[place : place + 1, :]
    right = [entry(place) for place in range(STEPS)]
    matrix = {}
    place = STEPS
    for low in range(STEPS):
        for high in range(low, STEPS):
            matrix[low, high] = entry(place)
            place += 1
    for pivot in range(STEPS):
        inverse = 1.0 / matrix[pivot, pivot]
        for row in range(pivot + 1, STEPS):
            factor = matrix[pivot, row] * inverse
            for col in range(row, STEPS):
                matrix[row, col] = matrix[row, col] - factor * matrix[pivot, col]
            right[row] = right[row] - factor * right[pivot]
        matrix[pivot, pivot] = inverse
    for pivot in reversed(range(STEPS)):
        for col in range(pivot + 1, STEPS):
            right[pivot] = right[pivot] - matrix[pivot, col] * right[col]
        right[pivot] = right[pivot] * matrix[pivot, pivot]
    pressure = right[0] * w_ref[0]
    residual = mw_ref[0] - right[0] * (mw_ref[0] - mw_ref[1])
    for place in range(1, STEPS):
        pressure = pressure + right[place] * w_ref[place]
        residual = residual - right[place] * (mw_ref[place] - mw_ref[place + 1])
    pressure_ref[...] = pressure
    residual_ref[...] = residual


def combine(sums, w, mw):
    shape = jax.ShapeDtypeStruct(w.shape[1:], jnp.float32)
    return pl.pallas_call(
        combine_kernel,
        out_shape=[shape, shape],
        compiler_params=pltpu.CompilerParams(vmem_limit_bytes=VMEM_BYTES),
        name="combine",
    )(sums, w, mw)


def total_over(values, axis):
    count = lax.axis_size(axis)
    if count & (count - 1):
        return lax.psum(values, axis)
    shift = 1
    while shift < count:
        pairs = [(place, place ^ shift) for place in range(count)]
        values = values + lax.ppermute(values, axis, pairs)
        shift *= 2
    return values


def on_device(tendency, thickness, level_count, block_mask, owner, inertia):
    lat_count = lax.axis_size("lat")
    lon_count = lax.axis_size("lon")
    fields, head, tail, sent = integrate(
        tendency, thickness, level_count, owner[:, 0], inertia, lon_count
    )
    south_pairs = [(place, place + 1) for place in range(lat_count - 1)]
    north_pairs = [(place + 1, place) for place in range(lat_count - 1)]
    north = lax.ppermute(tail, "lat", south_pairs)
    south = lax.ppermute(head, "lat", north_pairs)
    packed = edges(fields, north, south)
    east = lax.ppermute(packed, "lon", [((p + 1) % lon_count, p) for p in range(lon_count)])
    west = lax.ppermute(packed, "lon", [(p, (p + 1) % lon_count) for p in range(lon_count)])
    held = lax.all_to_all(sent, "lon", split_axis=0, concat_axis=0, tiled=True)
    w, mw, sums = krylov(fields, north, south, east, west)
    sums = total_over(total_over(sums, "lat"), "lon")
    pressure, residual = combine(sums, w, mw)
    return (held.reshape((1, 1) + held.shape), pressure, residual)


def solution(mesh):
    return jax.shard_map(
        on_device,
        mesh=mesh,
        in_specs=(
            P(None, None, "lat", "lon"),
            P(),
            P("lat", "lon"),
            P("lat", "lon"),
            P("lat", "lon"),
            P("lat", "lon"),
        ),
        out_specs=(P("lat", "lon", None, None, None, None), P("lat", "lon"), P("lat", "lon")),
        check_vma=False,
    )
```

```python
import functools

import jax
import jax.numpy as jnp
from jax import lax
from jax.experimental import pallas as pl
from jax.experimental.pallas import tpu as pltpu
from jax.sharding import PartitionSpec as P

STEPS = 4
RIM = STEPS + 1
ROWS = 8
LANES = 128
CHUNK = 32
FIELDS = 4
VMEM_BYTES = 16 * 1024 * 1024


def integrate_kernel(
    thick_hbm,
    owner_hbm,
    count_hbm,
    inertia_hbm,
    tend_hbm,
    fields_ref,
    head_ref,
    tail_ref,
    sent_ref,
    thick_ref,
    owner_ref,
    count_ref,
    inertia_ref,
    tend_ref,
    small_sems,
    chunk_sems,
):
    levels, rows = tend_hbm.shape[1:3]
    span = sent_ref.shape[2]
    chunk = max(CHUNK, span)
    small = [
        pltpu.make_async_copy(source, target, small_sems.at[place])
        for place, (source, target) in enumerate(
            (
                (thick_hbm, thick_ref),
                (owner_hbm, owner_ref),
                (count_hbm, count_ref),
                (inertia_hbm, inertia_ref),
            )
        )
    ]
    large = []
    for place in range(rows // chunk):
        part = pl.ds(place * chunk, chunk)
        large.append(
            pltpu.make_async_copy(
                tend_hbm.at[:, :, part], tend_ref.at[:, :, part], chunk_sems.at[place]
            )
        )
    for copy in small + large:
        copy.start()
    sent_ref[...] = jnp.zeros(sent_ref.shape, jnp.float32)
    for copy in small:
        copy.wait()
    for place, copy in enumerate(large):
        part = slice(place * chunk, (place + 1) * chunk)
        copy.wait()
        count = count_ref[part]
        first = jnp.zeros(count.shape, jnp.float32)
        second = jnp.zeros(count.shape, jnp.float32)
        depth = jnp.zeros(count.shape, jnp.float32)
        for level in range(levels):
            layer = jnp.where(count > level, thick_ref[level], 0.0)
            depth = depth + layer
            first = first + layer * tend_ref[0, level, part].astype(jnp.float32)
            second = second + layer * tend_ref[1, level, part].astype(jnp.float32)
        inertia = inertia_ref[part]
        for field, values in enumerate((first, second, depth, inertia)):
            fields_ref[field, part] = values
            if place == 0:
                head_ref[field] = values[:ROWS]
            if place == len(large) - 1:
                tail_ref[field] = values[chunk - ROWS :]
        for piece in range(chunk // span):
            target = owner_ref[place * (chunk // span) + piece]

            @pl.when(target >= 0)
            def _(target=target, piece=piece, first=first, second=second):
                rows_here = slice(piece * span, (piece + 1) * span)
                sent_ref[target, 0] = first[rows_here]
                sent_ref[target, 1] = second[rows_here]


def integrate(tendency, thickness, level_count, owner, inertia, lon_count):
    components, levels, rows, cols = tendency.shape
    span = rows // owner.shape[0]
    f32 = jnp.float32
    return pl.pallas_call(
        integrate_kernel,
        in_specs=[pl.BlockSpec(memory_space=pltpu.HBM)] * 5,
        out_shape=[
            jax.ShapeDtypeStruct((FIELDS, rows, cols), f32),
            jax.ShapeDtypeStruct((FIELDS, ROWS, cols), f32),
            jax.ShapeDtypeStruct((FIELDS, ROWS, cols), f32),
            jax.ShapeDtypeStruct((lon_count, components, span, cols), f32),
        ],
        scratch_shapes=[
            pltpu.SMEM(thickness.shape, f32),
            pltpu.SMEM(owner.shape, jnp.int32),
            pltpu.VMEM(level_count.shape, jnp.int32),
            pltpu.VMEM(inertia.shape, f32),
            pltpu.VMEM(tendency.shape, tendency.dtype),
            pltpu.SemaphoreType.DMA((4,)),
            pltpu.SemaphoreType.DMA((rows // max(CHUNK, span),)),
        ],
        cost_estimate=pl.CostEstimate(
            flops=6 * components * levels * rows * cols,
            bytes_accessed=2 * components * levels * rows * cols,
            transcendentals=0,
        ),
        name="integrate",
    )(thickness, owner, level_count, inertia, tendency)


def edges_kernel(fields_ref, north_ref, south_ref, out_ref):
    rows = fields_ref.shape[1]
    cols = fields_ref.shape[2]
    half = LANES // 2
    for top, size, ref in ((0, ROWS, north_ref), (ROWS, rows, fields_ref), (ROWS + rows, ROWS, south_ref)):
        lane = lax.broadcasted_iota(jnp.int32, (size, LANES), 1)
        packed = jnp.zeros((size, LANES), jnp.float32)
        for place in range(FIELDS):
            west = ref[place, :, :LANES]
            east = ref[place, :, cols - LANES :]
            at = place * RIM
            west = pltpu.roll(west, at, 1) if at else west
            packed = jnp.where((lane >= at) & (lane < at + RIM), west, packed)
            at = half + place * RIM
            east = pltpu.roll(east, (at + RIM) % LANES, 1)
            packed = jnp.where((lane >= at) & (lane < at + RIM), east, packed)
        out_ref[top : top + size] = packed


def edges(fields, north, south):
    rows = fields.shape[1] + 2 * ROWS
    return pl.pallas_call(
        edges_kernel,
        out_shape=jax.ShapeDtypeStruct((rows, LANES), jnp.float32),
        compiler_params=pltpu.CompilerParams(vmem_limit_bytes=VMEM_BYTES),
        name="edges",
    )(fields, north, south)


def smooth(field):
    rows, cols = field.shape
    tall = field + 0.5 * (pltpu.roll(field, 1, 0) + pltpu.roll(field, rows - 1, 0))
    return tall + 0.5 * (pltpu.roll(tall, 1, 1) + pltpu.roll(tall, cols - 1, 1))


def krylov_kernel(fields_ref, north_ref, south_ref, east_ref, west_ref, w_ref, mw_ref, sums_ref):
    rows = fields_ref.shape[1]
    cols = fields_ref.shape[2]
    tall = rows + 2 * ROWS
    wide = cols + LANES
    half = LANES // 2
    lane = lax.broadcasted_iota(jnp.int32, (tall, LANES), 1)
    from_east = east_ref[...]
    from_west = west_ref[...]
    padded = []
    for place in range(FIELDS):
        middle = jnp.concatenate([north_ref[place], fields_ref[place], south_ref[place]], axis=0)
        at = place * RIM
        high = pltpu.roll(from_east, LANES - at, 1) if at else from_east
        low = pltpu.roll(from_west, half - RIM - at, 1)
        side = jnp.where(lane < RIM, high, jnp.where(lane >= LANES - RIM, low, 0.0))
        padded.append(jnp.concatenate([middle, side], axis=1))
    first, second, depth, inertia = padded
    inside = inertia > 0.0
    east_west = pltpu.roll(first, wide - 1, 1) - pltpu.roll(first, 1, 1)
    north_south = pltpu.roll(second, tall - 1, 0) - pltpu.roll(second, 1, 0)
    source = jnp.where(depth > 0.0, 0.5 * (east_west + north_south), 0.0)
    diag = inertia + 2.0 * depth + smooth(depth)
    inverse = jnp.where(inside, 1.0 / jnp.where(inside, diag, 1.0), 0.0)
    own = (slice(ROWS, ROWS + rows), slice(0, cols))
    scaled = source
    mws = [scaled[own]]
    ws = []
    vector = scaled * inverse
    for step in range(STEPS):
        ws.append(vector[own])
        weighed = depth * vector
        scaled = depth * smooth(vector) + smooth(weighed) - 2.0 * weighed
        mws.append(scaled[own])
        vector = scaled * inverse
    for place, values in enumerate(ws):
        w_ref[place] = values
    for place, values in enumerate(mws):
        mw_ref[place] = values
    images = [mws[place] - mws[place + 1] for place in range(STEPS)]
    pairs = [ws[place] * mws[0] for place in range(STEPS)]
    for low in range(STEPS):
        for high in range(low, STEPS):
            pairs.append(ws[low] * images[high])
    half_lane = lax.broadcasted_iota(jnp.int32, (1, LANES), 1) < half
    lines = []
    for product in pairs:
        line = jnp.sum(product, axis=0, keepdims=True)
        total = line[:, :LANES]
        for start in range(LANES, cols, LANES):
            total = total + line[:, start : start + LANES]
        lines.append(total + pltpu.roll(total, half, 1))
    packed = [
        jnp.where(half_lane, lines[place], lines[place + 1]) for place in range(0, len(lines), 2)
    ]
    packed.append(jnp.zeros((ROWS - len(packed), LANES), jnp.float32))
    packed = jnp.concatenate(packed, axis=0)
    for place in range(sums_ref.shape[0]):
        sums_ref[place] = packed


def krylov(fields, north, south, east, west, devices):
    _, rows, cols = fields.shape
    f32 = jnp.float32
    return pl.pallas_call(
        krylov_kernel,
        out_shape=[
            jax.ShapeDtypeStruct((STEPS, rows, cols), f32),
            jax.ShapeDtypeStruct((STEPS + 1, rows, cols), f32),
            jax.ShapeDtypeStruct((devices, ROWS, LANES), f32),
        ],
        compiler_params=pltpu.CompilerParams(vmem_limit_bytes=VMEM_BYTES),
        name="krylov",
    )(fields, north, south, east, west)


def combine_kernel(sums_ref, w_ref, mw_ref, pressure_ref, residual_ref):
    packed = jnp.sum(sums_ref[...], axis=0)
    lower = lax.broadcasted_iota(jnp.int32, packed.shape, 1) < LANES // 2
    totals = (
        jnp.sum(jnp.where(lower, packed, 0.0), axis=1, keepdims=True),
        jnp.sum(jnp.where(lower, 0.0, packed), axis=1, keepdims=True),
    )
    entry = lambda place: totals[place % 2][place // 2 : place // 2 + 1, :]
    right = [entry(place) for place in range(STEPS)]
    matrix = {}
    place = STEPS
    for low in range(STEPS):
        for high in range(low, STEPS):
            matrix[low, high] = entry(place)
            place += 1
    for pivot in range(STEPS):
        inverse = 1.0 / matrix[pivot, pivot]
        for row in range(pivot + 1, STEPS):
            factor = matrix[pivot, row] * inverse
            for col in range(row, STEPS):
                matrix[row, col] = matrix[row, col] - factor * matrix[pivot, col]
            right[row] = right[row] - factor * right[pivot]
        matrix[pivot, pivot] = inverse
    for pivot in reversed(range(STEPS)):
        for col in range(pivot + 1, STEPS):
            right[pivot] = right[pivot] - matrix[pivot, col] * right[col]
        right[pivot] = right[pivot] * matrix[pivot, pivot]
    pressure = right[0] * w_ref[0]
    residual = mw_ref[0] - right[0] * (mw_ref[0] - mw_ref[1])
    for place in range(1, STEPS):
        pressure = pressure + right[place] * w_ref[place]
        residual = residual - right[place] * (mw_ref[place] - mw_ref[place + 1])
    pressure_ref[...] = pressure
    residual_ref[...] = residual


def combine(sums, w, mw):
    shape = jax.ShapeDtypeStruct(w.shape[1:], jnp.float32)
    return pl.pallas_call(
        combine_kernel,
        out_shape=[shape, shape],
        compiler_params=pltpu.CompilerParams(vmem_limit_bytes=VMEM_BYTES),
        name="combine",
    )(sums, w, mw)


def on_device(tendency, thickness, level_count, block_mask, owner, inertia):
    lat_count = lax.axis_size("lat")
    lon_count = lax.axis_size("lon")
    fields, head, tail, sent = integrate(
        tendency, thickness, level_count, owner[:, 0], inertia, lon_count
    )
    south_pairs = [(place, place + 1) for place in range(lat_count - 1)]
    north_pairs = [(place + 1, place) for place in range(lat_count - 1)]
    north = lax.ppermute(tail, "lat", south_pairs)
    south = lax.ppermute(head, "lat", north_pairs)
    packed = edges(fields, north, south)
    east = lax.ppermute(packed, "lon", [((p + 1) % lon_count, p) for p in range(lon_count)])
    west = lax.ppermute(packed, "lon", [(p, (p + 1) % lon_count) for p in range(lon_count)])
    sent, east, west = lax.optimization_barrier((sent, east, west))
    held = lax.all_to_all(sent, "lon", split_axis=0, concat_axis=0, tiled=True)
    w, mw, sums = krylov(fields, north, south, east, west, lat_count * lon_count)
    sums = lax.all_to_all(sums, ("lat", "lon"), split_axis=0, concat_axis=0, tiled=True)
    pressure, residual = combine(sums, w, mw)
    return (held.reshape((1, 1) + held.shape), pressure, residual)


def solution(mesh):
    return jax.shard_map(
        on_device,
        mesh=mesh,
        in_specs=(
            P(None, None, "lat", "lon"),
            P(),
            P("lat", "lon"),
            P("lat", "lon"),
            P("lat", "lon"),
            P("lat", "lon"),
        ),
        out_specs=(P("lat", "lon", None, None, None, None), P("lat", "lon"), P("lat", "lon")),
        check_vma=False,
    )
```

```python
import functools

import jax
import jax.numpy as jnp
from jax import lax
from jax.experimental import pallas as pl
from jax.experimental.pallas import tpu as pltpu
from jax.sharding import PartitionSpec as P

STEPS = 4
RIM = STEPS + 1
ROWS = 8
LANES = 128
CHUNK = 32
FIELDS = 4
VMEM_BYTES = 16 * 1024 * 1024


def integrate_kernel(
    thick_hbm,
    count_hbm,
    inertia_hbm,
    tend_hbm,
    fields_ref,
    head_ref,
    tail_ref,
    blocks_ref,
    thick_ref,
    count_ref,
    inertia_ref,
    tend_ref,
    small_sems,
    chunk_sems,
):
    levels, rows = tend_hbm.shape[1:3]
    chunk = CHUNK
    small = [
        pltpu.make_async_copy(source, target, small_sems.at[place])
        for place, (source, target) in enumerate(
            (
                (thick_hbm, thick_ref),
                (count_hbm, count_ref),
                (inertia_hbm, inertia_ref),
            )
        )
    ]
    large = []
    for place in range(rows // chunk):
        part = pl.ds(place * chunk, chunk)
        large.append(
            pltpu.make_async_copy(
                tend_hbm.at[:, :, part], tend_ref.at[:, :, part], chunk_sems.at[place]
            )
        )
    for copy in small + large:
        copy.start()
    for copy in small:
        copy.wait()
    for place, copy in enumerate(large):
        part = slice(place * chunk, (place + 1) * chunk)
        copy.wait()
        count = count_ref[part]
        first = jnp.zeros(count.shape, jnp.float32)
        second = jnp.zeros(count.shape, jnp.float32)
        depth = jnp.zeros(count.shape, jnp.float32)
        for level in range(levels):
            layer = jnp.where(count > level, thick_ref[level], 0.0)
            depth = depth + layer
            first = first + layer * tend_ref[0, level, part].astype(jnp.float32)
            second = second + layer * tend_ref[1, level, part].astype(jnp.float32)
        inertia = inertia_ref[part]
        for field, values in enumerate((first, second, depth, inertia)):
            fields_ref[field, part] = values
            if place == 0:
                head_ref[field] = values[:ROWS]
            if place == len(large) - 1:
                tail_ref[field] = values[chunk - ROWS :]
        blocks_ref[0, part] = first
        blocks_ref[1, part] = second


def integrate(tendency, thickness, level_count, inertia):
    components, levels, rows, cols = tendency.shape
    f32 = jnp.float32
    return pl.pallas_call(
        integrate_kernel,
        in_specs=[pl.BlockSpec(memory_space=pltpu.HBM)] * 4,
        out_shape=[
            jax.ShapeDtypeStruct((FIELDS, rows, cols), f32),
            jax.ShapeDtypeStruct((FIELDS, ROWS, cols), f32),
            jax.ShapeDtypeStruct((FIELDS, ROWS, cols), f32),
            jax.ShapeDtypeStruct((components, rows, cols), f32),
        ],
        scratch_shapes=[
            pltpu.SMEM(thickness.shape, f32),
            pltpu.VMEM(level_count.shape, jnp.int32),
            pltpu.VMEM(inertia.shape, f32),
            pltpu.VMEM(tendency.shape, tendency.dtype),
            pltpu.SemaphoreType.DMA((3,)),
            pltpu.SemaphoreType.DMA((rows // CHUNK,)),
        ],
        cost_estimate=pl.CostEstimate(
            flops=6 * components * levels * rows * cols,
            bytes_accessed=2 * components * levels * rows * cols,
            transcendentals=0,
        ),
        name="integrate",
    )(thickness, level_count, inertia, tendency)


def edges_kernel(fields_ref, north_ref, south_ref, out_ref):
    rows = fields_ref.shape[1]
    cols = fields_ref.shape[2]
    half = LANES // 2
    for top, size, ref in ((0, ROWS, north_ref), (ROWS, rows, fields_ref), (ROWS + rows, ROWS, south_ref)):
        lane = lax.broadcasted_iota(jnp.int32, (size, LANES), 1)
        packed = jnp.zeros((size, LANES), jnp.float32)
        for place in range(FIELDS):
            west = ref[place, :, :LANES]
            east = ref[place, :, cols - LANES :]
            at = place * RIM
            west = pltpu.roll(west, at, 1) if at else west
            packed = jnp.where((lane >= at) & (lane < at + RIM), west, packed)
            at = half + place * RIM
            east = pltpu.roll(east, (at + RIM) % LANES, 1)
            packed = jnp.where((lane >= at) & (lane < at + RIM), east, packed)
        out_ref[top : top + size] = packed


def edges(fields, north, south):
    rows = fields.shape[1] + 2 * ROWS
    return pl.pallas_call(
        edges_kernel,
        out_shape=jax.ShapeDtypeStruct((rows, LANES), jnp.float32),
        compiler_params=pltpu.CompilerParams(vmem_limit_bytes=VMEM_BYTES),
        name="edges",
    )(fields, north, south)


def smooth(field):
    rows, cols = field.shape
    tall = field + 0.5 * (pltpu.roll(field, 1, 0) + pltpu.roll(field, rows - 1, 0))
    return tall + 0.5 * (pltpu.roll(tall, 1, 1) + pltpu.roll(tall, cols - 1, 1))


def krylov_kernel(owner_ref, fields_ref, north_ref, south_ref, east_ref, west_ref, w_ref, mw_ref, sums_ref):
    rows = fields_ref.shape[1]
    cols = fields_ref.shape[2]
    tall = rows + 2 * ROWS
    wide = cols + LANES
    half = LANES // 2
    lane = lax.broadcasted_iota(jnp.int32, (tall, LANES), 1)
    from_east = east_ref[...]
    from_west = west_ref[...]
    padded = []
    for place in range(FIELDS):
        middle = jnp.concatenate([north_ref[place], fields_ref[place], south_ref[place]], axis=0)
        at = place * RIM
        high = pltpu.roll(from_east, LANES - at, 1) if at else from_east
        low = pltpu.roll(from_west, half - RIM - at, 1)
        side = jnp.where(lane < RIM, high, jnp.where(lane >= LANES - RIM, low, 0.0))
        padded.append(jnp.concatenate([middle, side], axis=1))
    first, second, depth, inertia = padded
    inside = inertia > 0.0
    east_west = pltpu.roll(first, wide - 1, 1) - pltpu.roll(first, 1, 1)
    north_south = pltpu.roll(second, tall - 1, 0) - pltpu.roll(second, 1, 0)
    source = jnp.where(depth > 0.0, 0.5 * (east_west + north_south), 0.0)
    diag = inertia + 2.0 * depth + smooth(depth)
    inverse = jnp.where(inside, 1.0 / jnp.where(inside, diag, 1.0), 0.0)
    own = (slice(ROWS, ROWS + rows), slice(0, cols))
    scaled = source
    mws = [scaled[own]]
    ws = []
    vector = scaled * inverse
    for step in range(STEPS):
        ws.append(vector[own])
        weighed = depth * vector
        scaled = depth * smooth(vector) + smooth(weighed) - 2.0 * weighed
        mws.append(scaled[own])
        vector = scaled * inverse
    for place, values in enumerate(ws):
        w_ref[place] = values
    for place, values in enumerate(mws):
        mw_ref[place] = values
    images = [mws[place] - mws[place + 1] for place in range(STEPS)]
    pairs = [ws[place] * mws[0] for place in range(STEPS)]
    for low in range(STEPS):
        for high in range(low, STEPS):
            pairs.append(ws[low] * images[high])
    half_lane = lax.broadcasted_iota(jnp.int32, (1, LANES), 1) < half
    lines = []
    for product in pairs:
        line = jnp.sum(product, axis=0, keepdims=True)
        total = line[:, :LANES]
        for start in range(LANES, cols, LANES):
            total = total + line[:, start : start + LANES]
        lines.append(total + pltpu.roll(total, half, 1))
    packed = [
        jnp.where(half_lane, lines[place], lines[place + 1]) for place in range(0, len(lines), 2)
    ]
    if len(packed) < ROWS - 1:
        packed.append(jnp.zeros((ROWS - 1 - len(packed), LANES), jnp.float32))
    place_lane = lax.broadcasted_iota(jnp.int32, (1, LANES), 1)
    owners = jnp.zeros((1, LANES), jnp.float32)
    for place in range(owner_ref.shape[0]):
        owners = jnp.where(place_lane == place, owner_ref[place].astype(jnp.float32), owners)
    packed.append(owners)
    packed = jnp.concatenate(packed, axis=0)
    sums_ref[...] = packed


def krylov(owner, fields, north, south, east, west):
    _, rows, cols = fields.shape
    f32 = jnp.float32
    return pl.pallas_call(
        krylov_kernel,
        in_specs=[pl.BlockSpec(memory_space=pltpu.SMEM)]
        + [pl.BlockSpec(memory_space=pltpu.VMEM)] * 5,
        out_shape=[
            jax.ShapeDtypeStruct((STEPS, rows, cols), f32),
            jax.ShapeDtypeStruct((STEPS + 1, rows, cols), f32),
            jax.ShapeDtypeStruct((ROWS, LANES), f32),
        ],
        compiler_params=pltpu.CompilerParams(vmem_limit_bytes=VMEM_BYTES),
        name="krylov",
    )(owner, fields, north, south, east, west)


def combine_kernel(sums_ref, w_ref, mw_ref, pressure_ref, residual_ref):
    packed = jnp.sum(sums_ref[...], axis=0)[: ROWS - 1]
    lower = lax.broadcasted_iota(jnp.int32, packed.shape, 1) < LANES // 2
    totals = (
        jnp.sum(jnp.where(lower, packed, 0.0), axis=1, keepdims=True),
        jnp.sum(jnp.where(lower, 0.0, packed), axis=1, keepdims=True),
    )
    entry = lambda place: totals[place % 2][place // 2 : place // 2 + 1, :]
    right = [entry(place) for place in range(STEPS)]
    matrix = {}
    place = STEPS
    for low in range(STEPS):
        for high in range(low, STEPS):
            matrix[low, high] = entry(place)
            place += 1
    for pivot in range(STEPS):
        inverse = 1.0 / matrix[pivot, pivot]
        for row in range(pivot + 1, STEPS):
            factor = matrix[pivot, row] * inverse
            for col in range(row, STEPS):
                matrix[row, col] = matrix[row, col] - factor * matrix[pivot, col]
            right[row] = right[row] - factor * right[pivot]
        matrix[pivot, pivot] = inverse
    for pivot in reversed(range(STEPS)):
        for col in range(pivot + 1, STEPS):
            right[pivot] = right[pivot] - matrix[pivot, col] * right[col]
        right[pivot] = right[pivot] * matrix[pivot, pivot]
    pressure = right[0] * w_ref[0]
    residual = mw_ref[0] - right[0] * (mw_ref[0] - mw_ref[1])
    for place in range(1, STEPS):
        pressure = pressure + right[place] * w_ref[place]
        residual = residual - right[place] * (mw_ref[place] - mw_ref[place + 1])
    pressure_ref[...] = pressure
    residual_ref[...] = residual


def combine(sums, w, mw):
    shape = jax.ShapeDtypeStruct(w.shape[1:], jnp.float32)
    return pl.pallas_call(
        combine_kernel,
        out_shape=[shape, shape],
        compiler_params=pltpu.CompilerParams(vmem_limit_bytes=VMEM_BYTES),
        name="combine",
    )(sums, w, mw)


def pick_kernel(sums_hbm, blocks_hbm, held_ref, owner_ref, owner_sem, sems):
    band = lax.axis_index("lat")
    me = lax.axis_index("lon").astype(jnp.float32)
    homes = owner_ref.shape[0]
    span = held_ref.shape[2]
    count = blocks_hbm.shape[2] // span
    mine = pl.ds(band * homes, homes)
    owners = pltpu.make_async_copy(
        sums_hbm.at[mine, pl.ds(ROWS - 1, 1)], owner_ref, owner_sem
    )
    owners.start()
    owners.wait()

    def copy(home, block):
        rows = pl.ds(pl.multiple_of(block * span, span), span)
        return pltpu.make_async_copy(blocks_hbm.at[home, :, rows], held_ref.at[home], sems.at[home])

    chosen = []
    for home in range(homes):
        block = jnp.int32(-1)
        for place in range(count):
            block = jnp.where(owner_ref[home, 0, place] == me, place, block)
        chosen.append(block)

        @pl.when(block >= 0)
        def _(home=home, block=block):
            copy(home, block).start()

        @pl.when(block < 0)
        def _(home=home):
            held_ref[home] = jnp.zeros(held_ref.shape[1:], jnp.float32)

    for home in range(homes):

        @pl.when(chosen[home] >= 0)
        def _(home=home):
            copy(home, chosen[home]).wait()


def pick(sums, blocks, count):
    homes, components, rows, cols = blocks.shape
    return pl.pallas_call(
        pick_kernel,
        in_specs=[pl.BlockSpec(memory_space=pltpu.HBM)] * 2,
        out_shape=jax.ShapeDtypeStruct((homes, components, rows // count, cols), jnp.float32),
        scratch_shapes=[
            pltpu.SMEM((homes, 1, LANES), jnp.float32),
            pltpu.SemaphoreType.DMA,
            pltpu.SemaphoreType.DMA((homes,)),
        ],
        name="pick",
    )(sums, blocks)


def on_device(tendency, thickness, level_count, block_mask, owner, inertia):
    lat_count = lax.axis_size("lat")
    lon_count = lax.axis_size("lon")
    fields, head, tail, blocks = integrate(tendency, thickness, level_count, inertia)
    blocks = lax.all_gather(blocks, "lon")
    south_pairs = [(place, place + 1) for place in range(lat_count - 1)]
    north_pairs = [(place + 1, place) for place in range(lat_count - 1)]
    north = lax.ppermute(tail, "lat", south_pairs)
    south = lax.ppermute(head, "lat", north_pairs)
    packed = edges(fields, north, south)
    east = lax.ppermute(packed, "lon", [((p + 1) % lon_count, p) for p in range(lon_count)])
    west = lax.ppermute(packed, "lon", [(p, (p + 1) % lon_count) for p in range(lon_count)])
    w, mw, sums = krylov(owner[:, 0], fields, north, south, east, west)
    sums = lax.all_gather(sums, ("lat", "lon"))
    pressure, residual = combine(sums, w, mw)
    held = pick(sums, blocks, owner.shape[0])
    return (held.reshape((1, 1) + held.shape), pressure, residual)


def solution(mesh):
    return jax.shard_map(
        on_device,
        mesh=mesh,
        in_specs=(
            P(None, None, "lat", "lon"),
            P(),
            P("lat", "lon"),
            P("lat", "lon"),
            P("lat", "lon"),
            P("lat", "lon"),
        ),
        out_specs=(P("lat", "lon", None, None, None, None), P("lat", "lon"), P("lat", "lon")),
        check_vma=False,
    )
```

```python
import functools

import jax
import jax.numpy as jnp
from jax import lax
from jax.experimental import pallas as pl
from jax.experimental.pallas import tpu as pltpu
from jax.sharding import PartitionSpec as P

STEPS = 4
RIM = STEPS + 1
ROWS = 8
LANES = 128
CHUNK = 32
FIELDS = 4
VMEM_BYTES = 16 * 1024 * 1024


def pack_edges(ref, part):
    cols = ref.shape[2]
    packed = None
    for place in range(FIELDS):
        west = ref[place, part, :LANES]
        east = ref[place, part, cols - LANES :]
        if packed is None:
            lane = lax.broadcasted_iota(jnp.int32, west.shape, 1)
            packed = jnp.zeros(west.shape, jnp.float32)
        at = place * RIM
        west = pltpu.roll(west, at, 1) if at else west
        packed = jnp.where((lane >= at) & (lane < at + RIM), west, packed)
        at = LANES // 2 + place * RIM
        east = pltpu.roll(east, (at + RIM) % LANES, 1)
        packed = jnp.where((lane >= at) & (lane < at + RIM), east, packed)
    return packed


def integrate_kernel(
    thick_hbm,
    owner_hbm,
    count_hbm,
    inertia_hbm,
    tend_hbm,
    fields_ref,
    head_ref,
    tail_ref,
    side_ref,
    sent_ref,
    thick_ref,
    owner_ref,
    count_ref,
    inertia_ref,
    tend_ref,
    small_sems,
    chunk_sems,
):
    levels, rows = tend_hbm.shape[1:3]
    span = sent_ref.shape[2]
    chunk = max(CHUNK, span)
    small = [
        pltpu.make_async_copy(source, target, small_sems.at[place])
        for place, (source, target) in enumerate(
            (
                (thick_hbm, thick_ref),
                (owner_hbm, owner_ref),
                (count_hbm, count_ref),
                (inertia_hbm, inertia_ref),
            )
        )
    ]
    large = []
    for place in range(rows // chunk):
        part = pl.ds(place * chunk, chunk)
        large.append(
            pltpu.make_async_copy(
                tend_hbm.at[:, :, part], tend_ref.at[:, :, part], chunk_sems.at[place]
            )
        )
    for copy in small + large:
        copy.start()
    sent_ref[...] = jnp.zeros(sent_ref.shape, jnp.float32)
    for copy in small:
        copy.wait()
    for place, copy in enumerate(large):
        part = slice(place * chunk, (place + 1) * chunk)
        copy.wait()
        count = count_ref[part]
        first = jnp.zeros(count.shape, jnp.float32)
        second = jnp.zeros(count.shape, jnp.float32)
        depth = jnp.zeros(count.shape, jnp.float32)
        for level in range(levels):
            layer = jnp.where(count > level, thick_ref[level], 0.0)
            depth = depth + layer
            first = first + layer * tend_ref[0, level, part].astype(jnp.float32)
            second = second + layer * tend_ref[1, level, part].astype(jnp.float32)
        inertia = inertia_ref[part]
        for field, values in enumerate((first, second, depth, inertia)):
            fields_ref[field, part] = values
            if place == 0:
                head_ref[field] = values[:ROWS]
            if place == len(large) - 1:
                tail_ref[field] = values[chunk - ROWS :]
        side_ref[part] = pack_edges(fields_ref, part)
        for piece in range(chunk // span):
            target = owner_ref[place * (chunk // span) + piece]

            @pl.when(target >= 0)
            def _(target=target, piece=piece, first=first, second=second):
                rows_here = slice(piece * span, (piece + 1) * span)
                sent_ref[target, 0] = first[rows_here]
                sent_ref[target, 1] = second[rows_here]


def integrate(tendency, thickness, level_count, owner, inertia, lon_count):
    components, levels, rows, cols = tendency.shape
    span = rows // owner.shape[0]
    f32 = jnp.float32
    return pl.pallas_call(
        integrate_kernel,
        in_specs=[pl.BlockSpec(memory_space=pltpu.HBM)] * 5,
        out_shape=[
            jax.ShapeDtypeStruct((FIELDS, rows, cols), f32),
            jax.ShapeDtypeStruct((FIELDS, ROWS, cols), f32),
            jax.ShapeDtypeStruct((FIELDS, ROWS, cols), f32),
            jax.ShapeDtypeStruct((rows, LANES), f32),
            jax.ShapeDtypeStruct((lon_count, components, span, cols), f32),
        ],
        scratch_shapes=[
            pltpu.SMEM(thickness.shape, f32),
            pltpu.SMEM(owner.shape, jnp.int32),
            pltpu.VMEM(level_count.shape, jnp.int32),
            pltpu.VMEM(inertia.shape, f32),
            pltpu.VMEM(tendency.shape, tendency.dtype),
            pltpu.SemaphoreType.DMA((4,)),
            pltpu.SemaphoreType.DMA((rows // max(CHUNK, span),)),
        ],
        cost_estimate=pl.CostEstimate(
            flops=6 * components * levels * rows * cols,
            bytes_accessed=2 * components * levels * rows * cols,
            transcendentals=0,
        ),
        name="integrate",
    )(thickness, owner, level_count, inertia, tendency)


def edges_kernel(side_ref, north_ref, south_ref, out_ref):
    rows = side_ref.shape[0]
    out_ref[:ROWS] = pack_edges(north_ref, slice(None))
    out_ref[ROWS : ROWS + rows] = side_ref[...]
    out_ref[ROWS + rows :] = pack_edges(south_ref, slice(None))


def edges(side, north, south):
    rows = side.shape[0] + 2 * ROWS
    return pl.pallas_call(
        edges_kernel,
        out_shape=jax.ShapeDtypeStruct((rows, LANES), jnp.float32),
        compiler_params=pltpu.CompilerParams(vmem_limit_bytes=VMEM_BYTES),
        name="edges",
    )(side, north, south)


def smooth(field):
    rows, cols = field.shape
    tall = field + 0.5 * (pltpu.roll(field, 1, 0) + pltpu.roll(field, rows - 1, 0))
    return tall + 0.5 * (pltpu.roll(tall, 1, 1) + pltpu.roll(tall, cols - 1, 1))


def krylov_kernel(fields_ref, north_ref, south_ref, east_ref, west_ref, w_ref, mw_ref, sums_ref):
    rows = fields_ref.shape[1]
    cols = fields_ref.shape[2]
    tall = rows + 2 * ROWS
    wide = cols + LANES
    half = LANES // 2
    lane = lax.broadcasted_iota(jnp.int32, (tall, LANES), 1)
    from_east = east_ref[...]
    from_west = west_ref[...]
    padded = []
    for place in range(FIELDS):
        middle = jnp.concatenate([north_ref[place], fields_ref[place], south_ref[place]], axis=0)
        at = place * RIM
        high = pltpu.roll(from_east, LANES - at, 1) if at else from_east
        low = pltpu.roll(from_west, half - RIM - at, 1)
        side = jnp.where(lane < RIM, high, jnp.where(lane >= LANES - RIM, low, 0.0))
        padded.append(jnp.concatenate([middle, side], axis=1))
    first, second, depth, inertia = padded
    inside = inertia > 0.0
    east_west = pltpu.roll(first, wide - 1, 1) - pltpu.roll(first, 1, 1)
    north_south = pltpu.roll(second, tall - 1, 0) - pltpu.roll(second, 1, 0)
    source = jnp.where(depth > 0.0, 0.5 * (east_west + north_south), 0.0)
    diag = inertia + 2.0 * depth + smooth(depth)
    inverse = jnp.where(inside, 1.0 / jnp.where(inside, diag, 1.0), 0.0)
    own = (slice(ROWS, ROWS + rows), slice(0, cols))
    scaled = source
    mws = [scaled[own]]
    ws = []
    vector = scaled * inverse
    for step in range(STEPS):
        ws.append(vector[own])
        weighed = depth * vector
        scaled = depth * smooth(vector) + smooth(weighed) - 2.0 * weighed
        mws.append(scaled[own])
        vector = scaled * inverse
    for place, values in enumerate(ws):
        w_ref[place] = values
    for place, values in enumerate(mws):
        mw_ref[place] = values
    images = [mws[place] - mws[place + 1] for place in range(STEPS)]
    pairs = [ws[place] * mws[0] for place in range(STEPS)]
    for low in range(STEPS):
        for high in range(low, STEPS):
            pairs.append(ws[low] * images[high])
    half_lane = lax.broadcasted_iota(jnp.int32, (1, LANES), 1) < half
    lines = []
    for product in pairs:
        line = jnp.sum(product, axis=0, keepdims=True)
        total = line[:, :LANES]
        for start in range(LANES, cols, LANES):
            total = total + line[:, start : start + LANES]
        lines.append(total + pltpu.roll(total, half, 1))
    packed = [
        jnp.where(half_lane, lines[place], lines[place + 1]) for place in range(0, len(lines), 2)
    ]
    packed.append(jnp.zeros((ROWS - len(packed), LANES), jnp.float32))
    packed = jnp.concatenate(packed, axis=0)
    for place in range(sums_ref.shape[0]):
        sums_ref[place] = packed


def krylov(fields, north, south, east, west, copies):
    _, rows, cols = fields.shape
    f32 = jnp.float32
    return pl.pallas_call(
        krylov_kernel,
        out_shape=[
            jax.ShapeDtypeStruct((STEPS, rows, cols), f32),
            jax.ShapeDtypeStruct((STEPS + 1, rows, cols), f32),
            jax.ShapeDtypeStruct((copies, ROWS, LANES), f32),
        ],
        compiler_params=pltpu.CompilerParams(vmem_limit_bytes=VMEM_BYTES),
        name="krylov",
    )(fields, north, south, east, west)


def combine_kernel(sums_ref, w_ref, mw_ref, arrived_ref, pressure_ref, residual_ref, held_ref):
    held_ref[...] = arrived_ref[...]
    packed = jnp.sum(sums_ref[...], axis=0)
    lower = lax.broadcasted_iota(jnp.int32, packed.shape, 1) < LANES // 2
    totals = (
        jnp.sum(jnp.where(lower, packed, 0.0), axis=1, keepdims=True),
        jnp.sum(jnp.where(lower, 0.0, packed), axis=1, keepdims=True),
    )
    entry = lambda place: totals[place % 2][place // 2 : place // 2 + 1, :]
    right = [entry(place) for place in range(STEPS)]
    matrix = {}
    place = STEPS
    for low in range(STEPS):
        for high in range(low, STEPS):
            matrix[low, high] = entry(place)
            place += 1
    for pivot in range(STEPS):
        inverse = 1.0 / matrix[pivot, pivot]
        for row in range(pivot + 1, STEPS):
            factor = matrix[pivot, row] * inverse
            for col in range(row, STEPS):
                matrix[row, col] = matrix[row, col] - factor * matrix[pivot, col]
            right[row] = right[row] - factor * right[pivot]
        matrix[pivot, pivot] = inverse
    for pivot in reversed(range(STEPS)):
        for col in range(pivot + 1, STEPS):
            right[pivot] = right[pivot] - matrix[pivot, col] * right[col]
        right[pivot] = right[pivot] * matrix[pivot, pivot]
    pressure = right[0] * w_ref[0]
    residual = mw_ref[0] - right[0] * (mw_ref[0] - mw_ref[1])
    for place in range(1, STEPS):
        pressure = pressure + right[place] * w_ref[place]
        residual = residual - right[place] * (mw_ref[place] - mw_ref[place + 1])
    pressure_ref[...] = pressure
    residual_ref[...] = residual


def combine(sums, w, mw, arrived):
    shape = jax.ShapeDtypeStruct(w.shape[1:], jnp.float32)
    return pl.pallas_call(
        combine_kernel,
        out_shape=[shape, shape, jax.ShapeDtypeStruct(arrived.shape, jnp.float32)],
        compiler_params=pltpu.CompilerParams(vmem_limit_bytes=VMEM_BYTES),
        name="combine",
    )(sums, w, mw, arrived)


def on_device(tendency, thickness, level_count, block_mask, owner, inertia):
    lat_count = lax.axis_size("lat")
    lon_count = lax.axis_size("lon")
    fields, head, tail, side, sent = integrate(
        tendency, thickness, level_count, owner[:, 0], inertia, lon_count
    )
    south_pairs = [(place, place + 1) for place in range(lat_count - 1)]
    north_pairs = [(place + 1, place) for place in range(lat_count - 1)]
    north = lax.ppermute(tail, "lat", south_pairs)
    south = lax.ppermute(head, "lat", north_pairs)
    packed = edges(side, north, south)
    sent, packed = lax.optimization_barrier((sent, packed))
    east = lax.ppermute(packed, "lon", [((p + 1) % lon_count, p) for p in range(lon_count)])
    west = lax.ppermute(packed, "lon", [(p, (p + 1) % lon_count) for p in range(lon_count)])
    arrived = lax.all_to_all(sent, "lon", split_axis=0, concat_axis=0, tiled=True)
    w, mw, sums = krylov(fields, north, south, east, west, lat_count)
    sums = lax.all_to_all(sums, "lat", split_axis=0, concat_axis=0, tiled=True)
    sums = jnp.broadcast_to(jnp.sum(sums, axis=0), (lon_count,) + sums.shape[1:])
    sums = lax.all_to_all(sums, "lon", split_axis=0, concat_axis=0, tiled=True)
    pressure, residual, held = combine(sums, w, mw, arrived)
    return (held.reshape((1, 1) + held.shape), pressure, residual)


def solution(mesh):
    return jax.shard_map(
        on_device,
        mesh=mesh,
        in_specs=(
            P(None, None, "lat", "lon"),
            P(),
            P("lat", "lon"),
            P("lat", "lon"),
            P("lat", "lon"),
            P("lat", "lon"),
        ),
        out_specs=(P("lat", "lon", None, None, None, None), P("lat", "lon"), P("lat", "lon")),
        check_vma=False,
    )
```

```python
import functools

import jax
import jax.numpy as jnp
from jax import lax
from jax.experimental import pallas as pl
from jax.experimental.pallas import tpu as pltpu
from jax.sharding import PartitionSpec as P

STEPS = 4
RIM = STEPS + 1
ROWS = 8
LANES = 128
CHUNK = 32
FIELDS = 4
VMEM_BYTES = 16 * 1024 * 1024
INTEGRATE_BYTES = 56350000


def pack_edges(ref, part):
    cols = ref.shape[2]
    packed = None
    for place in range(FIELDS):
        west = ref[place, part, :LANES]
        east = ref[place, part, cols - LANES :]
        if packed is None:
            lane = lax.broadcasted_iota(jnp.int32, west.shape, 1)
            packed = jnp.zeros(west.shape, jnp.float32)
        at = place * RIM
        west = pltpu.roll(west, at, 1) if at else west
        packed = jnp.where((lane >= at) & (lane < at + RIM), west, packed)
        at = LANES // 2 + place * RIM
        east = pltpu.roll(east, (at + RIM) % LANES, 1)
        packed = jnp.where((lane >= at) & (lane < at + RIM), east, packed)
    return packed


def integrate_kernel(
    thick_hbm,
    owner_hbm,
    count_hbm,
    inertia_hbm,
    tend_hbm,
    fields_ref,
    head_ref,
    tail_ref,
    side_ref,
    sent_ref,
    thick_ref,
    owner_ref,
    count_ref,
    inertia_ref,
    tend_ref,
    small_sems,
    chunk_sems,
):
    levels, rows = tend_hbm.shape[1:3]
    span = (sent_ref.shape[1] - ROWS) // 2
    chunk = max(CHUNK, span)
    small = [
        pltpu.make_async_copy(source, target, small_sems.at[place])
        for place, (source, target) in enumerate(
            (
                (thick_hbm, thick_ref),
                (owner_hbm, owner_ref),
                (count_hbm, count_ref),
                (inertia_hbm, inertia_ref),
            )
        )
    ]
    large = []
    for place in range(rows // chunk):
        part = pl.ds(place * chunk, chunk)
        large.append(
            pltpu.make_async_copy(
                tend_hbm.at[:, :, part], tend_ref.at[:, :, part], chunk_sems.at[place]
            )
        )
    for copy in small + large:
        copy.start()
    sent_ref[...] = jnp.zeros(sent_ref.shape, jnp.float32)
    for copy in small:
        copy.wait()
    for place, copy in enumerate(large):
        part = slice(place * chunk, (place + 1) * chunk)
        copy.wait()
        count = count_ref[part]
        first = jnp.zeros(count.shape, jnp.float32)
        second = jnp.zeros(count.shape, jnp.float32)
        depth = jnp.zeros(count.shape, jnp.float32)
        for level in range(levels):
            layer = jnp.where(count > level, thick_ref[level], 0.0)
            depth = depth + layer
            first = first + layer * tend_ref[0, level, part].astype(jnp.float32)
            second = second + layer * tend_ref[1, level, part].astype(jnp.float32)
        inertia = inertia_ref[part]
        for field, values in enumerate((first, second, depth, inertia)):
            fields_ref[field, part] = values
            if place == 0:
                head_ref[field] = values[:ROWS]
            if place == len(large) - 1:
                tail_ref[field] = values[chunk - ROWS :]
        side_ref[part] = pack_edges(fields_ref, part)
        for piece in range(chunk // span):
            target = owner_ref[place * (chunk // span) + piece]

            @pl.when(target >= 0)
            def _(target=target, piece=piece, first=first, second=second):
                rows_here = slice(piece * span, (piece + 1) * span)
                sent_ref[target, :span] = first[rows_here]
                sent_ref[target, span : 2 * span] = second[rows_here]


def integrate(tendency, thickness, level_count, owner, inertia, lon_count):
    components, levels, rows, cols = tendency.shape
    span = rows // owner.shape[0]
    f32 = jnp.float32
    return pl.pallas_call(
        integrate_kernel,
        in_specs=[pl.BlockSpec(memory_space=pltpu.HBM)] * 5,
        out_shape=[
            jax.ShapeDtypeStruct((FIELDS, rows, cols), f32),
            jax.ShapeDtypeStruct((FIELDS, ROWS, cols), f32),
            jax.ShapeDtypeStruct((FIELDS, ROWS, cols), f32),
            jax.ShapeDtypeStruct((rows, LANES), f32),
            jax.ShapeDtypeStruct((lon_count, components * span + ROWS, cols), f32),
        ],
        scratch_shapes=[
            pltpu.SMEM(thickness.shape, f32),
            pltpu.SMEM(owner.shape, jnp.int32),
            pltpu.VMEM(level_count.shape, jnp.int32),
            pltpu.VMEM(inertia.shape, f32),
            pltpu.VMEM(tendency.shape, tendency.dtype),
            pltpu.SemaphoreType.DMA((4,)),
            pltpu.SemaphoreType.DMA((rows // max(CHUNK, span),)),
        ],
        compiler_params=pltpu.CompilerParams(vmem_limit_bytes=INTEGRATE_BYTES),
        cost_estimate=pl.CostEstimate(
            flops=6 * components * levels * rows * cols,
            bytes_accessed=2 * components * levels * rows * cols,
            transcendentals=0,
        ),
        name="integrate",
    )(thickness, owner, level_count, inertia, tendency)


def edges_kernel(side_ref, north_ref, south_ref, out_ref):
    rows = side_ref.shape[0]
    out_ref[:ROWS] = pack_edges(north_ref, slice(None))
    out_ref[ROWS : ROWS + rows] = side_ref[...]
    out_ref[ROWS + rows :] = pack_edges(south_ref, slice(None))


def edges(side, north, south):
    rows = side.shape[0] + 2 * ROWS
    return pl.pallas_call(
        edges_kernel,
        out_shape=jax.ShapeDtypeStruct((rows, LANES), jnp.float32),
        compiler_params=pltpu.CompilerParams(vmem_limit_bytes=VMEM_BYTES),
        name="edges",
    )(side, north, south)


def smooth(field):
    rows, cols = field.shape
    tall = field + 0.5 * (pltpu.roll(field, 1, 0) + pltpu.roll(field, rows - 1, 0))
    return tall + 0.5 * (pltpu.roll(tall, 1, 1) + pltpu.roll(tall, cols - 1, 1))


def krylov_kernel(fields_ref, north_ref, south_ref, east_ref, west_ref, w_ref, mw_ref, sums_ref):
    rows = fields_ref.shape[1]
    cols = fields_ref.shape[2]
    tall = rows + 2 * ROWS
    wide = cols + LANES
    half = LANES // 2
    lane = lax.broadcasted_iota(jnp.int32, (tall, LANES), 1)
    from_east = east_ref[...]
    from_west = west_ref[...]
    padded = []
    for place in range(FIELDS):
        middle = jnp.concatenate([north_ref[place], fields_ref[place], south_ref[place]], axis=0)
        at = place * RIM
        high = pltpu.roll(from_east, LANES - at, 1) if at else from_east
        low = pltpu.roll(from_west, half - RIM - at, 1)
        side = jnp.where(lane < RIM, high, jnp.where(lane >= LANES - RIM, low, 0.0))
        padded.append(jnp.concatenate([middle, side], axis=1))
    first, second, depth, inertia = padded
    inside = inertia > 0.0
    east_west = pltpu.roll(first, wide - 1, 1) - pltpu.roll(first, 1, 1)
    north_south = pltpu.roll(second, tall - 1, 0) - pltpu.roll(second, 1, 0)
    source = jnp.where(depth > 0.0, 0.5 * (east_west + north_south), 0.0)
    diag = inertia + 2.0 * depth + smooth(depth)
    inverse = jnp.where(inside, 1.0 / jnp.where(inside, diag, 1.0), 0.0)
    own = (slice(ROWS, ROWS + rows), slice(0, cols))
    scaled = source
    mws = [scaled[own]]
    ws = []
    vector = scaled * inverse
    for step in range(STEPS):
        ws.append(vector[own])
        weighed = depth * vector
        scaled = depth * smooth(vector) + smooth(weighed) - 2.0 * weighed
        mws.append(scaled[own])
        vector = scaled * inverse
    for place, values in enumerate(ws):
        w_ref[place] = values
    for place, values in enumerate(mws):
        mw_ref[place] = values
    images = [mws[place] - mws[place + 1] for place in range(STEPS)]
    pairs = [ws[place] * mws[0] for place in range(STEPS)]
    for low in range(STEPS):
        for high in range(low, STEPS):
            pairs.append(ws[low] * images[high])
    half_lane = lax.broadcasted_iota(jnp.int32, (1, LANES), 1) < half
    lines = []
    for product in pairs:
        line = jnp.sum(product, axis=0, keepdims=True)
        total = line[:, :LANES]
        for start in range(LANES, cols, LANES):
            total = total + line[:, start : start + LANES]
        lines.append(total + pltpu.roll(total, half, 1))
    packed = [
        jnp.where(half_lane, lines[place], lines[place + 1]) for place in range(0, len(lines), 2)
    ]
    packed.append(jnp.zeros((ROWS - len(packed), LANES), jnp.float32))
    packed = jnp.concatenate(packed, axis=0)
    sums_ref[...] = packed


def krylov(fields, north, south, east, west):
    _, rows, cols = fields.shape
    f32 = jnp.float32
    return pl.pallas_call(
        krylov_kernel,
        out_shape=[
            jax.ShapeDtypeStruct((STEPS, rows, cols), f32),
            jax.ShapeDtypeStruct((STEPS + 1, rows, cols), f32),
            jax.ShapeDtypeStruct((ROWS, LANES), f32),
        ],
        compiler_params=pltpu.CompilerParams(vmem_limit_bytes=VMEM_BYTES),
        name="krylov",
    )(fields, north, south, east, west)


def combine_kernel(arrived_ref, w_ref, mw_ref, pressure_ref, residual_ref, held_ref):
    held_ref[...] = arrived_ref[:, : held_ref.shape[1]]
    packed = jnp.sum(arrived_ref[:, held_ref.shape[1] :, :LANES], axis=0)
    lower = lax.broadcasted_iota(jnp.int32, packed.shape, 1) < LANES // 2
    totals = (
        jnp.sum(jnp.where(lower, packed, 0.0), axis=1, keepdims=True),
        jnp.sum(jnp.where(lower, 0.0, packed), axis=1, keepdims=True),
    )
    entry = lambda place: totals[place % 2][place // 2 : place // 2 + 1, :]
    right = [entry(place) for place in range(STEPS)]
    matrix = {}
    place = STEPS
    for low in range(STEPS):
        for high in range(low, STEPS):
            matrix[low, high] = entry(place)
            place += 1
    for pivot in range(STEPS):
        inverse = 1.0 / matrix[pivot, pivot]
        for row in range(pivot + 1, STEPS):
            factor = matrix[pivot, row] * inverse
            for col in range(row, STEPS):
                matrix[row, col] = matrix[row, col] - factor * matrix[pivot, col]
            right[row] = right[row] - factor * right[pivot]
        matrix[pivot, pivot] = inverse
    for pivot in reversed(range(STEPS)):
        for col in range(pivot + 1, STEPS):
            right[pivot] = right[pivot] - matrix[pivot, col] * right[col]
        right[pivot] = right[pivot] * matrix[pivot, pivot]
    pressure = right[0] * w_ref[0]
    residual = mw_ref[0] - right[0] * (mw_ref[0] - mw_ref[1])
    for place in range(1, STEPS):
        pressure = pressure + right[place] * w_ref[place]
        residual = residual - right[place] * (mw_ref[place] - mw_ref[place + 1])
    pressure_ref[...] = pressure
    residual_ref[...] = residual


def combine(arrived, w, mw):
    slots, rows, cols = arrived.shape
    shape = jax.ShapeDtypeStruct(w.shape[1:], jnp.float32)
    return pl.pallas_call(
        combine_kernel,
        out_shape=[shape, shape, jax.ShapeDtypeStruct((slots, rows - ROWS, cols), jnp.float32)],
        compiler_params=pltpu.CompilerParams(vmem_limit_bytes=VMEM_BYTES),
        name="combine",
    )(arrived, w, mw)


def total_over(values, axis):
    count = lax.axis_size(axis)
    shift = 1
    while shift < count:
        pairs = [(place, place ^ shift) for place in range(count)]
        values = values + lax.ppermute(values, axis, pairs)
        shift *= 2
    return values


def on_device(tendency, thickness, level_count, block_mask, owner, inertia):
    lat_count = lax.axis_size("lat")
    lon_count = lax.axis_size("lon")
    fields, head, tail, side, sent = integrate(
        tendency, thickness, level_count, owner[:, 0], inertia, lon_count
    )
    south_pairs = [(place, place + 1) for place in range(lat_count - 1)]
    north_pairs = [(place + 1, place) for place in range(lat_count - 1)]
    north = lax.ppermute(tail, "lat", south_pairs)
    south = lax.ppermute(head, "lat", north_pairs)
    packed = edges(side, north, south)
    east = lax.ppermute(packed, "lon", [((p + 1) % lon_count, p) for p in range(lon_count)])
    west = lax.ppermute(packed, "lon", [(p, (p + 1) % lon_count) for p in range(lon_count)])
    w, mw, sums = krylov(fields, north, south, east, west)
    sums = jnp.broadcast_to(total_over(sums, "lat"), (lon_count,) + sums.shape)
    sent = lax.dynamic_update_slice(sent, sums, (0, sent.shape[1] - ROWS, 0))
    arrived = lax.all_to_all(sent, "lon", split_axis=0, concat_axis=0, tiled=True)
    pressure, residual, held = combine(arrived, w, mw)
    held = held.reshape((1, 1, lon_count, 2, held.shape[1] // 2, held.shape[2]))
    return (held, pressure, residual)


def solution(mesh):
    return jax.shard_map(
        on_device,
        mesh=mesh,
        in_specs=(
            P(None, None, "lat", "lon"),
            P(),
            P("lat", "lon"),
            P("lat", "lon"),
            P("lat", "lon"),
            P("lat", "lon"),
        ),
        out_specs=(P("lat", "lon", None, None, None, None), P("lat", "lon"), P("lat", "lon")),
        check_vma=False,
    )
```

```python
import jax
import jax.numpy as jnp
from jax import lax
from jax.experimental import pallas as pl
from jax.experimental.pallas import tpu as pltpu
from jax.sharding import PartitionSpec as P

STEPS = 4
RIM = STEPS + 1
ROWS = 8
LANES = 128
HALF = LANES // 2
EAST = 48
SEAM = HALF + EAST
CHUNK = 32
FIELDS = 4
VMEM_BYTES = 16 * 1024 * 1024


def lanes_of(shape):
    return lax.broadcasted_iota(jnp.int32, shape, len(shape) - 1)


def turn(values, amount):
    amount = amount % values.shape[1]
    return pltpu.roll(values, amount, 1) if amount else values


def is_even(axis):
    return lax.rem(lax.axis_index(axis), 2) == 0


def pack_edges(ref, part):
    cols = ref.shape[2]
    packed = None
    for place in range(FIELDS):
        west = ref[place, part, :LANES]
        east = ref[place, part, cols - LANES :]
        if packed is None:
            lane = lanes_of(west.shape)
            packed = jnp.zeros(west.shape, jnp.float32)
        at = place * RIM
        packed = jnp.where((lane >= at) & (lane < at + RIM), turn(west, at), packed)
        at = HALF + place * RIM
        packed = jnp.where((lane >= at) & (lane < at + RIM), turn(east, at + RIM), packed)
    return packed


def integrate_kernel(
    thick_hbm,
    owner_hbm,
    count_hbm,
    inertia_hbm,
    tend_hbm,
    fields_ref,
    near_ref,
    far_ref,
    side_ref,
    sent_ref,
    thick_ref,
    owner_ref,
    count_ref,
    inertia_ref,
    tend_ref,
    small_sems,
    chunk_sems,
):
    levels, rows = tend_hbm.shape[1:3]
    span = (sent_ref.shape[1] - ROWS) // 2
    chunk = max(CHUNK, span)
    even = is_even("lat")
    small = [
        pltpu.make_async_copy(source, target, small_sems.at[place])
        for place, (source, target) in enumerate(
            (
                (thick_hbm, thick_ref),
                (owner_hbm, owner_ref),
                (count_hbm, count_ref),
                (inertia_hbm, inertia_ref),
            )
        )
    ]
    large = []
    for place in range(rows // chunk):
        part = pl.ds(place * chunk, chunk)
        large.append(
            pltpu.make_async_copy(
                tend_hbm.at[:, :, part], tend_ref.at[:, :, part], chunk_sems.at[place]
            )
        )
    for copy in small + large:
        copy.start()
    sent_ref[...] = jnp.zeros(sent_ref.shape, jnp.float32)
    for copy in small:
        copy.wait()
    for place, copy in enumerate(large):
        part = slice(place * chunk, (place + 1) * chunk)
        copy.wait()
        count = count_ref[part]
        first = jnp.zeros(count.shape, jnp.float32)
        second = jnp.zeros(count.shape, jnp.float32)
        depth = jnp.zeros(count.shape, jnp.float32)
        for level in range(levels):
            layer = jnp.where(count > level, thick_ref[level], 0.0)
            depth = depth + layer
            first = first + layer * tend_ref[0, level, part].astype(jnp.float32)
            second = second + layer * tend_ref[1, level, part].astype(jnp.float32)
        inertia = inertia_ref[part]
        for field, values in enumerate((first, second, depth, inertia)):
            fields_ref[field, part] = values
        side_ref[part] = pack_edges(fields_ref, part)
        for piece in range(chunk // span):
            target = owner_ref[place * (chunk // span) + piece]

            @pl.when(target >= 0)
            def _(target=target, piece=piece, first=first, second=second):
                rows_here = slice(piece * span, (piece + 1) * span)
                sent_ref[target, :span] = first[rows_here]
                sent_ref[target, span : 2 * span] = second[rows_here]

    for field in range(FIELDS):
        head = fields_ref[field, :ROWS]
        tail = fields_ref[field, rows - ROWS :]
        near_ref[field] = jnp.where(even, tail, head)
        far_ref[field] = jnp.where(even, head, tail)


def integrate(tendency, thickness, level_count, owner, inertia, lon_count):
    components, levels, rows, cols = tendency.shape
    span = rows // owner.shape[0]
    f32 = jnp.float32
    return pl.pallas_call(
        integrate_kernel,
        in_specs=[pl.BlockSpec(memory_space=pltpu.HBM)] * 5,
        out_shape=[
            jax.ShapeDtypeStruct((FIELDS, rows, cols), f32),
            jax.ShapeDtypeStruct((FIELDS, ROWS, cols), f32),
            jax.ShapeDtypeStruct((FIELDS, ROWS, cols), f32),
            jax.ShapeDtypeStruct((rows, LANES), f32),
            jax.ShapeDtypeStruct((lon_count, components * span + ROWS, cols), f32),
        ],
        scratch_shapes=[
            pltpu.SMEM(thickness.shape, f32),
            pltpu.SMEM(owner.shape, jnp.int32),
            pltpu.VMEM(level_count.shape, jnp.int32),
            pltpu.VMEM(inertia.shape, f32),
            pltpu.VMEM(tendency.shape, tendency.dtype),
            pltpu.SemaphoreType.DMA((4,)),
            pltpu.SemaphoreType.DMA((rows // max(CHUNK, span),)),
        ],
        cost_estimate=pl.CostEstimate(
            flops=6 * components * levels * rows * cols,
            bytes_accessed=2 * components * levels * rows * cols,
            transcendentals=0,
        ),
        name="integrate",
    )(thickness, owner, level_count, inertia, tendency)


def edges_kernel(side_ref, near_ref, far_ref, out_ref):
    rows = side_ref.shape[0]
    even = is_even("lat")
    near = pack_edges(near_ref, slice(None))
    far = pack_edges(far_ref, slice(None))
    out_ref[:ROWS] = jnp.where(even, far, near)
    out_ref[ROWS : ROWS + rows] = side_ref[...]
    out_ref[ROWS + rows :] = jnp.where(even, near, far)


def edges(side, near, far):
    rows = side.shape[0] + 2 * ROWS
    return pl.pallas_call(
        edges_kernel,
        out_shape=jax.ShapeDtypeStruct((rows, LANES), jnp.float32),
        name="edges",
    )(side, near, far)


def smooth(field):
    rows, cols = field.shape
    tall = field + 0.5 * (pltpu.roll(field, 1, 0) + pltpu.roll(field, rows - 1, 0))
    return tall + 0.5 * (pltpu.roll(tall, 1, 1) + pltpu.roll(tall, cols - 1, 1))


def basis(first, second, depth, inertia):
    tall, wide = first.shape
    own = slice(ROWS, tall - ROWS)
    inside = inertia > 0.0
    east_west = pltpu.roll(first, wide - 1, 1) - pltpu.roll(first, 1, 1)
    north_south = pltpu.roll(second, tall - 1, 0) - pltpu.roll(second, 1, 0)
    scaled = jnp.where(depth > 0.0, 0.5 * (east_west + north_south), 0.0)
    diag = inertia + 2.0 * depth + smooth(depth)
    inverse = jnp.where(inside, 1.0 / jnp.where(inside, diag, 1.0), 0.0)
    mws = [scaled[own]]
    ws = []
    vector = scaled * inverse
    for step in range(STEPS):
        ws.append(vector[own])
        weighed = depth * vector
        scaled = depth * smooth(vector) + smooth(weighed) - 2.0 * weighed
        mws.append(scaled[own])
        if step + 1 < STEPS:
            vector = scaled * inverse
    return ws, mws


def moments(ws, mws, mask):
    ws = [jnp.where(mask, values, 0.0) for values in ws]
    images = [mws[place] - mws[place + 1] for place in range(STEPS)]
    pairs = [ws[place] * mws[0] for place in range(STEPS)]
    for low in range(STEPS):
        for high in range(low, STEPS):
            pairs.append(ws[low] * images[high])
    lower = lanes_of((1, LANES)) < HALF
    lines = []
    for product in pairs:
        line = jnp.sum(product, axis=0, keepdims=True)
        total = line[:, :LANES]
        for start in range(LANES, line.shape[1], LANES):
            total = total + line[:, start : start + LANES]
        lines.append(total + turn(total, HALF))
    packed = [
        jnp.where(lower, lines[place], lines[place + 1]) for place in range(0, len(lines), 2)
    ]
    packed.append(jnp.zeros((ROWS - len(packed), LANES), jnp.float32))
    return jnp.concatenate(packed, axis=0)


def interior_kernel(fields_ref, near_ref, far_ref, w_ref, mw_ref, strip_ref, sums_ref):
    cols = fields_ref.shape[2]
    even = is_even("lat")
    lane = lanes_of((strip_ref.shape[1], LANES))
    padded = []
    for place in range(FIELDS):
        near = near_ref[place]
        far = far_ref[place]
        north = jnp.where(even, far, near)
        south = jnp.where(even, near, far)
        values = jnp.concatenate([north, fields_ref[place], south], axis=0)
        east = turn(values[:, cols - LANES :], SEAM)
        strip_ref[place] = jnp.where(lane < HALF, values[:, :LANES], east)
        padded.append(values)
    ws, mws = basis(*padded)
    for place, values in enumerate(ws):
        w_ref[place] = values
    for place, values in enumerate(mws):
        mw_ref[place] = values
    lane = lanes_of(ws[0].shape)
    sums_ref[...] = moments(ws, mws, (lane >= RIM) & (lane < cols - RIM))


def interior(fields, near, far):
    _, rows, cols = fields.shape
    f32 = jnp.float32
    return pl.pallas_call(
        interior_kernel,
        out_shape=[
            jax.ShapeDtypeStruct((STEPS, rows, cols), f32),
            jax.ShapeDtypeStruct((STEPS + 1, rows, cols), f32),
            jax.ShapeDtypeStruct((FIELDS, rows + 2 * ROWS, LANES), f32),
            jax.ShapeDtypeStruct((ROWS, LANES), f32),
        ],
        compiler_params=pltpu.CompilerParams(vmem_limit_bytes=VMEM_BYTES),
        cost_estimate=pl.CostEstimate(
            flops=300 * rows * cols, bytes_accessed=64 * rows * cols, transcendentals=0
        ),
        name="interior",
    )(fields, near, far)


def strip_kernel(strip_in_ref, near_ref, far_ref, inner_ref, w_ref, mw_ref, sums_ref):
    even = is_even("lon")
    near = near_ref[...]
    far = far_ref[...]
    from_east = jnp.where(even, near, far)
    from_west = jnp.where(even, far, near)
    lane = lanes_of(near.shape)
    padded = []
    for place in range(FIELDS):
        at = place * RIM
        east = turn(from_east, SEAM - at)
        west = turn(from_west, HALF - RIM - at)
        halo = jnp.where(lane < SEAM + RIM, east, jnp.where(lane >= LANES - RIM, west, 0.0))
        padded.append(jnp.where(lane < SEAM, strip_in_ref[place], halo))
    ws, mws = basis(*padded)
    for place, values in enumerate(ws):
        w_ref[place] = values
    for place, values in enumerate(mws):
        mw_ref[place] = values
    lane = lanes_of(ws[0].shape)
    edge = (lane < RIM) | ((lane >= SEAM - RIM) & (lane < SEAM))
    sums_ref[...] = inner_ref[...] + moments(ws, mws, edge)


def strip(strip_in, near, far, inner):
    rows = strip_in.shape[1] - 2 * ROWS
    f32 = jnp.float32
    return pl.pallas_call(
        strip_kernel,
        out_shape=[
            jax.ShapeDtypeStruct((STEPS, rows, LANES), f32),
            jax.ShapeDtypeStruct((STEPS + 1, rows, LANES), f32),
            jax.ShapeDtypeStruct((ROWS, LANES), f32),
        ],
        compiler_params=pltpu.CompilerParams(vmem_limit_bytes=VMEM_BYTES),
        name="strip",
    )(strip_in, near, far, inner)


def combine_kernel(
    arrived_ref, w_ref, mw_ref, w_edge_ref, mw_edge_ref, pressure_ref, residual_ref, held_ref
):
    held_ref[...] = arrived_ref[:, : held_ref.shape[1]]
    packed = jnp.sum(arrived_ref[:, held_ref.shape[1] :, :LANES], axis=0)
    lower = lanes_of(packed.shape) < HALF
    totals = (
        jnp.sum(jnp.where(lower, packed, 0.0), axis=1, keepdims=True),
        jnp.sum(jnp.where(lower, 0.0, packed), axis=1, keepdims=True),
    )
    entry = lambda place: totals[place % 2][place // 2 : place // 2 + 1, :]
    right = [entry(place) for place in range(STEPS)]
    matrix = {}
    place = STEPS
    for low in range(STEPS):
        for high in range(low, STEPS):
            matrix[low, high] = entry(place)
            place += 1
    for pivot in range(STEPS):
        inverse = 1.0 / matrix[pivot, pivot]
        for row in range(pivot + 1, STEPS):
            factor = matrix[pivot, row] * inverse
            for col in range(row, STEPS):
                matrix[row, col] = matrix[row, col] - factor * matrix[pivot, col]
            right[row] = right[row] - factor * right[pivot]
        matrix[pivot, pivot] = inverse
    for pivot in reversed(range(STEPS)):
        for col in range(pivot + 1, STEPS):
            right[pivot] = right[pivot] - matrix[pivot, col] * right[col]
        right[pivot] = right[pivot] * matrix[pivot, pivot]

    def results(w_ref, mw_ref):
        pressure = right[0] * w_ref[0]
        residual = mw_ref[0] - right[0] * (mw_ref[0] - mw_ref[1])
        for place in range(1, STEPS):
            pressure = pressure + right[place] * w_ref[place]
            residual = residual - right[place] * (mw_ref[place] - mw_ref[place + 1])
        return pressure, residual

    inner = results(w_ref, mw_ref)
    edge = results(w_edge_ref, mw_edge_ref)
    cols = pressure_ref.shape[1]
    lane = lanes_of(edge[0].shape)
    for out_ref, inside, border in zip((pressure_ref, residual_ref), inner, edge):
        out_ref[:, :LANES] = jnp.where(lane < RIM, border, inside[:, :LANES])
        if cols > 2 * LANES:
            out_ref[:, LANES : cols - LANES] = inside[:, LANES : cols - LANES]
        out_ref[:, cols - LANES :] = jnp.where(
            lane >= LANES - RIM, turn(border, -SEAM), inside[:, cols - LANES :]
        )


def combine(arrived, w, mw, w_edge, mw_edge):
    slots, rows, cols = arrived.shape
    shape = jax.ShapeDtypeStruct(w.shape[1:], jnp.float32)
    return pl.pallas_call(
        combine_kernel,
        out_shape=[shape, shape, jax.ShapeDtypeStruct((slots, rows - ROWS, cols), jnp.float32)],
        compiler_params=pltpu.CompilerParams(vmem_limit_bytes=VMEM_BYTES),
        name="combine",
    )(arrived, w, mw, w_edge, mw_edge)


def total_over(values, axis):
    count = lax.axis_size(axis)
    shift = 1
    while shift < count:
        pairs = [(place, place ^ shift) for place in range(count)]
        values = values + lax.ppermute(values, axis, pairs)
        shift *= 2
    return values


def swap(values, axis, first, ring):
    count = lax.axis_size(axis)
    pairs = []
    for place in range(first, count if ring else count - 1, 2):
        beside = (place + 1) % count
        pairs += [(place, beside), (beside, place)]
    return lax.ppermute(values, axis, pairs)


def on_device(tendency, thickness, level_count, block_mask, owner, inertia):
    lon_count = lax.axis_size("lon")
    fields, near, far, side, sent = integrate(
        tendency, thickness, level_count, owner[:, 0], inertia, lon_count
    )
    near = swap(near, "lat", 0, False)
    far = swap(far, "lat", 1, False)
    packed = edges(side, near, far)
    near_edge = swap(packed, "lon", 0, True)
    far_edge = swap(packed, "lon", 1, True)
    w, mw, strip_in, inner = interior(fields, near, far)
    w_edge, mw_edge, sums = strip(strip_in, near_edge, far_edge, inner)
    sums = jnp.broadcast_to(total_over(sums, "lat"), (lon_count,) + sums.shape)
    sent = lax.dynamic_update_slice(sent, sums, (0, sent.shape[1] - ROWS, 0))
    arrived = lax.all_to_all(sent, "lon", split_axis=0, concat_axis=0, tiled=True)
    pressure, residual, held = combine(arrived, w, mw, w_edge, mw_edge)
    held = held.reshape((1, 1, lon_count, 2, held.shape[1] // 2, held.shape[2]))
    return (held, pressure, residual)


def solution(mesh):
    return jax.shard_map(
        on_device,
        mesh=mesh,
        in_specs=(
            P(None, None, "lat", "lon"),
            P(),
            P("lat", "lon"),
            P("lat", "lon"),
            P("lat", "lon"),
            P("lat", "lon"),
        ),
        out_specs=(P("lat", "lon", None, None, None, None), P("lat", "lon"), P("lat", "lon")),
        check_vma=False,
    )
```

```python
import functools

import jax
import jax.numpy as jnp
from jax import lax
from jax.experimental import pallas as pl
from jax.experimental.pallas import tpu as pltpu
from jax.sharding import PartitionSpec as P

STEPS = 4
RIM = STEPS + 1
ROWS = 8
LANES = 128
HALF = LANES // 2
EAST = 48
SEAM = HALF + EAST
CHUNK = 32
FIELDS = 4
VMEM_BYTES = 16 * 1024 * 1024
MIDDLE_BYTES = 56450000


def lanes_of(shape):
    return lax.broadcasted_iota(jnp.int32, shape, len(shape) - 1)


def turn(values, amount):
    amount = amount % values.shape[1]
    return pltpu.roll(values, amount, 1) if amount else values


def is_even(axis):
    return lax.rem(lax.axis_index(axis), 2) == 0


def pack_edges(ref, part):
    cols = ref.shape[2]
    packed = None
    for place in range(FIELDS):
        west = ref[place, part, :LANES]
        east = ref[place, part, cols - LANES :]
        if packed is None:
            lane = lanes_of(west.shape)
            packed = jnp.zeros(west.shape, jnp.float32)
        at = place * RIM
        packed = jnp.where((lane >= at) & (lane < at + RIM), turn(west, at), packed)
        at = HALF + place * RIM
        packed = jnp.where((lane >= at) & (lane < at + RIM), turn(east, at + RIM), packed)
    return packed


def integrate_kernel(bands, outer, thick_hbm, count_hbm, inertia_hbm, tend_hbm, *refs):
    if outer:
        fields_ref, side_ref, near_ref, far_ref = refs[:4]
        above = 0
    else:
        outer_side_hbm, fields_ref, side_ref = refs[:3]
        above = outer_side_hbm.shape[0] // 2
    thick_ref, count_ref, inertia_ref, tend_ref, thick_sem, small_sems, large_sems = refs[-7:]
    levels = tend_hbm.shape[1]
    even = is_even("lat")
    copies = [[pltpu.make_async_copy(thick_hbm, thick_ref, thick_sem)]]
    start = 0
    for place, (row, size) in enumerate(bands):
        there = pl.ds(row, size)
        here = pl.ds(start, size)
        count_copy = pltpu.make_async_copy(
            count_hbm.at[there], count_ref.at[here], small_sems.at[0, place]
        )
        inertia_copy = pltpu.make_async_copy(
            inertia_hbm.at[there], inertia_ref.at[here], small_sems.at[1, place]
        )
        tend_copy = pltpu.make_async_copy(
            tend_hbm.at[:, :, there], tend_ref.at[:, :, here], large_sems.at[place]
        )
        copies.append([count_copy, inertia_copy, tend_copy])
        start += size
    if not outer:
        for place, row in enumerate((0, above + start)):
            copies.append(
                [
                    pltpu.make_async_copy(
                        outer_side_hbm.at[pl.ds(place * above, above)],
                        side_ref.at[pl.ds(row, above)],
                        small_sems.at[place, len(bands)],
                    )
                ]
            )
    for group in copies:
        for copy in group:
            copy.start()
    copies[0][0].wait()
    start = 0
    for place, (row, size) in enumerate(bands):
        part = slice(start, start + size)
        for copy in copies[place + 1]:
            copy.wait()
        count = count_ref[part]
        first = jnp.zeros(count.shape, jnp.float32)
        second = jnp.zeros(count.shape, jnp.float32)
        depth = jnp.zeros(count.shape, jnp.float32)
        for level in range(levels):
            layer = jnp.where(count > level, thick_ref[level], 0.0)
            depth = depth + layer
            first = first + layer * tend_ref[0, level, part].astype(jnp.float32)
            second = second + layer * tend_ref[1, level, part].astype(jnp.float32)
        for field, values in enumerate((first, second, depth, inertia_ref[part])):
            fields_ref[field, part] = values
        side_ref[above + start : above + start + size] = pack_edges(fields_ref, part)
        start += size
    for group in copies[len(bands) + 1 :]:
        for copy in group:
            copy.wait()
    if outer:
        for field in range(FIELDS):
            head = fields_ref[field, :ROWS]
            tail = fields_ref[field, start - ROWS :]
            near_ref[field] = jnp.where(even, tail, head)
            far_ref[field] = jnp.where(even, head, tail)


def integrate(tendency, thickness, level_count, inertia, bands, outer_side=None):
    outer = outer_side is None
    around = [] if outer else [outer_side]
    components, levels, _, cols = tendency.shape
    rows = sum(size for _, size in bands)
    f32 = jnp.float32
    halo = jax.ShapeDtypeStruct((FIELDS, ROWS, cols), f32)
    return pl.pallas_call(
        functools.partial(integrate_kernel, bands, outer),
        in_specs=[pl.BlockSpec(memory_space=pltpu.HBM)] * (4 + len(around)),
        out_shape=[
            jax.ShapeDtypeStruct((FIELDS, rows, cols), f32),
            jax.ShapeDtypeStruct((rows + sum(x.shape[0] for x in around), LANES), f32),
        ]
        + ([halo, halo] if outer else []),
        scratch_shapes=[
            pltpu.SMEM(thickness.shape, f32),
            pltpu.VMEM((rows, cols), jnp.int32),
            pltpu.VMEM((rows, cols), f32),
            pltpu.VMEM((components, levels, rows, cols), tendency.dtype),
            pltpu.SemaphoreType.DMA,
            pltpu.SemaphoreType.DMA((2, len(bands) + 1)),
            pltpu.SemaphoreType.DMA((len(bands),)),
        ],
        cost_estimate=pl.CostEstimate(
            flops=6 * components * levels * rows * cols,
            bytes_accessed=2 * components * levels * rows * cols,
            transcendentals=0,
        ),
        compiler_params=None if outer else pltpu.CompilerParams(vmem_limit_bytes=MIDDLE_BYTES),
        name="outer" if outer else "middle",
    )(thickness, level_count, inertia, tendency, *around)


def edges_kernel(side_ref, near_ref, far_ref, out_ref):
    rows = side_ref.shape[0]
    even = is_even("lat")
    near = pack_edges(near_ref, slice(None))
    far = pack_edges(far_ref, slice(None))
    out_ref[:ROWS] = jnp.where(even, far, near)
    out_ref[ROWS : ROWS + rows] = side_ref[...]
    out_ref[ROWS + rows :] = jnp.where(even, near, far)


def edges(side, near, far):
    rows = side.shape[0] + 2 * ROWS
    return pl.pallas_call(
        edges_kernel,
        out_shape=jax.ShapeDtypeStruct((rows, LANES), jnp.float32),
        compiler_params=pltpu.CompilerParams(vmem_limit_bytes=VMEM_BYTES),
        name="edges",
    )(side, near, far)


def smooth(field):
    rows, cols = field.shape
    tall = field + 0.5 * (pltpu.roll(field, 1, 0) + pltpu.roll(field, rows - 1, 0))
    return tall + 0.5 * (pltpu.roll(tall, 1, 1) + pltpu.roll(tall, cols - 1, 1))


def basis(first, second, depth, inertia):
    tall, wide = first.shape
    own = slice(ROWS, tall - ROWS)
    inside = inertia > 0.0
    east_west = pltpu.roll(first, wide - 1, 1) - pltpu.roll(first, 1, 1)
    north_south = pltpu.roll(second, tall - 1, 0) - pltpu.roll(second, 1, 0)
    scaled = jnp.where(depth > 0.0, 0.5 * (east_west + north_south), 0.0)
    diag = inertia + 2.0 * depth + smooth(depth)
    inverse = jnp.where(inside, 1.0 / jnp.where(inside, diag, 1.0), 0.0)
    mws = [scaled[own]]
    ws = []
    vector = scaled * inverse
    for step in range(STEPS):
        ws.append(vector[own])
        weighed = depth * vector
        scaled = depth * smooth(vector) + smooth(weighed) - 2.0 * weighed
        mws.append(scaled[own])
        if step + 1 < STEPS:
            vector = scaled * inverse
    return ws, mws


def moments(ws, mws, mask):
    ws = [jnp.where(mask, values, 0.0) for values in ws]
    images = [mws[place] - mws[place + 1] for place in range(STEPS)]
    pairs = [ws[place] * mws[0] for place in range(STEPS)]
    for low in range(STEPS):
        for high in range(low, STEPS):
            pairs.append(ws[low] * images[high])
    lower = lanes_of((1, LANES)) < HALF
    lines = []
    for product in pairs:
        line = jnp.sum(product, axis=0, keepdims=True)
        total = line[:, :LANES]
        for start in range(LANES, line.shape[1], LANES):
            total = total + line[:, start : start + LANES]
        lines.append(total + turn(total, HALF))
    packed = [
        jnp.where(lower, lines[place], lines[place + 1]) for place in range(0, len(lines), 2)
    ]
    packed.append(jnp.zeros((ROWS - len(packed), LANES), jnp.float32))
    return jnp.concatenate(packed, axis=0)


def interior_kernel(
    owner_ref,
    outer_ref,
    middle_ref,
    near_ref,
    far_ref,
    w_ref,
    mw_ref,
    strip_ref,
    sums_ref,
    sent_ref,
):
    half = outer_ref.shape[1] // 2
    cols = outer_ref.shape[2]
    even = is_even("lat")
    lane = lanes_of((strip_ref.shape[1], LANES))
    padded = []
    for place in range(FIELDS):
        near = near_ref[place]
        far = far_ref[place]
        values = jnp.concatenate(
            [
                jnp.where(even, far, near),
                outer_ref[place, :half],
                middle_ref[place],
                outer_ref[place, half:],
                jnp.where(even, near, far),
            ],
            axis=0,
        )
        east = turn(values[:, cols - LANES :], SEAM)
        strip_ref[place] = jnp.where(lane < HALF, values[:, :LANES], east)
        padded.append(values)
    span = (sent_ref.shape[1] - ROWS) // 2
    sent_ref[...] = jnp.zeros(sent_ref.shape, jnp.float32)
    for block in range(owner_ref.shape[0]):
        target = owner_ref[block]
        rows = slice(ROWS + block * span, ROWS + (block + 1) * span)

        @pl.when(target >= 0)
        def _(target=target, rows=rows):
            sent_ref[target, :span] = padded[0][rows]
            sent_ref[target, span : 2 * span] = padded[1][rows]

    ws, mws = basis(*padded)
    for place, values in enumerate(ws):
        w_ref[place] = values
    for place, values in enumerate(mws):
        mw_ref[place] = values
    lane = lanes_of(ws[0].shape)
    sums_ref[...] = moments(ws, mws, (lane >= RIM) & (lane < cols - RIM))


def interior(owner, outer, middle, near, far, lon_count):
    cols = outer.shape[2]
    rows = outer.shape[1] + middle.shape[1]
    span = rows // owner.shape[0]
    f32 = jnp.float32
    return pl.pallas_call(
        interior_kernel,
        in_specs=[pl.BlockSpec(memory_space=pltpu.SMEM)]
        + [pl.BlockSpec(memory_space=pltpu.VMEM)] * 4,
        out_shape=[
            jax.ShapeDtypeStruct((STEPS, rows, cols), f32),
            jax.ShapeDtypeStruct((STEPS + 1, rows, cols), f32),
            jax.ShapeDtypeStruct((FIELDS, rows + 2 * ROWS, LANES), f32),
            jax.ShapeDtypeStruct((ROWS, LANES), f32),
            jax.ShapeDtypeStruct((lon_count, 2 * span + ROWS, cols), f32),
        ],
        compiler_params=pltpu.CompilerParams(vmem_limit_bytes=VMEM_BYTES),
        cost_estimate=pl.CostEstimate(
            flops=300 * rows * cols, bytes_accessed=64 * rows * cols, transcendentals=0
        ),
        name="interior",
    )(owner, outer, middle, near, far)


def strip_kernel(strip_in_ref, near_ref, far_ref, inner_ref, w_ref, mw_ref, sums_ref):
    even = is_even("lon")
    near = near_ref[...]
    far = far_ref[...]
    from_east = jnp.where(even, near, far)
    from_west = jnp.where(even, far, near)
    lane = lanes_of(near.shape)
    padded = []
    for place in range(FIELDS):
        at = place * RIM
        east = turn(from_east, SEAM - at)
        west = turn(from_west, HALF - RIM - at)
        halo = jnp.where(lane < SEAM + RIM, east, jnp.where(lane >= LANES - RIM, west, 0.0))
        padded.append(jnp.where(lane < SEAM, strip_in_ref[place], halo))
    ws, mws = basis(*padded)
    for place, values in enumerate(ws):
        w_ref[place] = values
    for place, values in enumerate(mws):
        mw_ref[place] = values
    lane = lanes_of(ws[0].shape)
    edge = (lane < RIM) | ((lane >= SEAM - RIM) & (lane < SEAM))
    sums_ref[...] = inner_ref[...] + moments(ws, mws, edge)


def strip(strip_in, near, far, inner):
    rows = strip_in.shape[1] - 2 * ROWS
    f32 = jnp.float32
    return pl.pallas_call(
        strip_kernel,
        out_shape=[
            jax.ShapeDtypeStruct((STEPS, rows, LANES), f32),
            jax.ShapeDtypeStruct((STEPS + 1, rows, LANES), f32),
            jax.ShapeDtypeStruct((ROWS, LANES), f32),
        ],
        compiler_params=pltpu.CompilerParams(vmem_limit_bytes=VMEM_BYTES),
        name="strip",
    )(strip_in, near, far, inner)


def combine_kernel(
    arrived_ref, w_ref, mw_ref, w_edge_ref, mw_edge_ref, pressure_ref, residual_ref, held_ref
):
    held_ref[...] = arrived_ref[:, : held_ref.shape[1]]
    packed = jnp.sum(arrived_ref[:, held_ref.shape[1] :, :LANES], axis=0)
    lower = lanes_of(packed.shape) < HALF
    totals = (
        jnp.sum(jnp.where(lower, packed, 0.0), axis=1, keepdims=True),
        jnp.sum(jnp.where(lower, 0.0, packed), axis=1, keepdims=True),
    )
    entry = lambda place: totals[place % 2][place // 2 : place // 2 + 1, :]
    right = [entry(place) for place in range(STEPS)]
    matrix = {}
    place = STEPS
    for low in range(STEPS):
        for high in range(low, STEPS):
            matrix[low, high] = entry(place)
            place += 1
    for pivot in range(STEPS):
        inverse = 1.0 / matrix[pivot, pivot]
        for row in range(pivot + 1, STEPS):
            factor = matrix[pivot, row] * inverse
            for col in range(row, STEPS):
                matrix[row, col] = matrix[row, col] - factor * matrix[pivot, col]
            right[row] = right[row] - factor * right[pivot]
        matrix[pivot, pivot] = inverse
    for pivot in reversed(range(STEPS)):
        for col in range(pivot + 1, STEPS):
            right[pivot] = right[pivot] - matrix[pivot, col] * right[col]
        right[pivot] = right[pivot] * matrix[pivot, pivot]

    def results(w_ref, mw_ref):
        pressure = right[0] * w_ref[0]
        residual = mw_ref[0] - right[0] * (mw_ref[0] - mw_ref[1])
        for place in range(1, STEPS):
            pressure = pressure + right[place] * w_ref[place]
            residual = residual - right[place] * (mw_ref[place] - mw_ref[place + 1])
        return pressure, residual

    inner = results(w_ref, mw_ref)
    edge = results(w_edge_ref, mw_edge_ref)
    cols = pressure_ref.shape[1]
    lane = lanes_of(edge[0].shape)
    for out_ref, inside, border in zip((pressure_ref, residual_ref), inner, edge):
        out_ref[:, :LANES] = jnp.where(lane < RIM, border, inside[:, :LANES])
        if cols > 2 * LANES:
            out_ref[:, LANES : cols - LANES] = inside[:, LANES : cols - LANES]
        out_ref[:, cols - LANES :] = jnp.where(
            lane >= LANES - RIM, turn(border, -SEAM), inside[:, cols - LANES :]
        )


def combine(arrived, w, mw, w_edge, mw_edge):
    slots, rows, cols = arrived.shape
    shape = jax.ShapeDtypeStruct(w.shape[1:], jnp.float32)
    return pl.pallas_call(
        combine_kernel,
        out_shape=[shape, shape, jax.ShapeDtypeStruct((slots, rows - ROWS, cols), jnp.float32)],
        compiler_params=pltpu.CompilerParams(vmem_limit_bytes=VMEM_BYTES),
        name="combine",
    )(arrived, w, mw, w_edge, mw_edge)


def total_over(values, axis):
    count = lax.axis_size(axis)
    shift = 1
    while shift < count:
        pairs = [(place, place ^ shift) for place in range(count)]
        values = values + lax.ppermute(values, axis, pairs)
        shift *= 2
    return values


def swap(values, axis, first, ring):
    count = lax.axis_size(axis)
    pairs = []
    for place in range(first, count if ring else count - 1, 2):
        beside = (place + 1) % count
        pairs += [(place, beside), (beside, place)]
    return lax.ppermute(values, axis, pairs)


def on_device(tendency, thickness, level_count, block_mask, owner, inertia):
    lon_count = lax.axis_size("lon")
    rows = level_count.shape[0]
    tall = min(CHUNK, rows // 4)
    inputs = (tendency, thickness, level_count, inertia)
    outer, outer_side, near, far = integrate(*inputs, ((0, tall), (rows - tall, tall)))
    bands = tuple((row, tall) for row in range(tall, rows - tall, tall))
    middle, side = integrate(*inputs, bands, outer_side)
    near = swap(near, "lat", 0, False)
    far = swap(far, "lat", 1, False)
    packed = edges(side, near, far)
    near_edge = swap(packed, "lon", 0, True)
    far_edge = swap(packed, "lon", 1, True)
    w, mw, strip_in, inner, sent = interior(owner[:, 0], outer, middle, near, far, lon_count)
    w_edge, mw_edge, sums = strip(strip_in, near_edge, far_edge, inner)
    sums = jnp.broadcast_to(total_over(sums, "lat"), (lon_count,) + sums.shape)
    sent = lax.dynamic_update_slice(sent, sums, (0, sent.shape[1] - ROWS, 0))
    arrived = lax.all_to_all(sent, "lon", split_axis=0, concat_axis=0, tiled=True)
    pressure, residual, held = combine(arrived, w, mw, w_edge, mw_edge)
    held = held.reshape((1, 1, lon_count, 2, held.shape[1] // 2, held.shape[2]))
    return (held, pressure, residual)


def solution(mesh):
    return jax.shard_map(
        on_device,
        mesh=mesh,
        in_specs=(
            P(None, None, "lat", "lon"),
            P(),
            P("lat", "lon"),
            P("lat", "lon"),
            P("lat", "lon"),
            P("lat", "lon"),
        ),
        out_specs=(P("lat", "lon", None, None, None, None), P("lat", "lon"), P("lat", "lon")),
        check_vma=False,
    )
```

```python
import functools

import jax
import jax.numpy as jnp
from jax import lax
from jax.experimental import pallas as pl
from jax.experimental.pallas import tpu as pltpu
from jax.sharding import PartitionSpec as P

STEPS = 4
RIM = STEPS + 1
ROWS = 8
LANES = 128
HALF = LANES // 2
QUARTER = LANES // 4
EAST = 48
SEAM = HALF + EAST
CHUNK = 32
FIELDS = 4
GROUPS = 6
PITCH = LANES // GROUPS
TAIL = 16
SUM_ROWS = 4
VMEM_BYTES = 16 * 1024 * 1024
MIDDLE_BYTES = 56450000


def lanes_of(shape):
    return lax.broadcasted_iota(jnp.int32, shape, len(shape) - 1)


def turn(values, amount):
    amount = amount % values.shape[1]
    return pltpu.roll(values, amount, 1) if amount else values


def is_even(axis):
    return lax.rem(lax.axis_index(axis), 2) == 0


def pack_edges(ref, part):
    cols = ref.shape[2]
    packed = None
    for place in range(FIELDS):
        west = ref[place, part, :LANES]
        east = ref[place, part, cols - LANES :]
        if packed is None:
            lane = lanes_of(west.shape)
            packed = jnp.zeros(west.shape, jnp.float32)
        at = place * RIM
        packed = jnp.where((lane >= at) & (lane < at + RIM), turn(west, at), packed)
        at = HALF + place * RIM
        packed = jnp.where((lane >= at) & (lane < at + RIM), turn(east, at + RIM), packed)
    return packed


def integrate_kernel(bands, outer, thick_hbm, count_hbm, inertia_hbm, tend_hbm, *refs):
    if outer:
        fields_ref, side_ref, near_ref, far_ref = refs[:4]
    else:
        fields_ref, side_ref = refs[:2]
    thick_ref, count_ref, inertia_ref, tend_ref, thick_sem, small_sems, large_sems = refs[-7:]
    levels = tend_hbm.shape[1]
    even = is_even("lat")
    copies = [[pltpu.make_async_copy(thick_hbm, thick_ref, thick_sem)]]
    start = 0
    for place, (row, size) in enumerate(bands):
        there = pl.ds(row, size)
        here = pl.ds(start, size)
        count_copy = pltpu.make_async_copy(
            count_hbm.at[there], count_ref.at[here], small_sems.at[0, place]
        )
        inertia_copy = pltpu.make_async_copy(
            inertia_hbm.at[there], inertia_ref.at[here], small_sems.at[1, place]
        )
        tend_copy = pltpu.make_async_copy(
            tend_hbm.at[:, :, there], tend_ref.at[:, :, here], large_sems.at[place]
        )
        copies.append([count_copy, inertia_copy, tend_copy])
        start += size
    for group in copies:
        for copy in group:
            copy.start()
    copies[0][0].wait()
    start = 0
    for place, (row, size) in enumerate(bands):
        part = slice(start, start + size)
        for copy in copies[place + 1]:
            copy.wait()
        count = count_ref[part]
        first = jnp.zeros(count.shape, jnp.float32)
        second = jnp.zeros(count.shape, jnp.float32)
        depth = jnp.zeros(count.shape, jnp.float32)
        for level in range(levels):
            layer = jnp.where(count > level, thick_ref[level], 0.0)
            depth = depth + layer
            first = first + layer * tend_ref[0, level, part].astype(jnp.float32)
            second = second + layer * tend_ref[1, level, part].astype(jnp.float32)
        for field, values in enumerate((first, second, depth, inertia_ref[part])):
            fields_ref[field, part] = values
        side_ref[part] = pack_edges(fields_ref, part)
        start += size
    if outer:
        for field in range(FIELDS):
            head = fields_ref[field, :ROWS]
            tail = fields_ref[field, start - ROWS :]
            near_ref[field] = jnp.where(even, tail, head)
            far_ref[field] = jnp.where(even, head, tail)


def integrate(tendency, thickness, level_count, inertia, bands, outer):
    components, levels, _, cols = tendency.shape
    rows = sum(size for _, size in bands)
    f32 = jnp.float32
    halo = jax.ShapeDtypeStruct((FIELDS, ROWS, cols), f32)
    return pl.pallas_call(
        functools.partial(integrate_kernel, bands, outer),
        in_specs=[pl.BlockSpec(memory_space=pltpu.HBM)] * 4,
        out_shape=[
            jax.ShapeDtypeStruct((FIELDS, rows, cols), f32),
            jax.ShapeDtypeStruct((rows, LANES), f32),
        ]
        + ([halo, halo] if outer else []),
        scratch_shapes=[
            pltpu.SMEM(thickness.shape, f32),
            pltpu.VMEM((rows, cols), jnp.int32),
            pltpu.VMEM((rows, cols), f32),
            pltpu.VMEM((components, levels, rows, cols), tendency.dtype),
            pltpu.SemaphoreType.DMA,
            pltpu.SemaphoreType.DMA((2, len(bands))),
            pltpu.SemaphoreType.DMA((len(bands),)),
        ],
        cost_estimate=pl.CostEstimate(
            flops=6 * components * levels * rows * cols,
            bytes_accessed=2 * components * levels * rows * cols,
            transcendentals=0,
        ),
        compiler_params=None if outer else pltpu.CompilerParams(vmem_limit_bytes=MIDDLE_BYTES),
        name="outer" if outer else "middle",
    )(thickness, level_count, inertia, tendency)


def edges_kernel(outer_ref, middle_ref, near_ref, far_ref, near_out_ref, far_out_ref):
    even_lat = is_even("lat")
    even_lon = is_even("lon")
    near = pack_edges(near_ref, slice(None))
    far = pack_edges(far_ref, slice(None))
    half = outer_ref.shape[0] // 2
    packed = jnp.concatenate(
        [
            jnp.where(even_lat, far, near),
            outer_ref[:half],
            middle_ref[...],
            outer_ref[half:],
            jnp.where(even_lat, near, far),
        ],
        axis=0,
    )
    size = near_out_ref.shape[0]
    lane = lanes_of(near_out_ref.shape)
    west = jnp.zeros(near_out_ref.shape, jnp.float32)
    east = jnp.zeros(near_out_ref.shape, jnp.float32)
    for group in range(GROUPS):
        rows = packed[group * size : (group + 1) * size]
        at = group * PITCH
        here = (lane >= at) & (lane < at + PITCH)
        west = jnp.where(here, turn(rows, at), west)
        east = jnp.where(here, turn(rows, at - HALF), east)
    near_out_ref[...] = jnp.where(even_lon, east, west)
    far_out_ref[...] = jnp.where(even_lon, west, east)


def edges(outer, middle, near, far):
    rows = outer.shape[0] + middle.shape[0] + 2 * ROWS
    message = jax.ShapeDtypeStruct((rows // GROUPS, LANES), jnp.float32)
    return pl.pallas_call(
        edges_kernel,
        out_shape=[message, message],
        compiler_params=pltpu.CompilerParams(vmem_limit_bytes=VMEM_BYTES),
        name="edges",
    )(outer, middle, near, far)


def smooth(field):
    rows, cols = field.shape
    tall = field + 0.5 * (pltpu.roll(field, 1, 0) + pltpu.roll(field, rows - 1, 0))
    return tall + 0.5 * (pltpu.roll(tall, 1, 1) + pltpu.roll(tall, cols - 1, 1))


def basis(first, second, depth, inertia):
    tall, wide = first.shape
    own = slice(ROWS, tall - ROWS)
    inside = inertia > 0.0
    east_west = pltpu.roll(first, wide - 1, 1) - pltpu.roll(first, 1, 1)
    north_south = pltpu.roll(second, tall - 1, 0) - pltpu.roll(second, 1, 0)
    scaled = jnp.where(depth > 0.0, 0.5 * (east_west + north_south), 0.0)
    diag = inertia + 2.0 * depth + smooth(depth)
    inverse = jnp.where(inside, 1.0 / jnp.where(inside, diag, 1.0), 0.0)
    mws = [scaled[own]]
    ws = []
    vector = scaled * inverse
    for step in range(STEPS):
        ws.append(vector[own])
        weighed = depth * vector
        scaled = depth * smooth(vector) + smooth(weighed) - 2.0 * weighed
        mws.append(scaled[own])
        if step + 1 < STEPS:
            vector = scaled * inverse
    return ws, mws


def moments(ws, mws, mask):
    ws = [jnp.where(mask, values, 0.0) for values in ws]
    images = [mws[place] - mws[place + 1] for place in range(STEPS)]
    pairs = [ws[place] * mws[0] for place in range(STEPS)]
    for low in range(STEPS):
        for high in range(low, STEPS):
            pairs.append(ws[low] * images[high])
    lines = []
    for product in pairs:
        line = jnp.sum(product, axis=0, keepdims=True)
        total = line[:, :LANES]
        for start in range(LANES, line.shape[1], LANES):
            total = total + line[:, start : start + LANES]
        total = total + turn(total, HALF)
        lines.append(total + turn(total, QUARTER))
    quarter = lanes_of((1, LANES)) // QUARTER
    packed = []
    for start in range(0, len(lines), 4):
        row = jnp.zeros((1, LANES), jnp.float32)
        for place, line in enumerate(lines[start : start + 4]):
            row = jnp.where(quarter == place, line, row)
        packed.append(row)
    packed.append(jnp.zeros((ROWS - len(packed), LANES), jnp.float32))
    return jnp.concatenate(packed, axis=0)


def interior_kernel(
    outer_ref,
    middle_ref,
    near_ref,
    far_ref,
    w_ref,
    mw_ref,
    strip_ref,
    sums_ref,
):
    half = outer_ref.shape[1] // 2
    cols = outer_ref.shape[2]
    even = is_even("lat")
    lane = lanes_of((strip_ref.shape[1], LANES))
    padded = []
    for place in range(FIELDS):
        near = near_ref[place]
        far = far_ref[place]
        values = jnp.concatenate(
            [
                jnp.where(even, far, near),
                outer_ref[place, :half],
                middle_ref[place],
                outer_ref[place, half:],
                jnp.where(even, near, far),
            ],
            axis=0,
        )
        east = turn(values[:, cols - LANES :], SEAM)
        strip_ref[place] = jnp.where(lane < HALF, values[:, :LANES], east)
        padded.append(values)
    ws, mws = basis(*padded)
    for place, values in enumerate(ws):
        w_ref[place] = values
    for place, values in enumerate(mws):
        mw_ref[place] = values
    lane = lanes_of(ws[0].shape)
    sums_ref[...] = moments(ws, mws, (lane >= RIM) & (lane < cols - RIM))


def interior(outer, middle, near, far):
    cols = outer.shape[2]
    rows = outer.shape[1] + middle.shape[1]
    f32 = jnp.float32
    return pl.pallas_call(
        interior_kernel,
        out_shape=[
            jax.ShapeDtypeStruct((STEPS, rows, cols), f32),
            jax.ShapeDtypeStruct((STEPS + 1, rows, cols), f32),
            jax.ShapeDtypeStruct((FIELDS, rows + 2 * ROWS, LANES), f32),
            jax.ShapeDtypeStruct((ROWS, LANES), f32),
        ],
        compiler_params=pltpu.CompilerParams(vmem_limit_bytes=VMEM_BYTES),
        cost_estimate=pl.CostEstimate(
            flops=300 * rows * cols, bytes_accessed=64 * rows * cols, transcendentals=0
        ),
        name="interior",
    )(outer, middle, near, far)


def strip_kernel(strip_in_ref, near_ref, far_ref, inner_ref, w_ref, mw_ref, sums_ref):
    even = is_even("lon")
    near = near_ref[...]
    far = far_ref[...]
    from_east = jnp.where(even, near, far)
    from_west = jnp.where(even, far, near)
    lane = lanes_of(near.shape)
    padded = []
    for place in range(FIELDS):
        halo = []
        for group in range(GROUPS):
            at = group * PITCH + place * RIM
            east = turn(from_east, SEAM - at)
            west = turn(from_west, LANES - RIM - at)
            west = jnp.where(lane >= LANES - RIM, west, 0.0)
            halo.append(jnp.where(lane < SEAM + RIM, east, west))
        halo = jnp.concatenate(halo, axis=0)
        padded.append(jnp.where(lanes_of(halo.shape) < SEAM, strip_in_ref[place], halo))
    ws, mws = basis(*padded)
    for place, values in enumerate(ws):
        w_ref[place] = values
    for place, values in enumerate(mws):
        mw_ref[place] = values
    lane = lanes_of(ws[0].shape)
    edge = (lane < RIM) | ((lane >= SEAM - RIM) & (lane < SEAM))
    sums_ref[...] = inner_ref[...] + moments(ws, mws, edge)


def strip(strip_in, near, far, inner):
    rows = strip_in.shape[1] - 2 * ROWS
    f32 = jnp.float32
    return pl.pallas_call(
        strip_kernel,
        out_shape=[
            jax.ShapeDtypeStruct((STEPS, rows, LANES), f32),
            jax.ShapeDtypeStruct((STEPS + 1, rows, LANES), f32),
            jax.ShapeDtypeStruct((ROWS, LANES), f32),
        ],
        compiler_params=pltpu.CompilerParams(vmem_limit_bytes=VMEM_BYTES),
        name="strip",
    )(strip_in, near, far, inner)


def power(exponent):
    size = jnp.abs(exponent)
    value = jnp.ones(exponent.shape, jnp.float32)
    for bit in range(7):
        up, down = 2.0 ** (1 << bit), 2.0 ** -(1 << bit)
        factor = jnp.where(exponent < 0, down, up)
        value = value * jnp.where((size >> bit) & 1 == 1, factor, 1.0)
    return value


def exponent_of(size):
    bits = jnp.ceil(jnp.log2(jnp.maximum(size, 2.0**-100)))
    return jnp.clip(bits, -100.0, 100.0).astype(jnp.int32)


def nearest(values):
    return jnp.floor(values + 0.5)


def place_kernel(owner_ref, outer_ref, middle_ref, sent_ref, scale_ref):
    count = owner_ref.shape[0]
    edge = outer_ref.shape[1] // 2
    between = middle_ref.shape[1]
    span = (2 * edge + between) // count
    sent_ref[...] = jnp.zeros(sent_ref.shape, jnp.int16)
    scale_ref[...] = jnp.zeros(scale_ref.shape, jnp.float32)
    for block in range(count):
        row = block * span
        if row < edge:
            ref, row = outer_ref, row
        elif row < edge + between:
            ref, row = middle_ref, row - edge
        else:
            ref, row = outer_ref, row - between
        target = owner_ref[block]

        @pl.when(target >= 0)
        def _(ref=ref, row=row, target=target):
            for half in range(ref.shape[2] // LANES):
                cols = slice(half * LANES, (half + 1) * LANES)
                rows = slice(row, row + span)
                values = jnp.concatenate([ref[0, rows, cols], ref[1, rows, cols]], axis=0)
                bits = exponent_of(jnp.max(jnp.abs(values), axis=0, keepdims=True))
                whole = jnp.clip(nearest(values * power(15 - bits)), -32767.0, 32767.0)
                there = slice(2 * span * half, 2 * span * (half + 1))
                sent_ref[target, there] = whole.astype(jnp.int32).astype(jnp.int16)
                scale_ref[target, half : half + 1] = bits.astype(jnp.float32)


def place(owner, outer, middle, lon_count):
    cols = outer.shape[2]
    rows = outer.shape[1] + middle.shape[1]
    span = rows // owner.shape[0]
    return pl.pallas_call(
        place_kernel,
        in_specs=[pl.BlockSpec(memory_space=pltpu.SMEM)]
        + [pl.BlockSpec(memory_space=pltpu.VMEM)] * 2,
        out_shape=[
            jax.ShapeDtypeStruct((lon_count, cols // LANES * 2 * span + TAIL, LANES), jnp.int16),
            jax.ShapeDtypeStruct((lon_count, ROWS, LANES), jnp.float32),
        ],
        compiler_params=pltpu.CompilerParams(vmem_limit_bytes=VMEM_BYTES),
        cost_estimate=pl.CostEstimate(
            flops=60 * rows * cols, bytes_accessed=12 * rows * cols, transcendentals=0
        ),
        name="place",
    )(owner, outer, middle)


def seal_kernel(sums_ref, other_ref, scale_ref, tail_ref):
    sums = sums_ref[:SUM_ROWS] + other_ref[:SUM_ROWS]
    bits = exponent_of(jnp.abs(sums))
    scaled = sums * power(-bits) * 2.0**14
    high = nearest(scaled)
    low = nearest((scaled - high) * 2.0**15)
    parts = jnp.concatenate([bits.astype(jnp.float32), high, low], axis=0)
    for slot in range(tail_ref.shape[0]):
        tile = jnp.concatenate([parts, scale_ref[slot, : TAIL - 3 * SUM_ROWS]], axis=0)
        tail_ref[slot] = tile.astype(jnp.int32).astype(jnp.int16)


def seal(sums, other, scale):
    return pl.pallas_call(
        seal_kernel,
        out_shape=jax.ShapeDtypeStruct((scale.shape[0], TAIL, LANES), jnp.int16),
        compiler_params=pltpu.CompilerParams(vmem_limit_bytes=VMEM_BYTES),
        name="seal",
    )(sums, other, scale)


def combine_kernel(
    arrived_ref, w_ref, mw_ref, w_edge_ref, mw_edge_ref, pressure_ref, residual_ref, held_ref
):
    rows = held_ref.shape[1]
    packed = jnp.zeros((SUM_ROWS, LANES), jnp.float32)
    for slot in range(held_ref.shape[0]):
        tail = arrived_ref[slot, arrived_ref.shape[1] - TAIL :].astype(jnp.int32)
        digits = tail.astype(jnp.float32)
        high = digits[SUM_ROWS : 2 * SUM_ROWS]
        low = digits[2 * SUM_ROWS : 3 * SUM_ROWS]
        packed = packed + (high + low * 2.0**-15) * power(tail[:SUM_ROWS] - 14)
        for half in range(held_ref.shape[2] // LANES):
            at = 3 * SUM_ROWS + half
            scale = power(tail[at : at + 1] - 15)
            whole = arrived_ref[slot, half * rows : (half + 1) * rows].astype(jnp.int32)
            held_ref[slot, :, half * LANES : (half + 1) * LANES] = whole.astype(jnp.float32) * scale
    quarter = lanes_of(packed.shape) // QUARTER
    totals = [
        jnp.sum(jnp.where(quarter == place, packed, 0.0), axis=1, keepdims=True)
        for place in range(4)
    ]
    entry = lambda place: totals[place % 4][place // 4 : place // 4 + 1, :]
    right = [entry(place) for place in range(STEPS)]
    matrix = {}
    place = STEPS
    for low in range(STEPS):
        for high in range(low, STEPS):
            matrix[low, high] = entry(place)
            place += 1
    for pivot in range(STEPS):
        inverse = 1.0 / matrix[pivot, pivot]
        for row in range(pivot + 1, STEPS):
            factor = matrix[pivot, row] * inverse
            for col in range(row, STEPS):
                matrix[row, col] = matrix[row, col] - factor * matrix[pivot, col]
            right[row] = right[row] - factor * right[pivot]
        matrix[pivot, pivot] = inverse
    for pivot in reversed(range(STEPS)):
        for col in range(pivot + 1, STEPS):
            right[pivot] = right[pivot] - matrix[pivot, col] * right[col]
        right[pivot] = right[pivot] * matrix[pivot, pivot]

    def results(w_ref, mw_ref):
        pressure = right[0] * w_ref[0]
        residual = mw_ref[0] - right[0] * (mw_ref[0] - mw_ref[1])
        for place in range(1, STEPS):
            pressure = pressure + right[place] * w_ref[place]
            residual = residual - right[place] * (mw_ref[place] - mw_ref[place + 1])
        return pressure, residual

    inner = results(w_ref, mw_ref)
    edge = results(w_edge_ref, mw_edge_ref)
    cols = pressure_ref.shape[1]
    lane = lanes_of(edge[0].shape)
    for out_ref, inside, border in zip((pressure_ref, residual_ref), inner, edge):
        out_ref[:, :LANES] = jnp.where(lane < RIM, border, inside[:, :LANES])
        if cols > 2 * LANES:
            out_ref[:, LANES : cols - LANES] = inside[:, LANES : cols - LANES]
        out_ref[:, cols - LANES :] = jnp.where(
            lane >= LANES - RIM, turn(border, -SEAM), inside[:, cols - LANES :]
        )


def combine(arrived, w, mw, w_edge, mw_edge):
    rows, cols = w.shape[1:]
    shape = jax.ShapeDtypeStruct((rows, cols), jnp.float32)
    held = (arrived.shape[0], (arrived.shape[1] - TAIL) * LANES // cols, cols)
    return pl.pallas_call(
        combine_kernel,
        out_shape=[shape, shape, jax.ShapeDtypeStruct(held, jnp.float32)],
        compiler_params=pltpu.CompilerParams(vmem_limit_bytes=VMEM_BYTES),
        name="combine",
    )(arrived, w, mw, w_edge, mw_edge)


def exchange(values, axis, distance):
    pairs = [(place, place ^ distance) for place in range(lax.axis_size(axis))]
    return lax.ppermute(values, axis, pairs)


def swap(values, axis, first, ring):
    count = lax.axis_size(axis)
    pairs = []
    for place in range(first, count if ring else count - 1, 2):
        beside = (place + 1) % count
        pairs += [(place, beside), (beside, place)]
    return lax.ppermute(values, axis, pairs)


def on_device(tendency, thickness, level_count, block_mask, owner, inertia):
    lat_count = lax.axis_size("lat")
    lon_count = lax.axis_size("lon")
    rows = level_count.shape[0]
    tall = min(CHUNK, rows // 4)
    inputs = (tendency, thickness, level_count, inertia)
    outer, outer_side, near, far = integrate(*inputs, ((0, tall), (rows - tall, tall)), True)
    bands = tuple((row, tall) for row in range(tall, rows - tall, tall))
    middle, middle_side = integrate(*inputs, bands, False)
    near = swap(near, "lat", 0, False)
    far = swap(far, "lat", 1, False)
    near_edge, far_edge = edges(outer_side, middle_side, near, far)
    near_edge = swap(near_edge, "lon", 0, True)
    far_edge = swap(far_edge, "lon", 1, True)
    w, mw, strip_in, inner = interior(outer, middle, near, far)
    w_edge, mw_edge, sums = strip(strip_in, near_edge, far_edge, inner)
    sent, scale = place(owner[:, 0], outer, middle, lon_count)
    shift = 1
    while 2 * shift < lat_count:
        sums = sums + exchange(sums, "lat", shift)
        shift *= 2
    tail = seal(sums, exchange(sums, "lat", shift), scale)
    sent = lax.dynamic_update_slice(sent, tail, (0, sent.shape[1] - TAIL, 0))
    arrived = lax.all_to_all(sent, "lon", split_axis=0, concat_axis=0, tiled=True)
    pressure, residual, held = combine(arrived, w, mw, w_edge, mw_edge)
    held = held.reshape((1, 1, lon_count, 2, held.shape[1] // 2, held.shape[2]))
    return (held, pressure, residual)


def solution(mesh):
    return jax.shard_map(
        on_device,
        mesh=mesh,
        in_specs=(
            P(None, None, "lat", "lon"),
            P(),
            P("lat", "lon"),
            P("lat", "lon"),
            P("lat", "lon"),
            P("lat", "lon"),
        ),
        out_specs=(P("lat", "lon", None, None, None, None), P("lat", "lon"), P("lat", "lon")),
        check_vma=False,
    )
```

```python
import functools

import jax
import jax.numpy as jnp
from jax import lax
from jax.experimental import pallas as pl
from jax.experimental.pallas import tpu as pltpu
from jax.sharding import PartitionSpec as P

STEPS = 4
RIM = STEPS + 1
ROWS = 8
LANES = 128
HALF = LANES // 2
QUARTER = LANES // 4
EAST = 48
SEAM = HALF + EAST
CHUNK = 32
FIELDS = 4
GROUPS = 6
PITCH = LANES // GROUPS
OUTER = 16
TAIL = 16
SUM_ROWS = 4
VMEM_BYTES = 16 * 1024 * 1024
MIDDLE_BYTES = 56450000


def lanes_of(shape):
    return lax.broadcasted_iota(jnp.int32, shape, len(shape) - 1)


def turn(values, amount):
    amount = amount % values.shape[1]
    return pltpu.roll(values, amount, 1) if amount else values


def is_even(axis):
    return lax.rem(lax.axis_index(axis), 2) == 0


def pack_edges(ref, part):
    cols = ref.shape[2]
    packed = None
    for place in range(FIELDS):
        west = ref[place, part, :LANES]
        east = ref[place, part, cols - LANES :]
        if packed is None:
            lane = lanes_of(west.shape)
            packed = jnp.zeros(west.shape, jnp.float32)
        at = place * RIM
        packed = jnp.where((lane >= at) & (lane < at + RIM), turn(west, at), packed)
        at = HALF + place * RIM
        packed = jnp.where((lane >= at) & (lane < at + RIM), turn(east, at + RIM), packed)
    return packed


def integrate_kernel(bands, outer, thick_hbm, count_hbm, inertia_hbm, tend_hbm, *refs):
    if outer:
        fields_ref, side_ref, near_ref, far_ref = refs[:4]
    else:
        fields_ref, side_ref = refs[:2]
    thick_ref, count_ref, inertia_ref, tend_ref, thick_sem, small_sems, large_sems = refs[-7:]
    levels = tend_hbm.shape[1]
    even = is_even("lat")
    copies = [[pltpu.make_async_copy(thick_hbm, thick_ref, thick_sem)]]
    start = 0
    for place, (row, size) in enumerate(bands):
        there = pl.ds(row, size)
        here = pl.ds(start, size)
        count_copy = pltpu.make_async_copy(
            count_hbm.at[there], count_ref.at[here], small_sems.at[0, place]
        )
        inertia_copy = pltpu.make_async_copy(
            inertia_hbm.at[there], inertia_ref.at[here], small_sems.at[1, place]
        )
        tend_copy = pltpu.make_async_copy(
            tend_hbm.at[:, :, there], tend_ref.at[:, :, here], large_sems.at[place]
        )
        copies.append([count_copy, inertia_copy, tend_copy])
        start += size
    for group in copies:
        for copy in group:
            copy.start()
    copies[0][0].wait()
    start = 0
    for place, (row, size) in enumerate(bands):
        part = slice(start, start + size)
        for copy in copies[place + 1]:
            copy.wait()
        count = count_ref[part]
        first = jnp.zeros(count.shape, jnp.float32)
        second = jnp.zeros(count.shape, jnp.float32)
        depth = jnp.zeros(count.shape, jnp.float32)
        for level in range(levels):
            layer = jnp.where(count > level, thick_ref[level], 0.0)
            depth = depth + layer
            first = first + layer * tend_ref[0, level, part].astype(jnp.float32)
            second = second + layer * tend_ref[1, level, part].astype(jnp.float32)
        for field, values in enumerate((first, second, depth, inertia_ref[part])):
            fields_ref[field, part] = values
        side_ref[part] = pack_edges(fields_ref, part)
        start += size
    if outer:
        for field in range(FIELDS):
            head = fields_ref[field, :ROWS]
            tail = fields_ref[field, start - ROWS :]
            near_ref[field] = jnp.where(even, tail, head)
            far_ref[field] = jnp.where(even, head, tail)


def integrate(tendency, thickness, level_count, inertia, bands, outer):
    components, levels, _, cols = tendency.shape
    rows = sum(size for _, size in bands)
    f32 = jnp.float32
    halo = jax.ShapeDtypeStruct((FIELDS, ROWS, cols), f32)
    return pl.pallas_call(
        functools.partial(integrate_kernel, bands, outer),
        in_specs=[pl.BlockSpec(memory_space=pltpu.HBM)] * 4,
        out_shape=[
            jax.ShapeDtypeStruct((FIELDS, rows, cols), f32),
            jax.ShapeDtypeStruct((rows, LANES), f32),
        ]
        + ([halo, halo] if outer else []),
        scratch_shapes=[
            pltpu.SMEM(thickness.shape, f32),
            pltpu.VMEM((rows, cols), jnp.int32),
            pltpu.VMEM((rows, cols), f32),
            pltpu.VMEM((components, levels, rows, cols), tendency.dtype),
            pltpu.SemaphoreType.DMA,
            pltpu.SemaphoreType.DMA((2, len(bands))),
            pltpu.SemaphoreType.DMA((len(bands),)),
        ],
        cost_estimate=pl.CostEstimate(
            flops=6 * components * levels * rows * cols,
            bytes_accessed=2 * components * levels * rows * cols,
            transcendentals=0,
        ),
        compiler_params=None if outer else pltpu.CompilerParams(vmem_limit_bytes=MIDDLE_BYTES),
        name="outer" if outer else "middle",
    )(thickness, level_count, inertia, tendency)


def edges_kernel(outer_ref, middle_ref, far_ref, near_ref, near_out_ref, far_out_ref):
    even_lat = is_even("lat")
    even_lon = is_even("lon")
    near = pack_edges(near_ref, slice(None))
    far = pack_edges(far_ref, slice(None))
    half = outer_ref.shape[0] // 2
    packed = jnp.concatenate(
        [
            jnp.where(even_lat, far, near),
            outer_ref[:half],
            middle_ref[...],
            outer_ref[half:],
            jnp.where(even_lat, near, far),
        ],
        axis=0,
    )
    size = near_out_ref.shape[0]
    lane = lanes_of(near_out_ref.shape)
    west = jnp.zeros(near_out_ref.shape, jnp.float32)
    east = jnp.zeros(near_out_ref.shape, jnp.float32)
    for group in range(GROUPS):
        rows = packed[group * size : (group + 1) * size]
        at = group * PITCH
        here = (lane >= at) & (lane < at + PITCH)
        west = jnp.where(here, turn(rows, at), west)
        east = jnp.where(here, turn(rows, at - HALF), east)
    near_out_ref[...] = jnp.where(even_lon, east, west)
    far_out_ref[...] = jnp.where(even_lon, west, east)


def edges(outer, middle, near, far):
    rows = outer.shape[0] + middle.shape[0] + 2 * ROWS
    message = jax.ShapeDtypeStruct((rows // GROUPS, LANES), jnp.float32)
    return pl.pallas_call(
        edges_kernel,
        out_shape=[message, message],
        compiler_params=pltpu.CompilerParams(vmem_limit_bytes=VMEM_BYTES),
        name="edges",
    )(outer, middle, far, near)


def smooth(field):
    rows, cols = field.shape
    tall = field + 0.5 * (pltpu.roll(field, 1, 0) + pltpu.roll(field, rows - 1, 0))
    return tall + 0.5 * (pltpu.roll(tall, 1, 1) + pltpu.roll(tall, cols - 1, 1))


def basis(first, second, depth, inertia):
    tall, wide = first.shape
    own = slice(ROWS, tall - ROWS)
    inside = inertia > 0.0
    east_west = pltpu.roll(first, wide - 1, 1) - pltpu.roll(first, 1, 1)
    north_south = pltpu.roll(second, tall - 1, 0) - pltpu.roll(second, 1, 0)
    scaled = jnp.where(depth > 0.0, 0.5 * (east_west + north_south), 0.0)
    diag = inertia + 2.0 * depth + smooth(depth)
    inverse = jnp.where(inside, 1.0 / jnp.where(inside, diag, 1.0), 0.0)
    mws = [scaled[own]]
    ws = []
    vector = scaled * inverse
    for step in range(STEPS):
        ws.append(vector[own])
        weighed = depth * vector
        scaled = depth * smooth(vector) + smooth(weighed) - 2.0 * weighed
        mws.append(scaled[own])
        if step + 1 < STEPS:
            vector = scaled * inverse
    return ws, mws


def moments(ws, mws, mask):
    ws = [jnp.where(mask, values, 0.0) for values in ws]
    images = [mws[place] - mws[place + 1] for place in range(STEPS)]
    pairs = [ws[place] * mws[0] for place in range(STEPS)]
    for low in range(STEPS):
        for high in range(low, STEPS):
            pairs.append(ws[low] * images[high])
    lines = []
    for product in pairs:
        line = jnp.sum(product, axis=0, keepdims=True)
        total = line[:, :LANES]
        for start in range(LANES, line.shape[1], LANES):
            total = total + line[:, start : start + LANES]
        total = total + turn(total, HALF)
        lines.append(total + turn(total, QUARTER))
    quarter = lanes_of((1, LANES)) // QUARTER
    packed = []
    for start in range(0, len(lines), 4):
        row = jnp.zeros((1, LANES), jnp.float32)
        for place, line in enumerate(lines[start : start + 4]):
            row = jnp.where(quarter == place, line, row)
        packed.append(row)
    packed.append(jnp.zeros((ROWS - len(packed), LANES), jnp.float32))
    return jnp.concatenate(packed, axis=0)


def interior_kernel(
    outer_ref,
    middle_ref,
    far_ref,
    near_ref,
    w_ref,
    mw_ref,
    strip_ref,
    sums_ref,
):
    half = outer_ref.shape[1] // 2
    cols = outer_ref.shape[2]
    even = is_even("lat")
    lane = lanes_of((strip_ref.shape[1], LANES))
    padded = []
    for place in range(FIELDS):
        near = near_ref[place]
        far = far_ref[place]
        values = jnp.concatenate(
            [
                jnp.where(even, far, near),
                outer_ref[place, :half],
                middle_ref[place],
                outer_ref[place, half:],
                jnp.where(even, near, far),
            ],
            axis=0,
        )
        east = turn(values[:, cols - LANES :], SEAM)
        strip_ref[place] = jnp.where(lane < HALF, values[:, :LANES], east)
        padded.append(values)
    ws, mws = basis(*padded)
    for place, values in enumerate(ws):
        w_ref[place] = values
    for place, values in enumerate(mws):
        mw_ref[place] = values
    lane = lanes_of(ws[0].shape)
    sums_ref[...] = moments(ws, mws, (lane >= RIM) & (lane < cols - RIM))


def interior(outer, middle, near, far):
    cols = outer.shape[2]
    rows = outer.shape[1] + middle.shape[1]
    f32 = jnp.float32
    return pl.pallas_call(
        interior_kernel,
        out_shape=[
            jax.ShapeDtypeStruct((STEPS, rows, cols), f32),
            jax.ShapeDtypeStruct((STEPS + 1, rows, cols), f32),
            jax.ShapeDtypeStruct((FIELDS, rows + 2 * ROWS, LANES), f32),
            jax.ShapeDtypeStruct((ROWS, LANES), f32),
        ],
        compiler_params=pltpu.CompilerParams(vmem_limit_bytes=VMEM_BYTES),
        cost_estimate=pl.CostEstimate(
            flops=300 * rows * cols, bytes_accessed=64 * rows * cols, transcendentals=0
        ),
        name="interior",
    )(outer, middle, far, near)


def strip_kernel(strip_in_ref, far_ref, near_ref, inner_ref, w_ref, mw_ref, sums_ref):
    even = is_even("lon")
    near = near_ref[...]
    far = far_ref[...]
    from_east = jnp.where(even, near, far)
    from_west = jnp.where(even, far, near)
    lane = lanes_of(near.shape)
    padded = []
    for place in range(FIELDS):
        halo = []
        for group in range(GROUPS):
            at = group * PITCH + place * RIM
            east = turn(from_east, SEAM - at)
            west = turn(from_west, LANES - RIM - at)
            west = jnp.where(lane >= LANES - RIM, west, 0.0)
            halo.append(jnp.where(lane < SEAM + RIM, east, west))
        halo = jnp.concatenate(halo, axis=0)
        padded.append(jnp.where(lanes_of(halo.shape) < SEAM, strip_in_ref[place], halo))
    ws, mws = basis(*padded)
    for place, values in enumerate(ws):
        w_ref[place] = values
    for place, values in enumerate(mws):
        mw_ref[place] = values
    lane = lanes_of(ws[0].shape)
    edge = (lane < RIM) | ((lane >= SEAM - RIM) & (lane < SEAM))
    sums_ref[...] = inner_ref[...] + moments(ws, mws, edge)


def strip(strip_in, near, far, inner):
    rows = strip_in.shape[1] - 2 * ROWS
    f32 = jnp.float32
    return pl.pallas_call(
        strip_kernel,
        out_shape=[
            jax.ShapeDtypeStruct((STEPS, rows, LANES), f32),
            jax.ShapeDtypeStruct((STEPS + 1, rows, LANES), f32),
            jax.ShapeDtypeStruct((ROWS, LANES), f32),
        ],
        compiler_params=pltpu.CompilerParams(vmem_limit_bytes=VMEM_BYTES),
        name="strip",
    )(strip_in, far, near, inner)


def power(exponent):
    size = jnp.abs(exponent)
    value = jnp.ones(exponent.shape, jnp.float32)
    for bit in range(7):
        up, down = 2.0 ** (1 << bit), 2.0 ** -(1 << bit)
        factor = jnp.where(exponent < 0, down, up)
        value = value * jnp.where((size >> bit) & 1 == 1, factor, 1.0)
    return value


def exponent_of(size):
    bits = jnp.ceil(jnp.log2(jnp.maximum(size, 2.0**-100)))
    return jnp.clip(bits, -100.0, 100.0).astype(jnp.int32)


def nearest(values):
    return jnp.floor(values + 0.5)


def place_kernel(owner_ref, outer_ref, middle_ref, sent_ref, scale_ref):
    count = owner_ref.shape[0]
    edge = outer_ref.shape[1] // 2
    between = middle_ref.shape[1]
    span = (2 * edge + between) // count
    sent_ref[...] = jnp.zeros(sent_ref.shape, jnp.int16)
    scale_ref[...] = jnp.zeros(scale_ref.shape, jnp.float32)
    for block in range(count):
        row = block * span
        if row < edge:
            ref, row = outer_ref, row
        elif row < edge + between:
            ref, row = middle_ref, row - edge
        else:
            ref, row = outer_ref, row - between
        target = owner_ref[block]

        @pl.when(target >= 0)
        def _(ref=ref, row=row, target=target):
            for half in range(ref.shape[2] // LANES):
                cols = slice(half * LANES, (half + 1) * LANES)
                rows = slice(row, row + span)
                values = jnp.concatenate([ref[0, rows, cols], ref[1, rows, cols]], axis=0)
                bits = exponent_of(jnp.max(jnp.abs(values), axis=0, keepdims=True))
                whole = jnp.clip(nearest(values * power(15 - bits)), -32767.0, 32767.0)
                there = slice(2 * span * half, 2 * span * (half + 1))
                sent_ref[target, there] = whole.astype(jnp.int32).astype(jnp.int16)
                scale_ref[target, half : half + 1] = bits.astype(jnp.float32)


def place(owner, outer, middle, lon_count):
    cols = outer.shape[2]
    rows = outer.shape[1] + middle.shape[1]
    span = rows // owner.shape[0]
    return pl.pallas_call(
        place_kernel,
        in_specs=[pl.BlockSpec(memory_space=pltpu.SMEM)]
        + [pl.BlockSpec(memory_space=pltpu.VMEM)] * 2,
        out_shape=[
            jax.ShapeDtypeStruct((lon_count, cols // LANES * 2 * span + TAIL, LANES), jnp.int16),
            jax.ShapeDtypeStruct((lon_count, ROWS, LANES), jnp.float32),
        ],
        compiler_params=pltpu.CompilerParams(vmem_limit_bytes=VMEM_BYTES),
        cost_estimate=pl.CostEstimate(
            flops=60 * rows * cols, bytes_accessed=12 * rows * cols, transcendentals=0
        ),
        name="place",
    )(owner, outer, middle)


def seal_kernel(sums_ref, other_ref, scale_ref, tail_ref):
    sums = sums_ref[:SUM_ROWS] + other_ref[:SUM_ROWS]
    bits = exponent_of(jnp.abs(sums))
    scaled = sums * power(-bits) * 2.0**14
    high = nearest(scaled)
    low = nearest((scaled - high) * 2.0**15)
    parts = jnp.concatenate([bits.astype(jnp.float32), high, low], axis=0)
    for slot in range(tail_ref.shape[0]):
        tile = jnp.concatenate([parts, scale_ref[slot, : TAIL - 3 * SUM_ROWS]], axis=0)
        tail_ref[slot] = tile.astype(jnp.int32).astype(jnp.int16)


def seal(sums, other, scale):
    return pl.pallas_call(
        seal_kernel,
        out_shape=jax.ShapeDtypeStruct((scale.shape[0], TAIL, LANES), jnp.int16),
        compiler_params=pltpu.CompilerParams(vmem_limit_bytes=VMEM_BYTES),
        name="seal",
    )(sums, other, scale)


def unpack_kernel(arrived_ref, held_ref, sums_ref):
    rows = held_ref.shape[1]
    packed = jnp.zeros((SUM_ROWS, LANES), jnp.float32)
    for slot in range(held_ref.shape[0]):
        tail = arrived_ref[slot, arrived_ref.shape[1] - TAIL :].astype(jnp.int32)
        digits = tail.astype(jnp.float32)
        high = digits[SUM_ROWS : 2 * SUM_ROWS]
        low = digits[2 * SUM_ROWS : 3 * SUM_ROWS]
        packed = packed + (high + low * 2.0**-15) * power(tail[:SUM_ROWS] - 14)
        for half in range(held_ref.shape[2] // LANES):
            at = 3 * SUM_ROWS + half
            scale = power(tail[at : at + 1] - 15)
            whole = arrived_ref[slot, half * rows : (half + 1) * rows].astype(jnp.int32)
            held_ref[slot, :, half * LANES : (half + 1) * LANES] = whole.astype(jnp.float32) * scale
    sums_ref[:SUM_ROWS] = packed
    sums_ref[SUM_ROWS:] = jnp.zeros((ROWS - SUM_ROWS, LANES), jnp.float32)


def unpack(arrived, cols):
    held = (arrived.shape[0], (arrived.shape[1] - TAIL) * LANES // cols, cols)
    return pl.pallas_call(
        unpack_kernel,
        out_shape=[
            jax.ShapeDtypeStruct(held, jnp.float32),
            jax.ShapeDtypeStruct((ROWS, LANES), jnp.float32),
        ],
        compiler_params=pltpu.CompilerParams(vmem_limit_bytes=VMEM_BYTES),
        name="unpack",
    )(arrived)


def combine_kernel(
    sums_ref, other_ref, w_ref, mw_ref, w_edge_ref, mw_edge_ref, pressure_ref, residual_ref
):
    packed = jnp.where(is_even("lat"), other_ref[:SUM_ROWS], sums_ref[:SUM_ROWS])
    quarter = lanes_of(packed.shape) // QUARTER
    totals = [
        jnp.sum(jnp.where(quarter == place, packed, 0.0), axis=1, keepdims=True)
        for place in range(4)
    ]
    entry = lambda place: totals[place % 4][place // 4 : place // 4 + 1, :]
    right = [entry(place) for place in range(STEPS)]
    matrix = {}
    place = STEPS
    for low in range(STEPS):
        for high in range(low, STEPS):
            matrix[low, high] = entry(place)
            place += 1
    for pivot in range(STEPS):
        inverse = 1.0 / matrix[pivot, pivot]
        for row in range(pivot + 1, STEPS):
            factor = matrix[pivot, row] * inverse
            for col in range(row, STEPS):
                matrix[row, col] = matrix[row, col] - factor * matrix[pivot, col]
            right[row] = right[row] - factor * right[pivot]
        matrix[pivot, pivot] = inverse
    for pivot in reversed(range(STEPS)):
        for col in range(pivot + 1, STEPS):
            right[pivot] = right[pivot] - matrix[pivot, col] * right[col]
        right[pivot] = right[pivot] * matrix[pivot, pivot]

    def results(w_ref, mw_ref):
        pressure = right[0] * w_ref[0]
        residual = mw_ref[0] - right[0] * (mw_ref[0] - mw_ref[1])
        for place in range(1, STEPS):
            pressure = pressure + right[place] * w_ref[place]
            residual = residual - right[place] * (mw_ref[place] - mw_ref[place + 1])
        return pressure, residual

    inner = results(w_ref, mw_ref)
    edge = results(w_edge_ref, mw_edge_ref)
    cols = pressure_ref.shape[1]
    lane = lanes_of(edge[0].shape)
    for out_ref, inside, border in zip((pressure_ref, residual_ref), inner, edge):
        out_ref[:, :LANES] = jnp.where(lane < RIM, border, inside[:, :LANES])
        if cols > 2 * LANES:
            out_ref[:, LANES : cols - LANES] = inside[:, LANES : cols - LANES]
        out_ref[:, cols - LANES :] = jnp.where(
            lane >= LANES - RIM, turn(border, -SEAM), inside[:, cols - LANES :]
        )


def combine(sums, other, w, mw, w_edge, mw_edge):
    shape = jax.ShapeDtypeStruct(w.shape[1:], jnp.float32)
    return pl.pallas_call(
        combine_kernel,
        out_shape=[shape, shape],
        compiler_params=pltpu.CompilerParams(vmem_limit_bytes=VMEM_BYTES),
        name="combine",
    )(sums, other, w, mw, w_edge, mw_edge)


def exchange_odd(values, axis, distance):
    pairs = [(place, place ^ distance) for place in range(1, lax.axis_size(axis), 2)]
    return lax.ppermute(values, axis, pairs)


def swap(values, axis, first, ring):
    count = lax.axis_size(axis)
    pairs = []
    for place in range(first, count if ring else count - 1, 2):
        beside = (place + 1) % count
        pairs += [(place, beside), (beside, place)]
    return lax.ppermute(values, axis, pairs)


def on_device(tendency, thickness, level_count, block_mask, owner, inertia):
    lat_count = lax.axis_size("lat")
    lon_count = lax.axis_size("lon")
    rows = level_count.shape[0]
    tall = OUTER
    inputs = (tendency, thickness, level_count, inertia)
    outer, outer_side, near, far = integrate(*inputs, ((0, tall), (rows - tall, tall)), True)
    bands = tuple(
        (row, min(CHUNK, rows - tall - row)) for row in range(tall, rows - tall, CHUNK)
    )
    middle, middle_side = integrate(*inputs, bands, False)
    far = swap(far, "lat", 1, False)
    near = swap(near, "lat", 0, False)
    near_edge, far_edge = edges(outer_side, middle_side, near, far)
    far_edge = swap(far_edge, "lon", 1, True)
    near_edge = swap(near_edge, "lon", 0, True)
    w, mw, strip_in, inner = interior(outer, middle, near, far)
    w_edge, mw_edge, sums = strip(strip_in, near_edge, far_edge, inner)
    sent, scale = place(owner[:, 0], outer, middle, lon_count)
    sums = sums + lax.ppermute(sums, "lat", [(p, p + 1) for p in range(0, lat_count, 2)])
    shift = 2
    while 2 * shift < lat_count:
        sums = sums + exchange_odd(sums, "lat", shift)
        shift *= 2
    tail = seal(sums, exchange_odd(sums, "lat", shift), scale)
    sent = lax.dynamic_update_slice(sent, tail, (0, sent.shape[1] - TAIL, 0))
    arrived = lax.all_to_all(sent, "lon", split_axis=0, concat_axis=0, tiled=True)
    held, sums = unpack(arrived, level_count.shape[1])
    other = lax.ppermute(sums, "lat", [(p + 1, p) for p in range(0, lat_count, 2)])
    pressure, residual = combine(sums, other, w, mw, w_edge, mw_edge)
    held = held.reshape((1, 1, lon_count, 2, held.shape[1] // 2, held.shape[2]))
    return (held, pressure, residual)


def solution(mesh):
    return jax.shard_map(
        on_device,
        mesh=mesh,
        in_specs=(
            P(None, None, "lat", "lon"),
            P(),
            P("lat", "lon"),
            P("lat", "lon"),
            P("lat", "lon"),
            P("lat", "lon"),
        ),
        out_specs=(P("lat", "lon", None, None, None, None), P("lat", "lon"), P("lat", "lon")),
        check_vma=False,
    )
```

```python
import functools

import jax
import jax.numpy as jnp
from jax import lax
from jax.experimental import pallas as pl
from jax.experimental.pallas import tpu as pltpu
from jax.sharding import PartitionSpec as P

STEPS = 4
RIM = STEPS + 1
ROWS = 8
LANES = 128
HALF = LANES // 2
QUARTER = LANES // 4
EAST = 48
SEAM = HALF + EAST
CHUNK = 32
FIELDS = 4
GROUPS = 6
PITCH = LANES // GROUPS
OUTER = 16
TAIL = 16
SUM_ROWS = 4
VMEM_BYTES = 16 * 1024 * 1024
WHOLE_BYTES = 56450000


def lanes_of(shape):
    return lax.broadcasted_iota(jnp.int32, shape, len(shape) - 1)


def turn(values, amount):
    amount = amount % values.shape[1]
    return pltpu.roll(values, amount, 1) if amount else values


def is_even(axis):
    return lax.rem(lax.axis_index(axis), 2) == 0


def pack_edges(ref, part):
    cols = ref.shape[2]
    packed = None
    for place in range(FIELDS):
        west = ref[place, part, :LANES]
        east = ref[place, part, cols - LANES :]
        if packed is None:
            lane = lanes_of(west.shape)
            packed = jnp.zeros(west.shape, jnp.float32)
        at = place * RIM
        packed = jnp.where((lane >= at) & (lane < at + RIM), turn(west, at), packed)
        at = HALF + place * RIM
        packed = jnp.where((lane >= at) & (lane < at + RIM), turn(east, at + RIM), packed)
    return packed


def integrate_kernel(bands, outer, thick_hbm, count_hbm, inertia_hbm, tend_hbm, *refs):
    outs, scratch = refs[:2], refs[2:]
    thick_ref, count_ref, inertia_ref, tend_ref, thick_sem, small_sems, large_sems = scratch
    levels = tend_hbm.shape[1]
    thick_copy = pltpu.make_async_copy(thick_hbm, thick_ref, thick_sem)
    copies = []
    start = 0
    for place, (row, size) in enumerate(bands):
        there = pl.ds(row, size)
        here = pl.ds(start, size)
        count_copy = pltpu.make_async_copy(
            count_hbm.at[there], count_ref.at[here], small_sems.at[0, place]
        )
        inertia_copy = pltpu.make_async_copy(
            inertia_hbm.at[there], inertia_ref.at[here], small_sems.at[1, place]
        )
        tend_copy = pltpu.make_async_copy(
            tend_hbm.at[:, :, there], tend_ref.at[:, :, here], large_sems.at[place]
        )
        copies.append((count_copy, inertia_copy, tend_copy))
        start += size
    thick_copy.start()
    for group in copies:
        for copy in group:
            copy.start()
    thick_copy.wait()
    start = 0
    results = []
    for place, (row, size) in enumerate(bands):
        part = slice(start, start + size)
        for copy in copies[place]:
            copy.wait()
        count = count_ref[part]
        first = jnp.zeros(count.shape, jnp.float32)
        second = jnp.zeros(count.shape, jnp.float32)
        depth = jnp.zeros(count.shape, jnp.float32)
        for level in range(levels):
            layer = jnp.where(count > level, thick_ref[level], 0.0)
            depth = depth + layer
            first = first + layer * tend_ref[0, level, part].astype(jnp.float32)
            second = second + layer * tend_ref[1, level, part].astype(jnp.float32)
        values = (first, second, depth, inertia_ref[part])
        if outer:
            results.append(values)
        else:
            fields_ref, side_ref = outs
            for field in range(FIELDS):
                fields_ref[field, part] = values[field]
            side_ref[part] = pack_edges(fields_ref, part)
        start += size
    if outer:
        near_ref, far_ref = outs
        even = is_even("lat")
        for field in range(FIELDS):
            head = results[0][field][:ROWS]
            tail = results[1][field][-ROWS:]
            near_ref[field] = jnp.where(even, tail, head)
            far_ref[field] = jnp.where(even, head, tail)


def integrate(tendency, thickness, level_count, inertia, bands, outer):
    components, levels, _, cols = tendency.shape
    rows = sum(size for _, size in bands)
    f32 = jnp.float32
    if outer:
        out_shape = [jax.ShapeDtypeStruct((FIELDS, ROWS, cols), f32)] * 2
    else:
        out_shape = [
            jax.ShapeDtypeStruct((FIELDS, rows, cols), f32),
            jax.ShapeDtypeStruct((rows, LANES), f32),
        ]
    return pl.pallas_call(
        functools.partial(integrate_kernel, bands, outer),
        in_specs=[pl.BlockSpec(memory_space=pltpu.HBM)] * 4,
        out_shape=out_shape,
        scratch_shapes=[
            pltpu.SMEM(thickness.shape, f32),
            pltpu.VMEM((rows, cols), jnp.int32),
            pltpu.VMEM((rows, cols), f32),
            pltpu.VMEM((components, levels, rows, cols), tendency.dtype),
            pltpu.SemaphoreType.DMA,
            pltpu.SemaphoreType.DMA((2, len(bands))),
            pltpu.SemaphoreType.DMA((len(bands),)),
        ],
        cost_estimate=pl.CostEstimate(
            flops=6 * components * levels * rows * cols,
            bytes_accessed=2 * components * levels * rows * cols,
            transcendentals=0,
        ),
        compiler_params=None if outer else pltpu.CompilerParams(vmem_limit_bytes=WHOLE_BYTES),
        name="outer" if outer else "whole",
    )(thickness, level_count, inertia, tendency)


def edges_kernel(side_ref, far_ref, near_ref, near_out_ref, far_out_ref):
    even_lat = is_even("lat")
    even_lon = is_even("lon")
    near = pack_edges(near_ref, slice(None))
    far = pack_edges(far_ref, slice(None))
    north = jnp.where(even_lat, far, near)
    south = jnp.where(even_lat, near, far)
    packed = jnp.concatenate([north, side_ref[...], south], axis=0)
    size = near_out_ref.shape[0]
    lane = lanes_of(near_out_ref.shape)
    west = jnp.zeros(near_out_ref.shape, jnp.float32)
    east = jnp.zeros(near_out_ref.shape, jnp.float32)
    for group in range(GROUPS):
        rows = packed[group * size : (group + 1) * size]
        at = group * PITCH
        here = (lane >= at) & (lane < at + PITCH)
        west = jnp.where(here, turn(rows, at), west)
        east = jnp.where(here, turn(rows, at - HALF), east)
    near_out_ref[...] = jnp.where(even_lon, east, west)
    far_out_ref[...] = jnp.where(even_lon, west, east)


def edges(side, near, far):
    rows = side.shape[0] + 2 * ROWS
    message = jax.ShapeDtypeStruct((rows // GROUPS, LANES), jnp.float32)
    return pl.pallas_call(
        edges_kernel,
        out_shape=[message, message],
        compiler_params=pltpu.CompilerParams(vmem_limit_bytes=VMEM_BYTES),
        name="edges",
    )(side, far, near)


def smooth(field):
    rows, cols = field.shape
    tall = field + 0.5 * (pltpu.roll(field, 1, 0) + pltpu.roll(field, rows - 1, 0))
    return tall + 0.5 * (pltpu.roll(tall, 1, 1) + pltpu.roll(tall, cols - 1, 1))


def basis(first, second, depth, inertia):
    tall, wide = first.shape
    own = slice(ROWS, tall - ROWS)
    inside = inertia > 0.0
    east_west = pltpu.roll(first, wide - 1, 1) - pltpu.roll(first, 1, 1)
    north_south = pltpu.roll(second, tall - 1, 0) - pltpu.roll(second, 1, 0)
    scaled = jnp.where(depth > 0.0, 0.5 * (east_west + north_south), 0.0)
    diag = inertia + 2.0 * depth + smooth(depth)
    inverse = jnp.where(inside, 1.0 / jnp.where(inside, diag, 1.0), 0.0)
    mws = [scaled[own]]
    ws = []
    vector = scaled * inverse
    for step in range(STEPS):
        ws.append(vector[own])
        weighed = depth * vector
        scaled = depth * smooth(vector) + smooth(weighed) - 2.0 * weighed
        mws.append(scaled[own])
        if step + 1 < STEPS:
            vector = scaled * inverse
    return ws, mws


def moments(ws, mws, mask):
    ws = [jnp.where(mask, values, 0.0) for values in ws]
    images = [mws[place] - mws[place + 1] for place in range(STEPS)]
    pairs = [ws[place] * mws[0] for place in range(STEPS)]
    for low in range(STEPS):
        for high in range(low, STEPS):
            pairs.append(ws[low] * images[high])
    lines = []
    for product in pairs:
        line = jnp.sum(product, axis=0, keepdims=True)
        total = line[:, :LANES]
        for start in range(LANES, line.shape[1], LANES):
            total = total + line[:, start : start + LANES]
        total = total + turn(total, HALF)
        lines.append(total + turn(total, QUARTER))
    quarter = lanes_of((1, LANES)) // QUARTER
    packed = []
    for start in range(0, len(lines), 4):
        row = jnp.zeros((1, LANES), jnp.float32)
        for place, line in enumerate(lines[start : start + 4]):
            row = jnp.where(quarter == place, line, row)
        packed.append(row)
    packed.append(jnp.zeros((ROWS - len(packed), LANES), jnp.float32))
    return jnp.concatenate(packed, axis=0)


def interior_kernel(
    fields_ref,
    far_ref,
    near_ref,
    w_ref,
    mw_ref,
    strip_ref,
    sums_ref,
):
    cols = fields_ref.shape[2]
    even = is_even("lat")
    lane = lanes_of((strip_ref.shape[1], LANES))
    padded = []
    for place in range(FIELDS):
        near = near_ref[place]
        far = far_ref[place]
        north = jnp.where(even, far, near)
        south = jnp.where(even, near, far)
        values = jnp.concatenate([north, fields_ref[place], south], axis=0)
        east = turn(values[:, cols - LANES :], SEAM)
        strip_ref[place] = jnp.where(lane < HALF, values[:, :LANES], east)
        padded.append(values)
    ws, mws = basis(*padded)
    for place, values in enumerate(ws):
        w_ref[place] = values
    for place, values in enumerate(mws):
        mw_ref[place] = values
    lane = lanes_of(ws[0].shape)
    sums_ref[...] = moments(ws, mws, (lane >= RIM) & (lane < cols - RIM))


def interior(fields, near, far):
    _, rows, cols = fields.shape
    f32 = jnp.float32
    return pl.pallas_call(
        interior_kernel,
        out_shape=[
            jax.ShapeDtypeStruct((STEPS, rows, cols), f32),
            jax.ShapeDtypeStruct((STEPS + 1, rows, cols), f32),
            jax.ShapeDtypeStruct((FIELDS, rows + 2 * ROWS, LANES), f32),
            jax.ShapeDtypeStruct((ROWS, LANES), f32),
        ],
        compiler_params=pltpu.CompilerParams(vmem_limit_bytes=VMEM_BYTES),
        cost_estimate=pl.CostEstimate(
            flops=300 * rows * cols, bytes_accessed=64 * rows * cols, transcendentals=0
        ),
        name="interior",
    )(fields, far, near)


def strip_kernel(strip_in_ref, far_ref, near_ref, inner_ref, w_ref, mw_ref, sums_ref):
    even = is_even("lon")
    near = near_ref[...]
    far = far_ref[...]
    from_east = jnp.where(even, near, far)
    from_west = jnp.where(even, far, near)
    lane = lanes_of(near.shape)
    padded = []
    for place in range(FIELDS):
        halo = []
        for group in range(GROUPS):
            at = group * PITCH + place * RIM
            east = turn(from_east, SEAM - at)
            west = turn(from_west, LANES - RIM - at)
            west = jnp.where(lane >= LANES - RIM, west, 0.0)
            halo.append(jnp.where(lane < SEAM + RIM, east, west))
        halo = jnp.concatenate(halo, axis=0)
        padded.append(jnp.where(lanes_of(halo.shape) < SEAM, strip_in_ref[place], halo))
    ws, mws = basis(*padded)
    for place, values in enumerate(ws):
        w_ref[place] = values
    for place, values in enumerate(mws):
        mw_ref[place] = values
    lane = lanes_of(ws[0].shape)
    edge = (lane < RIM) | ((lane >= SEAM - RIM) & (lane < SEAM))
    sums_ref[...] = inner_ref[...] + moments(ws, mws, edge)


def strip(strip_in, near, far, inner):
    rows = strip_in.shape[1] - 2 * ROWS
    f32 = jnp.float32
    return pl.pallas_call(
        strip_kernel,
        out_shape=[
            jax.ShapeDtypeStruct((STEPS, rows, LANES), f32),
            jax.ShapeDtypeStruct((STEPS + 1, rows, LANES), f32),
            jax.ShapeDtypeStruct((ROWS, LANES), f32),
        ],
        compiler_params=pltpu.CompilerParams(vmem_limit_bytes=VMEM_BYTES),
        name="strip",
    )(strip_in, far, near, inner)


def power(exponent):
    size = jnp.abs(exponent)
    value = jnp.ones(exponent.shape, jnp.float32)
    for bit in range(7):
        up, down = 2.0 ** (1 << bit), 2.0 ** -(1 << bit)
        factor = jnp.where(exponent < 0, down, up)
        value = value * jnp.where((size >> bit) & 1 == 1, factor, 1.0)
    return value


def exponent_of(size):
    bits = jnp.ceil(jnp.log2(jnp.maximum(size, 2.0**-100)))
    return jnp.clip(bits, -100.0, 100.0).astype(jnp.int32)


def nearest(values):
    return jnp.floor(values + 0.5)


def place_kernel(owner_ref, fields_ref, sent_ref, scale_ref):
    count = owner_ref.shape[0]
    span = fields_ref.shape[1] // count
    sent_ref[...] = jnp.zeros(sent_ref.shape, jnp.int16)
    scale_ref[...] = jnp.zeros(scale_ref.shape, jnp.float32)
    for block in range(count):
        target = owner_ref[block]

        @pl.when(target >= 0)
        def _(block=block, target=target):
            rows = slice(block * span, (block + 1) * span)
            for half in range(fields_ref.shape[2] // LANES):
                cols = slice(half * LANES, (half + 1) * LANES)
                pieces = [fields_ref[0, rows, cols], fields_ref[1, rows, cols]]
                values = jnp.concatenate(pieces, axis=0)
                bits = exponent_of(jnp.max(jnp.abs(values), axis=0, keepdims=True))
                whole = jnp.clip(nearest(values * power(15 - bits)), -32767.0, 32767.0)
                there = slice(2 * span * half, 2 * span * (half + 1))
                sent_ref[target, there] = whole.astype(jnp.int32).astype(jnp.int16)
                scale_ref[target, half : half + 1] = bits.astype(jnp.float32)


def place(owner, fields, lon_count):
    _, rows, cols = fields.shape
    span = rows // owner.shape[0]
    return pl.pallas_call(
        place_kernel,
        in_specs=[
            pl.BlockSpec(memory_space=pltpu.SMEM),
            pl.BlockSpec(memory_space=pltpu.VMEM),
        ],
        out_shape=[
            jax.ShapeDtypeStruct((lon_count, cols // LANES * 2 * span + TAIL, LANES), jnp.int16),
            jax.ShapeDtypeStruct((lon_count, ROWS, LANES), jnp.float32),
        ],
        compiler_params=pltpu.CompilerParams(vmem_limit_bytes=VMEM_BYTES),
        cost_estimate=pl.CostEstimate(
            flops=60 * rows * cols, bytes_accessed=12 * rows * cols, transcendentals=0
        ),
        name="place",
    )(owner, fields)


def seal_kernel(sums_ref, other_ref, scale_ref, tail_ref):
    sums = sums_ref[:SUM_ROWS] + other_ref[:SUM_ROWS]
    bits = exponent_of(jnp.abs(sums))
    scaled = sums * power(-bits) * 2.0**14
    high = nearest(scaled)
    low = nearest((scaled - high) * 2.0**15)
    parts = jnp.concatenate([bits.astype(jnp.float32), high, low], axis=0)
    for slot in range(tail_ref.shape[0]):
        tile = jnp.concatenate([parts, scale_ref[slot, : TAIL - 3 * SUM_ROWS]], axis=0)
        tail_ref[slot] = tile.astype(jnp.int32).astype(jnp.int16)


def seal(sums, other, scale):
    return pl.pallas_call(
        seal_kernel,
        out_shape=jax.ShapeDtypeStruct((scale.shape[0], TAIL, LANES), jnp.int16),
        compiler_params=pltpu.CompilerParams(vmem_limit_bytes=VMEM_BYTES),
        name="seal",
    )(sums, other, scale)


def combine_kernel(
    arrived_ref, w_ref, mw_ref, w_edge_ref, mw_edge_ref, pressure_ref, residual_ref, held_ref
):
    rows = held_ref.shape[1]
    packed = jnp.zeros((SUM_ROWS, LANES), jnp.float32)
    for slot in range(held_ref.shape[0]):
        tail = arrived_ref[slot, arrived_ref.shape[1] - TAIL :].astype(jnp.int32)
        digits = tail.astype(jnp.float32)
        high = digits[SUM_ROWS : 2 * SUM_ROWS]
        low = digits[2 * SUM_ROWS : 3 * SUM_ROWS]
        packed = packed + (high + low * 2.0**-15) * power(tail[:SUM_ROWS] - 14)
        for half in range(held_ref.shape[2] // LANES):
            at = 3 * SUM_ROWS + half
            scale = power(tail[at : at + 1] - 15)
            whole = arrived_ref[slot, half * rows : (half + 1) * rows].astype(jnp.int32)
            held_ref[slot, :, half * LANES : (half + 1) * LANES] = whole.astype(jnp.float32) * scale
    quarter = lanes_of(packed.shape) // QUARTER
    totals = [
        jnp.sum(jnp.where(quarter == place, packed, 0.0), axis=1, keepdims=True)
        for place in range(4)
    ]
    entry = lambda place: totals[place % 4][place // 4 : place // 4 + 1, :]
    right = [entry(place) for place in range(STEPS)]
    matrix = {}
    place = STEPS
    for low in range(STEPS):
        for high in range(low, STEPS):
            matrix[low, high] = entry(place)
            place += 1
    for pivot in range(STEPS):
        inverse = 1.0 / matrix[pivot, pivot]
        for row in range(pivot + 1, STEPS):
            factor = matrix[pivot, row] * inverse
            for col in range(row, STEPS):
                matrix[row, col] = matrix[row, col] - factor * matrix[pivot, col]
            right[row] = right[row] - factor * right[pivot]
        matrix[pivot, pivot] = inverse
    for pivot in reversed(range(STEPS)):
        for col in range(pivot + 1, STEPS):
            right[pivot] = right[pivot] - matrix[pivot, col] * right[col]
        right[pivot] = right[pivot] * matrix[pivot, pivot]

    def results(w_ref, mw_ref):
        pressure = right[0] * w_ref[0]
        residual = mw_ref[0] - right[0] * (mw_ref[0] - mw_ref[1])
        for place in range(1, STEPS):
            pressure = pressure + right[place] * w_ref[place]
            residual = residual - right[place] * (mw_ref[place] - mw_ref[place + 1])
        return pressure, residual

    inner = results(w_ref, mw_ref)
    edge = results(w_edge_ref, mw_edge_ref)
    cols = pressure_ref.shape[1]
    lane = lanes_of(edge[0].shape)
    for out_ref, inside, border in zip((pressure_ref, residual_ref), inner, edge):
        out_ref[:, :LANES] = jnp.where(lane < RIM, border, inside[:, :LANES])
        if cols > 2 * LANES:
            out_ref[:, LANES : cols - LANES] = inside[:, LANES : cols - LANES]
        out_ref[:, cols - LANES :] = jnp.where(
            lane >= LANES - RIM, turn(border, -SEAM), inside[:, cols - LANES :]
        )


def combine(arrived, w, mw, w_edge, mw_edge):
    rows, cols = w.shape[1:]
    shape = jax.ShapeDtypeStruct((rows, cols), jnp.float32)
    held = (arrived.shape[0], (arrived.shape[1] - TAIL) * LANES // cols, cols)
    return pl.pallas_call(
        combine_kernel,
        out_shape=[shape, shape, jax.ShapeDtypeStruct(held, jnp.float32)],
        compiler_params=pltpu.CompilerParams(vmem_limit_bytes=VMEM_BYTES),
        name="combine",
    )(arrived, w, mw, w_edge, mw_edge)


def exchange(values, axis, distance):
    pairs = [(place, place ^ distance) for place in range(lax.axis_size(axis))]
    return lax.ppermute(values, axis, pairs)


def swap(values, axis, first, ring):
    count = lax.axis_size(axis)
    pairs = []
    for place in range(first, count if ring else count - 1, 2):
        beside = (place + 1) % count
        pairs += [(place, beside), (beside, place)]
    return lax.ppermute(values, axis, pairs)


def on_device(tendency, thickness, level_count, block_mask, owner, inertia):
    lat_count = lax.axis_size("lat")
    lon_count = lax.axis_size("lon")
    rows = level_count.shape[0]
    inputs = (tendency, thickness, level_count, inertia)
    near, far = integrate(*inputs, ((0, OUTER), (rows - OUTER, OUTER)), True)
    bands = tuple((row, CHUNK) for row in range(0, rows, CHUNK))
    fields, side = integrate(*inputs, bands, False)
    far = swap(far, "lat", 1, False)
    near = swap(near, "lat", 0, False)
    near_edge, far_edge = edges(side, near, far)
    far_edge = swap(far_edge, "lon", 1, True)
    near_edge = swap(near_edge, "lon", 0, True)
    w, mw, strip_in, inner = interior(fields, near, far)
    w_edge, mw_edge, sums = strip(strip_in, near_edge, far_edge, inner)
    sent, scale = place(owner[:, 0], fields, lon_count)
    shift = 1
    while 2 * shift < lat_count:
        sums = sums + exchange(sums, "lat", shift)
        shift *= 2
    tail = seal(sums, exchange(sums, "lat", shift), scale)
    sent = lax.dynamic_update_slice(sent, tail, (0, sent.shape[1] - TAIL, 0))
    arrived = lax.all_to_all(sent, "lon", split_axis=0, concat_axis=0, tiled=True)
    pressure, residual, held = combine(arrived, w, mw, w_edge, mw_edge)
    held = held.reshape((1, 1, lon_count, 2, held.shape[1] // 2, held.shape[2]))
    return (held, pressure, residual)


def solution(mesh):
    return jax.shard_map(
        on_device,
        mesh=mesh,
        in_specs=(
            P(None, None, "lat", "lon"),
            P(),
            P("lat", "lon"),
            P("lat", "lon"),
            P("lat", "lon"),
            P("lat", "lon"),
        ),
        out_specs=(P("lat", "lon", None, None, None, None), P("lat", "lon"), P("lat", "lon")),
        check_vma=False,
    )
```

```python
import functools

import jax
import jax.numpy as jnp
from jax import lax
from jax.experimental import pallas as pl
from jax.experimental.pallas import tpu as pltpu
from jax.sharding import PartitionSpec as P

STEPS = 4
RIM = STEPS + 1
ROWS = 8
LANES = 128
HALF = LANES // 2
QUARTER = LANES // 4
EAST = 48
SEAM = HALF + EAST
CHUNK = 32
FIELDS = 4
GROUPS = 6
PITCH = LANES // GROUPS
PIECES = 2
OUTER = 16
TAIL = 16
SUM_ROWS = 4
VMEM_BYTES = 16 * 1024 * 1024
WHOLE_BYTES = 56450000


def lanes_of(shape):
    return lax.broadcasted_iota(jnp.int32, shape, len(shape) - 1)


def turn(values, amount):
    amount = amount % values.shape[1]
    return pltpu.roll(values, amount, 1) if amount else values


def is_even(axis):
    return lax.rem(lax.axis_index(axis), 2) == 0


def pack_edges(ref, part):
    cols = ref.shape[2]
    packed = None
    for place in range(FIELDS):
        west = ref[place, part, :LANES]
        east = ref[place, part, cols - LANES :]
        if packed is None:
            lane = lanes_of(west.shape)
            packed = jnp.zeros(west.shape, jnp.float32)
        at = place * RIM
        packed = jnp.where((lane >= at) & (lane < at + RIM), turn(west, at), packed)
        at = HALF + place * RIM
        packed = jnp.where((lane >= at) & (lane < at + RIM), turn(east, at + RIM), packed)
    return packed


def integrate_kernel(bands, outer, thick_hbm, count_hbm, inertia_hbm, tend_hbm, *refs):
    outs, scratch = refs[:2], refs[2:]
    thick_ref, count_ref, inertia_ref, tend_ref, thick_sem, small_sems, large_sems = scratch
    levels = tend_hbm.shape[1]
    thick_copy = pltpu.make_async_copy(thick_hbm, thick_ref, thick_sem)
    copies = []
    start = 0
    for place, (row, size) in enumerate(bands):
        there = pl.ds(row, size)
        here = pl.ds(start, size)
        count_copy = pltpu.make_async_copy(
            count_hbm.at[there], count_ref.at[here], small_sems.at[0, place]
        )
        inertia_copy = pltpu.make_async_copy(
            inertia_hbm.at[there], inertia_ref.at[here], small_sems.at[1, place]
        )
        tend_copy = pltpu.make_async_copy(
            tend_hbm.at[:, :, there], tend_ref.at[:, :, here], large_sems.at[place]
        )
        copies.append((count_copy, inertia_copy, tend_copy))
        start += size
    thick_copy.start()
    for group in copies:
        for copy in group:
            copy.start()
    thick_copy.wait()
    start = 0
    results = []
    for place, (row, size) in enumerate(bands):
        part = slice(start, start + size)
        for copy in copies[place]:
            copy.wait()
        count = count_ref[part]
        first = jnp.zeros(count.shape, jnp.float32)
        second = jnp.zeros(count.shape, jnp.float32)
        depth = jnp.zeros(count.shape, jnp.float32)
        for level in range(levels):
            layer = jnp.where(count > level, thick_ref[level], 0.0)
            depth = depth + layer
            first = first + layer * tend_ref[0, level, part].astype(jnp.float32)
            second = second + layer * tend_ref[1, level, part].astype(jnp.float32)
        values = (first, second, depth, inertia_ref[part])
        if outer:
            results.append(values)
        else:
            fields_ref, side_ref = outs
            for field in range(FIELDS):
                fields_ref[field, part] = values[field]
            side_ref[part] = pack_edges(fields_ref, part)
        start += size
    if outer:
        near_ref, far_ref = outs
        even = is_even("lat")
        for field in range(FIELDS):
            head = results[0][field][:ROWS]
            tail = results[1][field][-ROWS:]
            near_ref[field] = jnp.where(even, tail, head)
            far_ref[field] = jnp.where(even, head, tail)


def integrate(tendency, thickness, level_count, inertia, bands, outer):
    components, levels, _, cols = tendency.shape
    rows = sum(size for _, size in bands)
    f32 = jnp.float32
    if outer:
        out_shape = [jax.ShapeDtypeStruct((FIELDS, ROWS, cols), f32)] * 2
    else:
        out_shape = [
            jax.ShapeDtypeStruct((FIELDS, rows, cols), f32),
            jax.ShapeDtypeStruct((rows, LANES), f32),
        ]
    return pl.pallas_call(
        functools.partial(integrate_kernel, bands, outer),
        in_specs=[pl.BlockSpec(memory_space=pltpu.HBM)] * 4,
        out_shape=out_shape,
        scratch_shapes=[
            pltpu.SMEM(thickness.shape, f32),
            pltpu.VMEM((rows, cols), jnp.int32),
            pltpu.VMEM((rows, cols), f32),
            pltpu.VMEM((components, levels, rows, cols), tendency.dtype),
            pltpu.SemaphoreType.DMA,
            pltpu.SemaphoreType.DMA((2, len(bands))),
            pltpu.SemaphoreType.DMA((len(bands),)),
        ],
        cost_estimate=pl.CostEstimate(
            flops=6 * components * levels * rows * cols,
            bytes_accessed=2 * components * levels * rows * cols,
            transcendentals=0,
        ),
        compiler_params=None if outer else pltpu.CompilerParams(vmem_limit_bytes=WHOLE_BYTES),
        name="outer" if outer else "whole",
    )(thickness, level_count, inertia, tendency)


def edges_kernel(side_ref, near_ref, far_ref, near_out_ref, far_out_ref):
    even_lat = is_even("lat")
    even_lon = is_even("lon")
    near = pack_edges(near_ref, slice(None))
    far = pack_edges(far_ref, slice(None))
    north = jnp.where(even_lat, far, near)
    south = jnp.where(even_lat, near, far)
    packed = jnp.concatenate([north, side_ref[...], south], axis=0)
    size = near_out_ref.shape[0]
    lane = lanes_of(near_out_ref.shape)
    west = jnp.zeros(near_out_ref.shape, jnp.float32)
    east = jnp.zeros(near_out_ref.shape, jnp.float32)
    for group in range(GROUPS):
        rows = packed[group * size : (group + 1) * size]
        at = group * PITCH
        here = (lane >= at) & (lane < at + PITCH)
        west = jnp.where(here, turn(rows, at), west)
        east = jnp.where(here, turn(rows, at - HALF), east)
    near_out_ref[...] = jnp.where(even_lon, east, west)
    far_out_ref[...] = jnp.where(even_lon, west, east)


def edges(side, near, far):
    rows = side.shape[0] + 2 * ROWS
    message = jax.ShapeDtypeStruct((rows // GROUPS, LANES), jnp.float32)
    return pl.pallas_call(
        edges_kernel,
        out_shape=[message, message],
        compiler_params=pltpu.CompilerParams(vmem_limit_bytes=VMEM_BYTES),
        name="edges",
    )(side, near, far)


def smooth(field):
    rows, cols = field.shape
    tall = field + 0.5 * (pltpu.roll(field, 1, 0) + pltpu.roll(field, rows - 1, 0))
    return tall + 0.5 * (pltpu.roll(tall, 1, 1) + pltpu.roll(tall, cols - 1, 1))


def basis(first, second, depth, inertia):
    tall, wide = first.shape
    own = slice(ROWS, tall - ROWS)
    inside = inertia > 0.0
    east_west = pltpu.roll(first, wide - 1, 1) - pltpu.roll(first, 1, 1)
    north_south = pltpu.roll(second, tall - 1, 0) - pltpu.roll(second, 1, 0)
    scaled = jnp.where(depth > 0.0, 0.5 * (east_west + north_south), 0.0)
    diag = inertia + 2.0 * depth + smooth(depth)
    inverse = jnp.where(inside, 1.0 / jnp.where(inside, diag, 1.0), 0.0)
    mws = [scaled[own]]
    ws = []
    vector = scaled * inverse
    for step in range(STEPS):
        ws.append(vector[own])
        weighed = depth * vector
        scaled = depth * smooth(vector) + smooth(weighed) - 2.0 * weighed
        mws.append(scaled[own])
        if step + 1 < STEPS:
            vector = scaled * inverse
    return ws, mws


def moments(ws, mws, mask):
    ws = [jnp.where(mask, values, 0.0) for values in ws]
    images = [mws[place] - mws[place + 1] for place in range(STEPS)]
    pairs = [ws[place] * mws[0] for place in range(STEPS)]
    for low in range(STEPS):
        for high in range(low, STEPS):
            pairs.append(ws[low] * images[high])
    lines = []
    for product in pairs:
        line = jnp.sum(product, axis=0, keepdims=True)
        total = line[:, :LANES]
        for start in range(LANES, line.shape[1], LANES):
            total = total + line[:, start : start + LANES]
        total = total + turn(total, HALF)
        lines.append(total + turn(total, QUARTER))
    quarter = lanes_of((1, LANES)) // QUARTER
    packed = []
    for start in range(0, len(lines), 4):
        row = jnp.zeros((1, LANES), jnp.float32)
        for place, line in enumerate(lines[start : start + 4]):
            row = jnp.where(quarter == place, line, row)
        packed.append(row)
    packed.append(jnp.zeros((ROWS - len(packed), LANES), jnp.float32))
    return jnp.concatenate(packed, axis=0)


def interior_kernel(
    fields_ref,
    near_ref,
    far_ref,
    w_ref,
    mw_ref,
    strip_ref,
    sums_ref,
):
    cols = fields_ref.shape[2]
    even = is_even("lat")
    lane = lanes_of((strip_ref.shape[1], LANES))
    padded = []
    for place in range(FIELDS):
        near = near_ref[place]
        far = far_ref[place]
        north = jnp.where(even, far, near)
        south = jnp.where(even, near, far)
        values = jnp.concatenate([north, fields_ref[place], south], axis=0)
        east = turn(values[:, cols - LANES :], SEAM)
        strip_ref[place] = jnp.where(lane < HALF, values[:, :LANES], east)
        padded.append(values)
    ws, mws = basis(*padded)
    for place, values in enumerate(ws):
        w_ref[place] = values
    for place, values in enumerate(mws):
        mw_ref[place] = values
    lane = lanes_of(ws[0].shape)
    sums_ref[...] = moments(ws, mws, (lane >= RIM) & (lane < cols - RIM))


def interior(fields, near, far):
    _, rows, cols = fields.shape
    f32 = jnp.float32
    return pl.pallas_call(
        interior_kernel,
        out_shape=[
            jax.ShapeDtypeStruct((STEPS, rows, cols), f32),
            jax.ShapeDtypeStruct((STEPS + 1, rows, cols), f32),
            jax.ShapeDtypeStruct((FIELDS, rows + 2 * ROWS, LANES), f32),
            jax.ShapeDtypeStruct((ROWS, LANES), f32),
        ],
        compiler_params=pltpu.CompilerParams(vmem_limit_bytes=VMEM_BYTES),
        cost_estimate=pl.CostEstimate(
            flops=300 * rows * cols, bytes_accessed=64 * rows * cols, transcendentals=0
        ),
        name="interior",
    )(fields, near, far)


def strip_kernel(strip_in_ref, far_ref, near_ref, inner_ref, w_ref, mw_ref, sums_ref):
    even = is_even("lon")
    near = near_ref[...]
    far = far_ref[...]
    from_east = jnp.where(even, near, far)
    from_west = jnp.where(even, far, near)
    lane = lanes_of(near.shape)
    padded = []
    for place in range(FIELDS):
        halo = []
        for group in range(GROUPS):
            at = group * PITCH + place * RIM
            east = turn(from_east, SEAM - at)
            west = turn(from_west, LANES - RIM - at)
            west = jnp.where(lane >= LANES - RIM, west, 0.0)
            halo.append(jnp.where(lane < SEAM + RIM, east, west))
        halo = jnp.concatenate(halo, axis=0)
        padded.append(jnp.where(lanes_of(halo.shape) < SEAM, strip_in_ref[place], halo))
    ws, mws = basis(*padded)
    for place, values in enumerate(ws):
        w_ref[place] = values
    for place, values in enumerate(mws):
        mw_ref[place] = values
    lane = lanes_of(ws[0].shape)
    edge = (lane < RIM) | ((lane >= SEAM - RIM) & (lane < SEAM))
    sums_ref[...] = inner_ref[...] + moments(ws, mws, edge)


def strip(strip_in, near, far, inner):
    rows = strip_in.shape[1] - 2 * ROWS
    f32 = jnp.float32
    return pl.pallas_call(
        strip_kernel,
        out_shape=[
            jax.ShapeDtypeStruct((STEPS, rows, LANES), f32),
            jax.ShapeDtypeStruct((STEPS + 1, rows, LANES), f32),
            jax.ShapeDtypeStruct((ROWS, LANES), f32),
        ],
        compiler_params=pltpu.CompilerParams(vmem_limit_bytes=VMEM_BYTES),
        name="strip",
    )(strip_in, far, near, inner)


def power(exponent):
    size = jnp.abs(exponent)
    value = jnp.ones(exponent.shape, jnp.float32)
    for bit in range(7):
        up, down = 2.0 ** (1 << bit), 2.0 ** -(1 << bit)
        factor = jnp.where(exponent < 0, down, up)
        value = value * jnp.where((size >> bit) & 1 == 1, factor, 1.0)
    return value


def exponent_of(size):
    bits = jnp.ceil(jnp.log2(jnp.maximum(size, 2.0**-100)))
    return jnp.clip(bits, -100.0, 100.0).astype(jnp.int32)


def nearest(values):
    return jnp.floor(values + 0.5)


def place_kernel(owner_ref, fields_ref, sent_ref, scale_ref):
    count = owner_ref.shape[0]
    span = fields_ref.shape[1] // count
    sent_ref[...] = jnp.zeros(sent_ref.shape, jnp.int16)
    scale_ref[...] = jnp.zeros(scale_ref.shape, jnp.float32)
    for block in range(count):
        target = owner_ref[block]

        @pl.when(target >= 0)
        def _(block=block, target=target):
            rows = slice(block * span, (block + 1) * span)
            for half in range(fields_ref.shape[2] // LANES):
                cols = slice(half * LANES, (half + 1) * LANES)
                pieces = [fields_ref[0, rows, cols], fields_ref[1, rows, cols]]
                values = jnp.concatenate(pieces, axis=0)
                bits = exponent_of(jnp.max(jnp.abs(values), axis=0, keepdims=True))
                whole = jnp.clip(nearest(values * power(15 - bits)), -32767.0, 32767.0)
                there = slice(2 * span * half, 2 * span * (half + 1))
                sent_ref[target, there] = whole.astype(jnp.int32).astype(jnp.int16)
                scale_ref[target, half : half + 1] = bits.astype(jnp.float32)


def place(owner, fields, lon_count):
    _, rows, cols = fields.shape
    span = rows // owner.shape[0]
    return pl.pallas_call(
        place_kernel,
        in_specs=[
            pl.BlockSpec(memory_space=pltpu.SMEM),
            pl.BlockSpec(memory_space=pltpu.VMEM),
        ],
        out_shape=[
            jax.ShapeDtypeStruct((lon_count, cols // LANES * 2 * span + TAIL, LANES), jnp.int16),
            jax.ShapeDtypeStruct((lon_count, ROWS, LANES), jnp.float32),
        ],
        compiler_params=pltpu.CompilerParams(vmem_limit_bytes=VMEM_BYTES),
        cost_estimate=pl.CostEstimate(
            flops=60 * rows * cols, bytes_accessed=12 * rows * cols, transcendentals=0
        ),
        name="place",
    )(owner, fields)


def seal_kernel(sums_ref, other_ref, scale_ref, tail_ref):
    sums = sums_ref[:SUM_ROWS] + other_ref[:SUM_ROWS]
    bits = exponent_of(jnp.abs(sums))
    scaled = sums * power(-bits) * 2.0**14
    high = nearest(scaled)
    low = nearest((scaled - high) * 2.0**15)
    parts = jnp.concatenate([bits.astype(jnp.float32), high, low], axis=0)
    for slot in range(tail_ref.shape[0]):
        tile = jnp.concatenate([parts, scale_ref[slot, : TAIL - 3 * SUM_ROWS]], axis=0)
        tail_ref[slot] = tile.astype(jnp.int32).astype(jnp.int16)


def seal(sums, other, scale):
    return pl.pallas_call(
        seal_kernel,
        out_shape=jax.ShapeDtypeStruct((scale.shape[0], TAIL, LANES), jnp.int16),
        compiler_params=pltpu.CompilerParams(vmem_limit_bytes=VMEM_BYTES),
        name="seal",
    )(sums, other, scale)


def combine_kernel(
    arrived_ref,
    w_ref,
    mw_ref,
    w_edge_ref,
    mw_edge_ref,
    pressure_hbm,
    residual_hbm,
    held_hbm,
    pressure_ref,
    residual_ref,
    held_ref,
    held_sem,
    sems,
):
    rows = held_ref.shape[1]
    packed = jnp.zeros((SUM_ROWS, LANES), jnp.float32)
    for slot in range(held_ref.shape[0]):
        tail = arrived_ref[slot, arrived_ref.shape[1] - TAIL :].astype(jnp.int32)
        digits = tail.astype(jnp.float32)
        high = digits[SUM_ROWS : 2 * SUM_ROWS]
        low = digits[2 * SUM_ROWS : 3 * SUM_ROWS]
        packed = packed + (high + low * 2.0**-15) * power(tail[:SUM_ROWS] - 14)
        for half in range(held_ref.shape[2] // LANES):
            at = 3 * SUM_ROWS + half
            scale = power(tail[at : at + 1] - 15)
            whole = arrived_ref[slot, half * rows : (half + 1) * rows].astype(jnp.int32)
            held_ref[slot, :, half * LANES : (half + 1) * LANES] = whole.astype(jnp.float32) * scale
    held_copy = pltpu.make_async_copy(held_ref, held_hbm, held_sem)
    held_copy.start()
    quarter = lanes_of(packed.shape) // QUARTER
    totals = [
        jnp.sum(jnp.where(quarter == place, packed, 0.0), axis=1, keepdims=True)
        for place in range(4)
    ]
    entry = lambda place: totals[place % 4][place // 4 : place // 4 + 1, :]
    right = [entry(place) for place in range(STEPS)]
    matrix = {}
    place = STEPS
    for low in range(STEPS):
        for high in range(low, STEPS):
            matrix[low, high] = entry(place)
            place += 1
    for pivot in range(STEPS):
        inverse = 1.0 / matrix[pivot, pivot]
        for row in range(pivot + 1, STEPS):
            factor = matrix[pivot, row] * inverse
            for col in range(row, STEPS):
                matrix[row, col] = matrix[row, col] - factor * matrix[pivot, col]
            right[row] = right[row] - factor * right[pivot]
        matrix[pivot, pivot] = inverse
    for pivot in reversed(range(STEPS)):
        for col in range(pivot + 1, STEPS):
            right[pivot] = right[pivot] - matrix[pivot, col] * right[col]
        right[pivot] = right[pivot] * matrix[pivot, pivot]

    def results(w_ref, mw_ref, part):
        pressure = right[0] * w_ref[0, part]
        residual = mw_ref[0, part] - right[0] * (mw_ref[0, part] - mw_ref[1, part])
        for place in range(1, STEPS):
            pressure = pressure + right[place] * w_ref[place, part]
            image = mw_ref[place, part] - mw_ref[place + 1, part]
            residual = residual - right[place] * image
        return pressure, residual

    rows, cols = pressure_ref.shape
    copies = []
    for piece in range(PIECES):
        part = slice(piece * rows // PIECES, (piece + 1) * rows // PIECES)
        inner = results(w_ref, mw_ref, part)
        edge = results(w_edge_ref, mw_edge_ref, part)
        lane = lanes_of(edge[0].shape)
        for field, (out_ref, out_hbm, inside, border) in enumerate(
            zip((pressure_ref, residual_ref), (pressure_hbm, residual_hbm), inner, edge)
        ):
            out_ref[part, :LANES] = jnp.where(lane < RIM, border, inside[:, :LANES])
            if cols > 2 * LANES:
                out_ref[part, LANES : cols - LANES] = inside[:, LANES : cols - LANES]
            out_ref[part, cols - LANES :] = jnp.where(
                lane >= LANES - RIM, turn(border, -SEAM), inside[:, cols - LANES :]
            )
            there = pl.ds(piece * rows // PIECES, rows // PIECES)
            copy = pltpu.make_async_copy(
                out_ref.at[there], out_hbm.at[there], sems.at[field, piece]
            )
            copy.start()
            copies.append(copy)
    held_copy.wait()
    for copy in copies:
        copy.wait()


def combine(arrived, w, mw, w_edge, mw_edge):
    rows, cols = w.shape[1:]
    shape = jax.ShapeDtypeStruct((rows, cols), jnp.float32)
    held = (arrived.shape[0], (arrived.shape[1] - TAIL) * LANES // cols, cols)
    return pl.pallas_call(
        combine_kernel,
        out_shape=[shape, shape, jax.ShapeDtypeStruct(held, jnp.float32)],
        out_specs=[pl.BlockSpec(memory_space=pltpu.HBM)] * 3,
        scratch_shapes=[
            pltpu.VMEM((rows, cols), jnp.float32),
            pltpu.VMEM((rows, cols), jnp.float32),
            pltpu.VMEM(held, jnp.float32),
            pltpu.SemaphoreType.DMA,
            pltpu.SemaphoreType.DMA((2, PIECES)),
        ],
        compiler_params=pltpu.CompilerParams(vmem_limit_bytes=VMEM_BYTES),
        name="combine",
    )(arrived, w, mw, w_edge, mw_edge)


def exchange(values, axis, distance):
    pairs = [(place, place ^ distance) for place in range(lax.axis_size(axis))]
    return lax.ppermute(values, axis, pairs)


def swap(values, axis, first, ring):
    count = lax.axis_size(axis)
    pairs = []
    for place in range(first, count if ring else count - 1, 2):
        beside = (place + 1) % count
        pairs += [(place, beside), (beside, place)]
    return lax.ppermute(values, axis, pairs)


def on_device(tendency, thickness, level_count, block_mask, owner, inertia):
    lat_count = lax.axis_size("lat")
    lon_count = lax.axis_size("lon")
    rows = level_count.shape[0]
    inputs = (tendency, thickness, level_count, inertia)
    near, far = integrate(*inputs, ((0, OUTER), (rows - OUTER, OUTER)), True)
    bands = tuple((row, CHUNK) for row in range(0, rows, CHUNK))
    fields, side = integrate(*inputs, bands, False)
    near = swap(near, "lat", 0, False)
    far = swap(far, "lat", 1, False)
    near_edge, far_edge = edges(side, near, far)
    far_edge = swap(far_edge, "lon", 1, True)
    near_edge = swap(near_edge, "lon", 0, True)
    w, mw, strip_in, inner = interior(fields, near, far)
    w_edge, mw_edge, sums = strip(strip_in, near_edge, far_edge, inner)
    sent, scale = place(owner[:, 0], fields, lon_count)
    shift = 1
    while 2 * shift < lat_count:
        sums = sums + exchange(sums, "lat", shift)
        shift *= 2
    tail = seal(sums, exchange(sums, "lat", shift), scale)
    sent = lax.dynamic_update_slice(sent, tail, (0, sent.shape[1] - TAIL, 0))
    arrived = lax.all_to_all(sent, "lon", split_axis=0, concat_axis=0, tiled=True)
    pressure, residual, held = combine(arrived, w, mw, w_edge, mw_edge)
    held = held.reshape((1, 1, lon_count, 2, held.shape[1] // 2, held.shape[2]))
    return (held, pressure, residual)


def solution(mesh):
    return jax.shard_map(
        on_device,
        mesh=mesh,
        in_specs=(
            P(None, None, "lat", "lon"),
            P(),
            P("lat", "lon"),
            P("lat", "lon"),
            P("lat", "lon"),
            P("lat", "lon"),
        ),
        out_specs=(P("lat", "lon", None, None, None, None), P("lat", "lon"), P("lat", "lon")),
        check_vma=False,
    )
```

```python
import functools

import jax
import jax.numpy as jnp
from jax import lax
from jax.experimental import pallas as pl
from jax.experimental.pallas import tpu as pltpu
from jax.sharding import PartitionSpec as P

STEPS = 4
RIM = STEPS + 1
ROWS = 8
LANES = 128
HALF = LANES // 2
QUARTER = LANES // 4
EAST = 48
SEAM = HALF + EAST
CHUNK = 16
FIELDS = 4
GROUPS = 6
PITCH = LANES // GROUPS
PIECES = 2
OUTER = 16
TAIL = 16
SUM_ROWS = 4
VMEM_BYTES = 16 * 1024 * 1024
WHOLE_BYTES = 56450000


def lanes_of(shape):
    return lax.broadcasted_iota(jnp.int32, shape, len(shape) - 1)


def turn(values, amount):
    amount = amount % values.shape[1]
    return pltpu.roll(values, amount, 1) if amount else values


def sides(near, far):
    place = lax.axis_index("lat")
    even = is_even("lat")
    last = lax.axis_size("lat") - 1
    north = jnp.where(place == 0, 0.0, jnp.where(even, far, near))
    south = jnp.where(place == last, 0.0, jnp.where(even, near, far))
    return north, south


def is_even(axis):
    return lax.rem(lax.axis_index(axis), 2) == 0


def pack_edges(ref, part):
    cols = ref.shape[2]
    packed = None
    for place in range(FIELDS):
        west = ref[place, part, :LANES]
        east = ref[place, part, cols - LANES :]
        if packed is None:
            lane = lanes_of(west.shape)
            packed = jnp.zeros(west.shape, jnp.float32)
        at = place * RIM
        packed = jnp.where((lane >= at) & (lane < at + RIM), turn(west, at), packed)
        at = HALF + place * RIM
        packed = jnp.where((lane >= at) & (lane < at + RIM), turn(east, at + RIM), packed)
    return packed


def integrate_kernel(bands, outer, thick_hbm, count_hbm, inertia_hbm, tend_hbm, *refs):
    outs, scratch = refs[:2], refs[2:]
    thick_ref, count_ref, inertia_ref, tend_ref, thick_sem, small_sems, large_sems = scratch[:7]
    levels = tend_hbm.shape[1]
    thick_copy = pltpu.make_async_copy(thick_hbm, thick_ref, thick_sem)
    copies = []
    start = 0
    for place, (row, size) in enumerate(bands):
        there = pl.ds(row, size)
        here = pl.ds(start, size)
        count_copy = pltpu.make_async_copy(
            count_hbm.at[there], count_ref.at[here], small_sems.at[0, place]
        )
        inertia_copy = pltpu.make_async_copy(
            inertia_hbm.at[there], inertia_ref.at[here], small_sems.at[1, place]
        )
        tend_copy = pltpu.make_async_copy(
            tend_hbm.at[:, :, there], tend_ref.at[:, :, here], large_sems.at[place]
        )
        copies.append((count_copy, inertia_copy, tend_copy))
        start += size
    thick_copy.start()
    for group in copies:
        for copy in group:
            copy.start()
    thick_copy.wait()
    start = 0
    results = []
    for place, (row, size) in enumerate(bands):
        part = slice(start, start + size)
        for copy in copies[place]:
            copy.wait()
        count = count_ref[part]
        first = jnp.zeros(count.shape, jnp.float32)
        second = jnp.zeros(count.shape, jnp.float32)
        depth = jnp.zeros(count.shape, jnp.float32)
        for level in range(levels):
            layer = jnp.where(count > level, thick_ref[level], 0.0)
            depth = depth + layer
            first = first + layer * tend_ref[0, level, part].astype(jnp.float32)
            second = second + layer * tend_ref[1, level, part].astype(jnp.float32)
        values = (first, second, depth, inertia_ref[part])
        if outer:
            results.append(values)
        else:
            fields_hbm, side_ref = outs
            fields_ref, out_sems = scratch[7:]
            for field in range(FIELDS):
                fields_ref[field, part] = values[field]
            here = pl.ds(start, size)
            done = pltpu.make_async_copy(
                fields_ref.at[:, here], fields_hbm.at[:, here], out_sems.at[place]
            )
            done.start()
            results.append(done)
            side_ref[part] = pack_edges(fields_ref, part)
        start += size
    if outer:
        near_ref, far_ref = outs
        even = is_even("lat")
        for field in range(FIELDS):
            head = results[0][field][:ROWS]
            tail = results[1][field][-ROWS:]
            near_ref[field] = jnp.where(even, tail, head)
            far_ref[field] = jnp.where(even, head, tail)
    else:
        for done in results:
            done.wait()


def integrate(tendency, thickness, level_count, inertia, bands, outer):
    components, levels, _, cols = tendency.shape
    rows = sum(size for _, size in bands)
    f32 = jnp.float32
    if outer:
        out_shape = [jax.ShapeDtypeStruct((FIELDS, ROWS, cols), f32)] * 2
        out_space = [pltpu.VMEM] * 2
        extra = []
    else:
        out_space = [pltpu.HBM, pltpu.VMEM]
        extra = [
            pltpu.VMEM((FIELDS, rows, cols), f32),
            pltpu.SemaphoreType.DMA((len(bands),)),
        ]
        out_shape = [
            jax.ShapeDtypeStruct((FIELDS, rows, cols), f32),
            jax.ShapeDtypeStruct((rows, LANES), f32),
        ]
    return pl.pallas_call(
        functools.partial(integrate_kernel, bands, outer),
        in_specs=[pl.BlockSpec(memory_space=pltpu.HBM)] * 4,
        out_shape=out_shape,
        out_specs=[pl.BlockSpec(memory_space=space) for space in out_space],
        scratch_shapes=[
            pltpu.SMEM(thickness.shape, f32),
            pltpu.VMEM((rows, cols), jnp.int32),
            pltpu.VMEM((rows, cols), f32),
            pltpu.VMEM((components, levels, rows, cols), tendency.dtype),
            pltpu.SemaphoreType.DMA,
            pltpu.SemaphoreType.DMA((2, len(bands))),
            pltpu.SemaphoreType.DMA((len(bands),)),
            *extra,
        ],
        cost_estimate=pl.CostEstimate(
            flops=6 * components * levels * rows * cols,
            bytes_accessed=2 * components * levels * rows * cols,
            transcendentals=0,
        ),
        compiler_params=None if outer else pltpu.CompilerParams(vmem_limit_bytes=WHOLE_BYTES),
        name="outer" if outer else "whole",
    )(thickness, level_count, inertia, tendency)


def edges_kernel(side_ref, near_ref, far_ref, near_out_ref, far_out_ref):
    even_lon = is_even("lon")
    near = pack_edges(near_ref, slice(None))
    far = pack_edges(far_ref, slice(None))
    north, south = sides(near, far)
    packed = jnp.concatenate([north, side_ref[...], south], axis=0)
    size = near_out_ref.shape[0]
    lane = lanes_of(near_out_ref.shape)
    west = jnp.zeros(near_out_ref.shape, jnp.float32)
    east = jnp.zeros(near_out_ref.shape, jnp.float32)
    for group in range(GROUPS):
        rows = packed[group * size : (group + 1) * size]
        at = group * PITCH
        here = (lane >= at) & (lane < at + PITCH)
        west = jnp.where(here, turn(rows, at), west)
        east = jnp.where(here, turn(rows, at - HALF), east)
    near_out_ref[...] = jnp.where(even_lon, east, west)
    far_out_ref[...] = jnp.where(even_lon, west, east)


def edges(side, near, far):
    rows = side.shape[0] + 2 * ROWS
    message = jax.ShapeDtypeStruct((rows // GROUPS, LANES), jnp.float32)
    return pl.pallas_call(
        edges_kernel,
        out_shape=[message, message],
        compiler_params=pltpu.CompilerParams(vmem_limit_bytes=VMEM_BYTES),
        name="edges",
    )(side, near, far)


def smooth(field):
    rows, cols = field.shape
    tall = field + 0.5 * (pltpu.roll(field, 1, 0) + pltpu.roll(field, rows - 1, 0))
    return tall + 0.5 * (pltpu.roll(tall, 1, 1) + pltpu.roll(tall, cols - 1, 1))


def basis(first, second, depth, inertia):
    tall, wide = first.shape
    own = slice(ROWS, tall - ROWS)
    inside = inertia > 0.0
    east_west = pltpu.roll(first, wide - 1, 1) - pltpu.roll(first, 1, 1)
    north_south = pltpu.roll(second, tall - 1, 0) - pltpu.roll(second, 1, 0)
    scaled = jnp.where(depth > 0.0, 0.5 * (east_west + north_south), 0.0)
    diag = inertia + 2.0 * depth + smooth(depth)
    inverse = jnp.where(inside, 1.0 / jnp.where(inside, diag, 1.0), 0.0)
    mws = [scaled[own]]
    ws = []
    vector = scaled * inverse
    for step in range(STEPS):
        ws.append(vector[own])
        weighed = depth * vector
        scaled = depth * smooth(vector) + smooth(weighed) - 2.0 * weighed
        mws.append(scaled[own])
        if step + 1 < STEPS:
            vector = scaled * inverse
    return ws, mws


def moments(ws, mws, mask):
    ws = [jnp.where(mask, values, 0.0) for values in ws]
    images = [mws[place] - mws[place + 1] for place in range(STEPS)]
    pairs = [ws[place] * mws[0] for place in range(STEPS)]
    for low in range(STEPS):
        for high in range(low, STEPS):
            pairs.append(ws[low] * images[high])
    lines = []
    for product in pairs:
        line = jnp.sum(product, axis=0, keepdims=True)
        total = line[:, :LANES]
        for start in range(LANES, line.shape[1], LANES):
            total = total + line[:, start : start + LANES]
        total = total + turn(total, HALF)
        lines.append(total + turn(total, QUARTER))
    quarter = lanes_of((1, LANES)) // QUARTER
    packed = []
    for start in range(0, len(lines), 4):
        row = jnp.zeros((1, LANES), jnp.float32)
        for place, line in enumerate(lines[start : start + 4]):
            row = jnp.where(quarter == place, line, row)
        packed.append(row)
    packed.append(jnp.zeros((ROWS - len(packed), LANES), jnp.float32))
    return jnp.concatenate(packed, axis=0)


def interior_kernel(
    fields_ref,
    near_ref,
    far_ref,
    w_ref,
    mw_ref,
    strip_ref,
    sums_ref,
):
    cols = fields_ref.shape[2]
    lane = lanes_of((strip_ref.shape[1], LANES))
    padded = []
    for place in range(FIELDS):
        north, south = sides(near_ref[place], far_ref[place])
        values = jnp.concatenate([north, fields_ref[place], south], axis=0)
        east = turn(values[:, cols - LANES :], SEAM)
        strip_ref[place] = jnp.where(lane < HALF, values[:, :LANES], east)
        padded.append(values)
    ws, mws = basis(*padded)
    for place, values in enumerate(ws):
        w_ref[place] = values
    for place, values in enumerate(mws):
        mw_ref[place] = values
    lane = lanes_of(ws[0].shape)
    sums_ref[...] = moments(ws, mws, (lane >= RIM) & (lane < cols - RIM))


def interior(fields, near, far):
    _, rows, cols = fields.shape
    f32 = jnp.float32
    return pl.pallas_call(
        interior_kernel,
        out_shape=[
            jax.ShapeDtypeStruct((STEPS, rows, cols), f32),
            jax.ShapeDtypeStruct((STEPS + 1, rows, cols), f32),
            jax.ShapeDtypeStruct((FIELDS, rows + 2 * ROWS, LANES), f32),
            jax.ShapeDtypeStruct((ROWS, LANES), f32),
        ],
        compiler_params=pltpu.CompilerParams(vmem_limit_bytes=VMEM_BYTES),
        cost_estimate=pl.CostEstimate(
            flops=300 * rows * cols, bytes_accessed=64 * rows * cols, transcendentals=0
        ),
        name="interior",
    )(fields, near, far)


def strip_kernel(strip_in_ref, far_ref, near_ref, inner_ref, w_ref, mw_ref, sums_ref):
    even = is_even("lon")
    near = near_ref[...]
    far = far_ref[...]
    from_east = jnp.where(even, near, far)
    from_west = jnp.where(even, far, near)
    lane = lanes_of(near.shape)
    padded = []
    for place in range(FIELDS):
        halo = []
        for group in range(GROUPS):
            at = group * PITCH + place * RIM
            east = turn(from_east, SEAM - at)
            west = turn(from_west, LANES - RIM - at)
            west = jnp.where(lane >= LANES - RIM, west, 0.0)
            halo.append(jnp.where(lane < SEAM + RIM, east, west))
        halo = jnp.concatenate(halo, axis=0)
        padded.append(jnp.where(lanes_of(halo.shape) < SEAM, strip_in_ref[place], halo))
    ws, mws = basis(*padded)
    for place, values in enumerate(ws):
        w_ref[place] = values
    for place, values in enumerate(mws):
        mw_ref[place] = values
    lane = lanes_of(ws[0].shape)
    edge = (lane < RIM) | ((lane >= SEAM - RIM) & (lane < SEAM))
    sums_ref[...] = inner_ref[...] + moments(ws, mws, edge)


def strip(strip_in, near, far, inner):
    rows = strip_in.shape[1] - 2 * ROWS
    f32 = jnp.float32
    return pl.pallas_call(
        strip_kernel,
        out_shape=[
            jax.ShapeDtypeStruct((STEPS, rows, LANES), f32),
            jax.ShapeDtypeStruct((STEPS + 1, rows, LANES), f32),
            jax.ShapeDtypeStruct((ROWS, LANES), f32),
        ],
        compiler_params=pltpu.CompilerParams(vmem_limit_bytes=VMEM_BYTES),
        name="strip",
    )(strip_in, far, near, inner)


def power(exponent):
    size = jnp.abs(exponent)
    value = jnp.ones(exponent.shape, jnp.float32)
    for bit in range(7):
        up, down = 2.0 ** (1 << bit), 2.0 ** -(1 << bit)
        factor = jnp.where(exponent < 0, down, up)
        value = value * jnp.where((size >> bit) & 1 == 1, factor, 1.0)
    return value


def exponent_of(size):
    bits = jnp.ceil(jnp.log2(jnp.maximum(size, 2.0**-100)))
    return jnp.clip(bits, -100.0, 100.0).astype(jnp.int32)


def nearest(values):
    return jnp.floor(values + 0.5)


def place_kernel(owner_ref, fields_ref, sent_ref, scale_ref):
    count = owner_ref.shape[0]
    span = fields_ref.shape[1] // count
    sent_ref[...] = jnp.zeros(sent_ref.shape, jnp.int16)
    scale_ref[...] = jnp.zeros(scale_ref.shape, jnp.float32)
    for block in range(count):
        target = owner_ref[block]

        @pl.when(target >= 0)
        def _(block=block, target=target):
            rows = slice(block * span, (block + 1) * span)
            for half in range(fields_ref.shape[2] // LANES):
                cols = slice(half * LANES, (half + 1) * LANES)
                pieces = [fields_ref[0, rows, cols], fields_ref[1, rows, cols]]
                values = jnp.concatenate(pieces, axis=0)
                bits = exponent_of(jnp.max(jnp.abs(values), axis=0, keepdims=True))
                whole = jnp.clip(nearest(values * power(15 - bits)), -32767.0, 32767.0)
                there = slice(2 * span * half, 2 * span * (half + 1))
                sent_ref[target, there] = whole.astype(jnp.int32).astype(jnp.int16)
                scale_ref[target, half : half + 1] = bits.astype(jnp.float32)


def place(owner, fields, lon_count):
    _, rows, cols = fields.shape
    span = rows // owner.shape[0]
    return pl.pallas_call(
        place_kernel,
        in_specs=[
            pl.BlockSpec(memory_space=pltpu.SMEM),
            pl.BlockSpec(memory_space=pltpu.VMEM),
        ],
        out_shape=[
            jax.ShapeDtypeStruct((lon_count, cols // LANES * 2 * span + TAIL, LANES), jnp.int16),
            jax.ShapeDtypeStruct((lon_count, ROWS, LANES), jnp.float32),
        ],
        compiler_params=pltpu.CompilerParams(vmem_limit_bytes=VMEM_BYTES),
        cost_estimate=pl.CostEstimate(
            flops=60 * rows * cols, bytes_accessed=12 * rows * cols, transcendentals=0
        ),
        name="place",
    )(owner, fields)


def seal_kernel(sums_ref, other_ref, scale_ref, tail_ref):
    sums = sums_ref[:SUM_ROWS] + other_ref[:SUM_ROWS]
    bits = exponent_of(jnp.abs(sums))
    scaled = sums * power(-bits) * 2.0**14
    high = nearest(scaled)
    low = nearest((scaled - high) * 2.0**15)
    parts = jnp.concatenate([bits.astype(jnp.float32), high, low], axis=0)
    for slot in range(tail_ref.shape[0]):
        tile = jnp.concatenate([parts, scale_ref[slot, : TAIL - 3 * SUM_ROWS]], axis=0)
        tail_ref[slot] = tile.astype(jnp.int32).astype(jnp.int16)


def seal(sums, other, scale):
    return pl.pallas_call(
        seal_kernel,
        out_shape=jax.ShapeDtypeStruct((scale.shape[0], TAIL, LANES), jnp.int16),
        compiler_params=pltpu.CompilerParams(vmem_limit_bytes=VMEM_BYTES),
        name="seal",
    )(sums, other, scale)


def combine_kernel(
    arrived_ref,
    w_ref,
    mw_ref,
    w_edge_ref,
    mw_edge_ref,
    pressure_hbm,
    residual_hbm,
    held_hbm,
    pressure_ref,
    residual_ref,
    held_ref,
    held_sem,
    sems,
):
    rows = held_ref.shape[1]
    packed = jnp.zeros((SUM_ROWS, LANES), jnp.float32)
    for slot in range(held_ref.shape[0]):
        tail = arrived_ref[slot, arrived_ref.shape[1] - TAIL :].astype(jnp.int32)
        digits = tail.astype(jnp.float32)
        high = digits[SUM_ROWS : 2 * SUM_ROWS]
        low = digits[2 * SUM_ROWS : 3 * SUM_ROWS]
        packed = packed + (high + low * 2.0**-15) * power(tail[:SUM_ROWS] - 14)
        for half in range(held_ref.shape[2] // LANES):
            at = 3 * SUM_ROWS + half
            scale = power(tail[at : at + 1] - 15)
            whole = arrived_ref[slot, half * rows : (half + 1) * rows].astype(jnp.int32)
            held_ref[slot, :, half * LANES : (half + 1) * LANES] = whole.astype(jnp.float32) * scale
    held_copy = pltpu.make_async_copy(held_ref, held_hbm, held_sem)
    held_copy.start()
    quarter = lanes_of(packed.shape) // QUARTER
    totals = [
        jnp.sum(jnp.where(quarter == place, packed, 0.0), axis=1, keepdims=True)
        for place in range(4)
    ]
    entry = lambda place: totals[place % 4][place // 4 : place // 4 + 1, :]
    right = [entry(place) for place in range(STEPS)]
    matrix = {}
    place = STEPS
    for low in range(STEPS):
        for high in range(low, STEPS):
            matrix[low, high] = entry(place)
            place += 1
    for pivot in range(STEPS):
        inverse = 1.0 / matrix[pivot, pivot]
        for row in range(pivot + 1, STEPS):
            factor = matrix[pivot, row] * inverse
            for col in range(row, STEPS):
                matrix[row, col] = matrix[row, col] - factor * matrix[pivot, col]
            right[row] = right[row] - factor * right[pivot]
        matrix[pivot, pivot] = inverse
    for pivot in reversed(range(STEPS)):
        for col in range(pivot + 1, STEPS):
            right[pivot] = right[pivot] - matrix[pivot, col] * right[col]
        right[pivot] = right[pivot] * matrix[pivot, pivot]

    def results(w_ref, mw_ref, part):
        pressure = right[0] * w_ref[0, part]
        residual = mw_ref[0, part] - right[0] * (mw_ref[0, part] - mw_ref[1, part])
        for place in range(1, STEPS):
            pressure = pressure + right[place] * w_ref[place, part]
            image = mw_ref[place, part] - mw_ref[place + 1, part]
            residual = residual - right[place] * image
        return pressure, residual

    rows, cols = pressure_ref.shape
    copies = []
    for piece in range(PIECES):
        part = slice(piece * rows // PIECES, (piece + 1) * rows // PIECES)
        inner = results(w_ref, mw_ref, part)
        edge = results(w_edge_ref, mw_edge_ref, part)
        lane = lanes_of(edge[0].shape)
        for field, (out_ref, out_hbm, inside, border) in enumerate(
            zip((pressure_ref, residual_ref), (pressure_hbm, residual_hbm), inner, edge)
        ):
            out_ref[part, :LANES] = jnp.where(lane < RIM, border, inside[:, :LANES])
            if cols > 2 * LANES:
                out_ref[part, LANES : cols - LANES] = inside[:, LANES : cols - LANES]
            out_ref[part, cols - LANES :] = jnp.where(
                lane >= LANES - RIM, turn(border, -SEAM), inside[:, cols - LANES :]
            )
            there = pl.ds(piece * rows // PIECES, rows // PIECES)
            copy = pltpu.make_async_copy(
                out_ref.at[there], out_hbm.at[there], sems.at[field, piece]
            )
            copy.start()
            copies.append(copy)
    held_copy.wait()
    for copy in copies:
        copy.wait()


def combine(arrived, w, mw, w_edge, mw_edge):
    rows, cols = w.shape[1:]
    shape = jax.ShapeDtypeStruct((rows, cols), jnp.float32)
    held = (arrived.shape[0], (arrived.shape[1] - TAIL) * LANES // cols, cols)
    return pl.pallas_call(
        combine_kernel,
        out_shape=[shape, shape, jax.ShapeDtypeStruct(held, jnp.float32)],
        out_specs=[pl.BlockSpec(memory_space=pltpu.HBM)] * 3,
        scratch_shapes=[
            pltpu.VMEM((rows, cols), jnp.float32),
            pltpu.VMEM((rows, cols), jnp.float32),
            pltpu.VMEM(held, jnp.float32),
            pltpu.SemaphoreType.DMA,
            pltpu.SemaphoreType.DMA((2, PIECES)),
        ],
        compiler_params=pltpu.CompilerParams(vmem_limit_bytes=VMEM_BYTES),
        name="combine",
    )(arrived, w, mw, w_edge, mw_edge)


def exchange(values, axis, distance):
    pairs = [(place, place ^ distance) for place in range(lax.axis_size(axis))]
    return lax.ppermute(values, axis, pairs)


def swap(values, axis, first):
    count = lax.axis_size(axis)
    pairs = []
    for place in range(first, count, 2):
        beside = (place + 1) % count
        pairs += [(place, beside), (beside, place)]
    return lax.ppermute(values, axis, pairs)


def on_device(tendency, thickness, level_count, block_mask, owner, inertia):
    lat_count = lax.axis_size("lat")
    lon_count = lax.axis_size("lon")
    rows = level_count.shape[0]
    inputs = (tendency, thickness, level_count, inertia)
    near, far = integrate(*inputs, ((0, OUTER), (rows - OUTER, OUTER)), True)
    bands = tuple((row, CHUNK) for row in range(0, rows, CHUNK))
    fields, side = integrate(*inputs, bands, False)
    near = swap(near, "lat", 0)
    far = swap(far, "lat", 1)
    near_edge, far_edge = edges(side, near, far)
    far_edge = swap(far_edge, "lon", 1)
    near_edge = swap(near_edge, "lon", 0)
    w, mw, strip_in, inner = interior(fields, near, far)
    w_edge, mw_edge, sums = strip(strip_in, near_edge, far_edge, inner)
    sent, scale = place(owner[:, 0], fields, lon_count)
    shift = 1
    while 2 * shift < lat_count:
        sums = sums + exchange(sums, "lat", shift)
        shift *= 2
    tail = seal(sums, exchange(sums, "lat", shift), scale)
    sent = lax.dynamic_update_slice(sent, tail, (0, sent.shape[1] - TAIL, 0))
    arrived = lax.all_to_all(sent, "lon", split_axis=0, concat_axis=0, tiled=True)
    pressure, residual, held = combine(arrived, w, mw, w_edge, mw_edge)
    held = held.reshape((1, 1, lon_count, 2, held.shape[1] // 2, held.shape[2]))
    return (held, pressure, residual)


def solution(mesh):
    return jax.shard_map(
        on_device,
        mesh=mesh,
        in_specs=(
            P(None, None, "lat", "lon"),
            P(),
            P("lat", "lon"),
            P("lat", "lon"),
            P("lat", "lon"),
            P("lat", "lon"),
        ),
        out_specs=(P("lat", "lon", None, None, None, None), P("lat", "lon"), P("lat", "lon")),
        check_vma=False,
    )
```

```python
import functools

import jax
import jax.numpy as jnp
from jax import lax
from jax.experimental import pallas as pl
from jax.experimental.pallas import tpu as pltpu
from jax.sharding import PartitionSpec as P

STEPS = 4
RIM = STEPS + 1
ROWS = 8
LANES = 128
HALF = LANES // 2
QUARTER = LANES // 4
EAST = 48
SEAM = HALF + EAST
CHUNK = 32
FIELDS = 4
GROUPS = 6
PITCH = LANES // GROUPS
PIECES = 2
OUTER = 16
TAIL = 16
SUM_ROWS = 4
VMEM_BYTES = 16 * 1024 * 1024
MIDDLE_BYTES = 56450000


def lanes_of(shape):
    return lax.broadcasted_iota(jnp.int32, shape, len(shape) - 1)


def turn(values, amount):
    amount = amount % values.shape[1]
    return pltpu.roll(values, amount, 1) if amount else values


def sides(near, far):
    place = lax.axis_index("lat")
    even = is_even("lat")
    last = lax.axis_size("lat") - 1
    north = jnp.where(place == 0, 0.0, jnp.where(even, far, near))
    south = jnp.where(place == last, 0.0, jnp.where(even, near, far))
    return north, south


def is_even(axis):
    return lax.rem(lax.axis_index(axis), 2) == 0


def pack_edges(ref, part):
    cols = ref.shape[2]
    packed = None
    for place in range(FIELDS):
        west = ref[place, part, :LANES]
        east = ref[place, part, cols - LANES :]
        if packed is None:
            lane = lanes_of(west.shape)
            packed = jnp.zeros(west.shape, jnp.float32)
        at = place * RIM
        packed = jnp.where((lane >= at) & (lane < at + RIM), turn(west, at), packed)
        at = HALF + place * RIM
        packed = jnp.where((lane >= at) & (lane < at + RIM), turn(east, at + RIM), packed)
    return packed


def integrate_kernel(bands, outer, thick_hbm, count_hbm, inertia_hbm, tend_hbm, *refs):
    if outer:
        fields_ref, side_ref, near_ref, far_ref = refs[:4]
    else:
        fields_ref, side_ref = refs[:2]
    thick_ref, count_ref, inertia_ref, tend_ref, thick_sem, small_sems, large_sems = refs[-7:]
    levels = tend_hbm.shape[1]
    even = is_even("lat")
    copies = [[pltpu.make_async_copy(thick_hbm, thick_ref, thick_sem)]]
    start = 0
    for place, (row, size) in enumerate(bands):
        there = pl.ds(row, size)
        here = pl.ds(start, size)
        count_copy = pltpu.make_async_copy(
            count_hbm.at[there], count_ref.at[here], small_sems.at[0, place]
        )
        inertia_copy = pltpu.make_async_copy(
            inertia_hbm.at[there], inertia_ref.at[here], small_sems.at[1, place]
        )
        tend_copy = pltpu.make_async_copy(
            tend_hbm.at[:, :, there], tend_ref.at[:, :, here], large_sems.at[place]
        )
        copies.append([count_copy, inertia_copy, tend_copy])
        start += size
    for group in copies:
        for copy in group:
            copy.start()
    copies[0][0].wait()
    start = 0
    for place, (row, size) in enumerate(bands):
        part = slice(start, start + size)
        for copy in copies[place + 1]:
            copy.wait()
        count = count_ref[part]
        first = jnp.zeros(count.shape, jnp.float32)
        second = jnp.zeros(count.shape, jnp.float32)
        depth = jnp.zeros(count.shape, jnp.float32)
        for level in range(levels):
            layer = jnp.where(count > level, thick_ref[level], 0.0)
            depth = depth + layer
            first = first + layer * tend_ref[0, level, part].astype(jnp.float32)
            second = second + layer * tend_ref[1, level, part].astype(jnp.float32)
        for field, values in enumerate((first, second, depth, inertia_ref[part])):
            fields_ref[field, part] = values
        side_ref[part] = pack_edges(fields_ref, part)
        start += size
    if outer:
        for field in range(FIELDS):
            head = fields_ref[field, :ROWS]
            tail = fields_ref[field, start - ROWS :]
            near_ref[field] = jnp.where(even, tail, head)
            far_ref[field] = jnp.where(even, head, tail)


def integrate(tendency, thickness, level_count, inertia, bands, outer):
    components, levels, _, cols = tendency.shape
    rows = sum(size for _, size in bands)
    f32 = jnp.float32
    halo = jax.ShapeDtypeStruct((FIELDS, ROWS, cols), f32)
    return pl.pallas_call(
        functools.partial(integrate_kernel, bands, outer),
        in_specs=[pl.BlockSpec(memory_space=pltpu.HBM)] * 4,
        out_shape=[
            jax.ShapeDtypeStruct((FIELDS, rows, cols), f32),
            jax.ShapeDtypeStruct((rows, LANES), f32),
        ]
        + ([halo, halo] if outer else []),
        scratch_shapes=[
            pltpu.SMEM(thickness.shape, f32),
            pltpu.VMEM((rows, cols), jnp.int32),
            pltpu.VMEM((rows, cols), f32),
            pltpu.VMEM((components, levels, rows, cols), tendency.dtype),
            pltpu.SemaphoreType.DMA,
            pltpu.SemaphoreType.DMA((2, len(bands))),
            pltpu.SemaphoreType.DMA((len(bands),)),
        ],
        cost_estimate=pl.CostEstimate(
            flops=6 * components * levels * rows * cols,
            bytes_accessed=2 * components * levels * rows * cols,
            transcendentals=0,
        ),
        compiler_params=None if outer else pltpu.CompilerParams(vmem_limit_bytes=MIDDLE_BYTES),
        name="outer" if outer else "middle",
    )(thickness, level_count, inertia, tendency)


def edges_kernel(outer_ref, middle_ref, near_ref, far_ref, near_out_ref, far_out_ref):
    even_lon = is_even("lon")
    near = pack_edges(near_ref, slice(None))
    far = pack_edges(far_ref, slice(None))
    half = outer_ref.shape[0] // 2
    north, south = sides(near, far)
    packed = jnp.concatenate(
        [north, outer_ref[:half], middle_ref[...], outer_ref[half:], south], axis=0
    )
    size = near_out_ref.shape[0]
    lane = lanes_of(near_out_ref.shape)
    west = jnp.zeros(near_out_ref.shape, jnp.float32)
    east = jnp.zeros(near_out_ref.shape, jnp.float32)
    for group in range(GROUPS):
        rows = packed[group * size : (group + 1) * size]
        at = group * PITCH
        here = (lane >= at) & (lane < at + PITCH)
        west = jnp.where(here, turn(rows, at), west)
        east = jnp.where(here, turn(rows, at - HALF), east)
    near_out_ref[...] = jnp.where(even_lon, east, west)
    far_out_ref[...] = jnp.where(even_lon, west, east)


def edges(outer, middle, near, far):
    rows = outer.shape[0] + middle.shape[0] + 2 * ROWS
    message = jax.ShapeDtypeStruct((rows // GROUPS, LANES), jnp.float32)
    return pl.pallas_call(
        edges_kernel,
        out_shape=[message, message],
        compiler_params=pltpu.CompilerParams(vmem_limit_bytes=VMEM_BYTES),
        name="edges",
    )(outer, middle, near, far)


def smooth(field):
    rows, cols = field.shape
    tall = field + 0.5 * (pltpu.roll(field, 1, 0) + pltpu.roll(field, rows - 1, 0))
    return tall + 0.5 * (pltpu.roll(tall, 1, 1) + pltpu.roll(tall, cols - 1, 1))


def basis(first, second, depth, inertia):
    tall, wide = first.shape
    own = slice(ROWS, tall - ROWS)
    inside = inertia > 0.0
    east_west = pltpu.roll(first, wide - 1, 1) - pltpu.roll(first, 1, 1)
    north_south = pltpu.roll(second, tall - 1, 0) - pltpu.roll(second, 1, 0)
    scaled = jnp.where(depth > 0.0, 0.5 * (east_west + north_south), 0.0)
    diag = inertia + 2.0 * depth + smooth(depth)
    inverse = jnp.where(inside, 1.0 / jnp.where(inside, diag, 1.0), 0.0)
    mws = [scaled[own]]
    ws = []
    vector = scaled * inverse
    for step in range(STEPS):
        ws.append(vector[own])
        weighed = depth * vector
        scaled = depth * smooth(vector) + smooth(weighed) - 2.0 * weighed
        mws.append(scaled[own])
        if step + 1 < STEPS:
            vector = scaled * inverse
    return ws, mws


def moments(ws, mws, mask):
    ws = [jnp.where(mask, values, 0.0) for values in ws]
    images = [mws[place] - mws[place + 1] for place in range(STEPS)]
    pairs = [ws[place] * mws[0] for place in range(STEPS)]
    for low in range(STEPS):
        for high in range(low, STEPS):
            pairs.append(ws[low] * images[high])
    lines = []
    for product in pairs:
        line = jnp.sum(product, axis=0, keepdims=True)
        total = line[:, :LANES]
        for start in range(LANES, line.shape[1], LANES):
            total = total + line[:, start : start + LANES]
        total = total + turn(total, HALF)
        lines.append(total + turn(total, QUARTER))
    quarter = lanes_of((1, LANES)) // QUARTER
    packed = []
    for start in range(0, len(lines), 4):
        row = jnp.zeros((1, LANES), jnp.float32)
        for place, line in enumerate(lines[start : start + 4]):
            row = jnp.where(quarter == place, line, row)
        packed.append(row)
    packed.append(jnp.zeros((ROWS - len(packed), LANES), jnp.float32))
    return jnp.concatenate(packed, axis=0)


def interior_kernel(
    outer_ref,
    middle_ref,
    near_ref,
    far_ref,
    w_ref,
    mw_ref,
    strip_ref,
    sums_ref,
):
    half = outer_ref.shape[1] // 2
    cols = outer_ref.shape[2]
    lane = lanes_of((strip_ref.shape[1], LANES))
    padded = []
    for place in range(FIELDS):
        north, south = sides(near_ref[place], far_ref[place])
        pieces = [
            north,
            outer_ref[place, :half],
            middle_ref[place],
            outer_ref[place, half:],
            south,
        ]
        values = jnp.concatenate(pieces, axis=0)
        east = turn(values[:, cols - LANES :], SEAM)
        strip_ref[place] = jnp.where(lane < HALF, values[:, :LANES], east)
        padded.append(values)
    ws, mws = basis(*padded)
    for place, values in enumerate(ws):
        w_ref[place] = values
    for place, values in enumerate(mws):
        mw_ref[place] = values
    lane = lanes_of(ws[0].shape)
    sums_ref[...] = moments(ws, mws, (lane >= RIM) & (lane < cols - RIM))


def interior(outer, middle, near, far):
    cols = outer.shape[2]
    rows = outer.shape[1] + middle.shape[1]
    f32 = jnp.float32
    return pl.pallas_call(
        interior_kernel,
        out_shape=[
            jax.ShapeDtypeStruct((STEPS, rows, cols), f32),
            jax.ShapeDtypeStruct((STEPS + 1, rows, cols), f32),
            jax.ShapeDtypeStruct((FIELDS, rows + 2 * ROWS, LANES), f32),
            jax.ShapeDtypeStruct((ROWS, LANES), f32),
        ],
        compiler_params=pltpu.CompilerParams(vmem_limit_bytes=VMEM_BYTES),
        cost_estimate=pl.CostEstimate(
            flops=300 * rows * cols, bytes_accessed=64 * rows * cols, transcendentals=0
        ),
        name="interior",
    )(outer, middle, near, far)


def strip_kernel(strip_in_ref, far_ref, near_ref, inner_ref, w_ref, mw_ref, sums_ref):
    even = is_even("lon")
    near = near_ref[...]
    far = far_ref[...]
    from_east = jnp.where(even, near, far)
    from_west = jnp.where(even, far, near)
    lane = lanes_of(near.shape)
    padded = []
    for place in range(FIELDS):
        halo = []
        for group in range(GROUPS):
            at = group * PITCH + place * RIM
            east = turn(from_east, SEAM - at)
            west = turn(from_west, LANES - RIM - at)
            west = jnp.where(lane >= LANES - RIM, west, 0.0)
            halo.append(jnp.where(lane < SEAM + RIM, east, west))
        halo = jnp.concatenate(halo, axis=0)
        padded.append(jnp.where(lanes_of(halo.shape) < SEAM, strip_in_ref[place], halo))
    ws, mws = basis(*padded)
    for place, values in enumerate(ws):
        w_ref[place] = values
    for place, values in enumerate(mws):
        mw_ref[place] = values
    lane = lanes_of(ws[0].shape)
    edge = (lane < RIM) | ((lane >= SEAM - RIM) & (lane < SEAM))
    sums_ref[...] = inner_ref[...] + moments(ws, mws, edge)


def strip(strip_in, near, far, inner):
    rows = strip_in.shape[1] - 2 * ROWS
    f32 = jnp.float32
    return pl.pallas_call(
        strip_kernel,
        out_shape=[
            jax.ShapeDtypeStruct((STEPS, rows, LANES), f32),
            jax.ShapeDtypeStruct((STEPS + 1, rows, LANES), f32),
            jax.ShapeDtypeStruct((ROWS, LANES), f32),
        ],
        compiler_params=pltpu.CompilerParams(vmem_limit_bytes=VMEM_BYTES),
        name="strip",
    )(strip_in, far, near, inner)


def power(exponent):
    size = jnp.abs(exponent)
    value = jnp.ones(exponent.shape, jnp.float32)
    for bit in range(7):
        up, down = 2.0 ** (1 << bit), 2.0 ** -(1 << bit)
        factor = jnp.where(exponent < 0, down, up)
        value = value * jnp.where((size >> bit) & 1 == 1, factor, 1.0)
    return value


def exponent_of(size):
    bits = jnp.ceil(jnp.log2(jnp.maximum(size, 2.0**-100)))
    return jnp.clip(bits, -100.0, 100.0).astype(jnp.int32)


def nearest(values):
    return jnp.floor(values + 0.5)


def place_kernel(owner_ref, outer_ref, middle_ref, sent_ref, scale_ref):
    count = owner_ref.shape[0]
    edge = outer_ref.shape[1] // 2
    between = middle_ref.shape[1]
    span = (2 * edge + between) // count
    sent_ref[...] = jnp.zeros(sent_ref.shape, jnp.int16)
    scale_ref[...] = jnp.zeros(scale_ref.shape, jnp.float32)
    for block in range(count):
        row = block * span
        if row < edge:
            ref, row = outer_ref, row
        elif row < edge + between:
            ref, row = middle_ref, row - edge
        else:
            ref, row = outer_ref, row - between
        target = owner_ref[block]

        @pl.when(target >= 0)
        def _(ref=ref, row=row, target=target):
            for half in range(ref.shape[2] // LANES):
                cols = slice(half * LANES, (half + 1) * LANES)
                rows = slice(row, row + span)
                values = jnp.concatenate([ref[0, rows, cols], ref[1, rows, cols]], axis=0)
                bits = exponent_of(jnp.max(jnp.abs(values), axis=0, keepdims=True))
                whole = jnp.clip(nearest(values * power(15 - bits)), -32767.0, 32767.0)
                there = slice(2 * span * half, 2 * span * (half + 1))
                sent_ref[target, there] = whole.astype(jnp.int32).astype(jnp.int16)
                scale_ref[target, half : half + 1] = bits.astype(jnp.float32)


def place(owner, outer, middle, lon_count):
    cols = outer.shape[2]
    rows = outer.shape[1] + middle.shape[1]
    span = rows // owner.shape[0]
    return pl.pallas_call(
        place_kernel,
        in_specs=[pl.BlockSpec(memory_space=pltpu.SMEM)]
        + [pl.BlockSpec(memory_space=pltpu.VMEM)] * 2,
        out_shape=[
            jax.ShapeDtypeStruct((lon_count, cols // LANES * 2 * span + TAIL, LANES), jnp.int16),
            jax.ShapeDtypeStruct((lon_count, ROWS, LANES), jnp.float32),
        ],
        compiler_params=pltpu.CompilerParams(vmem_limit_bytes=VMEM_BYTES),
        cost_estimate=pl.CostEstimate(
            flops=60 * rows * cols, bytes_accessed=12 * rows * cols, transcendentals=0
        ),
        name="place",
    )(owner, outer, middle)


def seal_kernel(sums_ref, other_ref, scale_ref, tail_ref):
    sums = sums_ref[:SUM_ROWS] + other_ref[:SUM_ROWS]
    bits = exponent_of(jnp.abs(sums))
    scaled = sums * power(-bits) * 2.0**14
    high = nearest(scaled)
    low = nearest((scaled - high) * 2.0**15)
    parts = jnp.concatenate([bits.astype(jnp.float32), high, low], axis=0)
    for slot in range(tail_ref.shape[0]):
        tile = jnp.concatenate([parts, scale_ref[slot, : TAIL - 3 * SUM_ROWS]], axis=0)
        tail_ref[slot] = tile.astype(jnp.int32).astype(jnp.int16)


def seal(sums, other, scale):
    return pl.pallas_call(
        seal_kernel,
        out_shape=jax.ShapeDtypeStruct((scale.shape[0], TAIL, LANES), jnp.int16),
        compiler_params=pltpu.CompilerParams(vmem_limit_bytes=VMEM_BYTES),
        name="seal",
    )(sums, other, scale)


def tally_kernel(arrived_ref, sums_ref):
    packed = jnp.zeros((SUM_ROWS, LANES), jnp.float32)
    for slot in range(arrived_ref.shape[0]):
        tail = arrived_ref[slot, arrived_ref.shape[1] - TAIL :].astype(jnp.int32)
        digits = tail.astype(jnp.float32)
        high = digits[SUM_ROWS : 2 * SUM_ROWS]
        low = digits[2 * SUM_ROWS : 3 * SUM_ROWS]
        packed = packed + (high + low * 2.0**-15) * power(tail[:SUM_ROWS] - 14)
    sums_ref[:SUM_ROWS] = packed
    sums_ref[SUM_ROWS:] = jnp.zeros((ROWS - SUM_ROWS, LANES), jnp.float32)


def tally(arrived):
    return pl.pallas_call(
        tally_kernel,
        out_shape=jax.ShapeDtypeStruct((ROWS, LANES), jnp.float32),
        compiler_params=pltpu.CompilerParams(vmem_limit_bytes=VMEM_BYTES),
        name="tally",
    )(arrived)


def combine_kernel(
    sums_ref,
    other_ref,
    arrived_ref,
    w_ref,
    mw_ref,
    w_edge_ref,
    mw_edge_ref,
    pressure_hbm,
    residual_hbm,
    held_hbm,
    pressure_ref,
    residual_ref,
    held_ref,
    held_sem,
    sems,
):
    rows = held_ref.shape[1]
    for slot in range(held_ref.shape[0]):
        tail = arrived_ref[slot, arrived_ref.shape[1] - TAIL :].astype(jnp.int32)
        for half in range(held_ref.shape[2] // LANES):
            at = 3 * SUM_ROWS + half
            scale = power(tail[at : at + 1] - 15)
            whole = arrived_ref[slot, half * rows : (half + 1) * rows].astype(jnp.int32)
            held_ref[slot, :, half * LANES : (half + 1) * LANES] = whole.astype(jnp.float32) * scale
    held_copy = pltpu.make_async_copy(held_ref, held_hbm, held_sem)
    held_copy.start()
    packed = jnp.where(is_even("lat"), other_ref[:SUM_ROWS], sums_ref[:SUM_ROWS])
    quarter = lanes_of(packed.shape) // QUARTER
    totals = [
        jnp.sum(jnp.where(quarter == place, packed, 0.0), axis=1, keepdims=True)
        for place in range(4)
    ]
    entry = lambda place: totals[place % 4][place // 4 : place // 4 + 1, :]
    right = [entry(place) for place in range(STEPS)]
    matrix = {}
    place = STEPS
    for low in range(STEPS):
        for high in range(low, STEPS):
            matrix[low, high] = entry(place)
            place += 1
    for pivot in range(STEPS):
        inverse = 1.0 / matrix[pivot, pivot]
        for row in range(pivot + 1, STEPS):
            factor = matrix[pivot, row] * inverse
            for col in range(row, STEPS):
                matrix[row, col] = matrix[row, col] - factor * matrix[pivot, col]
            right[row] = right[row] - factor * right[pivot]
        matrix[pivot, pivot] = inverse
    for pivot in reversed(range(STEPS)):
        for col in range(pivot + 1, STEPS):
            right[pivot] = right[pivot] - matrix[pivot, col] * right[col]
        right[pivot] = right[pivot] * matrix[pivot, pivot]

    def results(w_ref, mw_ref, part):
        pressure = right[0] * w_ref[0, part]
        residual = mw_ref[0, part] - right[0] * (mw_ref[0, part] - mw_ref[1, part])
        for place in range(1, STEPS):
            pressure = pressure + right[place] * w_ref[place, part]
            image = mw_ref[place, part] - mw_ref[place + 1, part]
            residual = residual - right[place] * image
        return pressure, residual

    rows, cols = pressure_ref.shape
    copies = []
    for piece in range(PIECES):
        part = slice(piece * rows // PIECES, (piece + 1) * rows // PIECES)
        inner = results(w_ref, mw_ref, part)
        edge = results(w_edge_ref, mw_edge_ref, part)
        lane = lanes_of(edge[0].shape)
        for field, (out_ref, out_hbm, inside, border) in enumerate(
            zip((pressure_ref, residual_ref), (pressure_hbm, residual_hbm), inner, edge)
        ):
            out_ref[part, :LANES] = jnp.where(lane < RIM, border, inside[:, :LANES])
            if cols > 2 * LANES:
                out_ref[part, LANES : cols - LANES] = inside[:, LANES : cols - LANES]
            out_ref[part, cols - LANES :] = jnp.where(
                lane >= LANES - RIM, turn(border, -SEAM), inside[:, cols - LANES :]
            )
            there = pl.ds(piece * rows // PIECES, rows // PIECES)
            copy = pltpu.make_async_copy(
                out_ref.at[there], out_hbm.at[there], sems.at[field, piece]
            )
            copy.start()
            copies.append(copy)
    held_copy.wait()
    for copy in copies:
        copy.wait()


def combine(sums, other, arrived, w, mw, w_edge, mw_edge):
    rows, cols = w.shape[1:]
    shape = jax.ShapeDtypeStruct((rows, cols), jnp.float32)
    held = (arrived.shape[0], (arrived.shape[1] - TAIL) * LANES // cols, cols)
    return pl.pallas_call(
        combine_kernel,
        out_shape=[shape, shape, jax.ShapeDtypeStruct(held, jnp.float32)],
        out_specs=[pl.BlockSpec(memory_space=pltpu.HBM)] * 3,
        scratch_shapes=[
            pltpu.VMEM((rows, cols), jnp.float32),
            pltpu.VMEM((rows, cols), jnp.float32),
            pltpu.VMEM(held, jnp.float32),
            pltpu.SemaphoreType.DMA,
            pltpu.SemaphoreType.DMA((2, PIECES)),
        ],
        compiler_params=pltpu.CompilerParams(vmem_limit_bytes=VMEM_BYTES),
        name="combine",
    )(sums, other, arrived, w, mw, w_edge, mw_edge)


def exchange_odd(values, distance):
    pairs = [
        (place, place ^ distance if place % 2 else place) for place in range(lax.axis_size("lat"))
    ]
    return lax.ppermute(values, "lat", pairs)


def swap(values, axis, first):
    count = lax.axis_size(axis)
    pairs = []
    for place in range(first, count, 2):
        beside = (place + 1) % count
        pairs += [(place, beside), (beside, place)]
    return lax.ppermute(values, axis, pairs)


def on_device(tendency, thickness, level_count, block_mask, owner, inertia):
    lat_count = lax.axis_size("lat")
    lon_count = lax.axis_size("lon")
    rows = level_count.shape[0]
    tall = OUTER
    inputs = (tendency, thickness, level_count, inertia)
    outer, outer_side, near, far = integrate(*inputs, ((0, tall), (rows - tall, tall)), True)
    bands = tuple(
        (row, min(CHUNK, rows - tall - row)) for row in range(tall, rows - tall, CHUNK)
    )
    middle, middle_side = integrate(*inputs, bands, False)
    near = swap(near, "lat", 0)
    far = swap(far, "lat", 1)
    near_edge, far_edge = edges(outer_side, middle_side, near, far)
    far_edge = swap(far_edge, "lon", 1)
    near_edge = swap(near_edge, "lon", 0)
    w, mw, strip_in, inner = interior(outer, middle, near, far)
    w_edge, mw_edge, sums = strip(strip_in, near_edge, far_edge, inner)
    sent, scale = place(owner[:, 0], outer, middle, lon_count)
    sums = sums + swap(sums, "lat", 0)
    shift = 2
    while 2 * shift < lat_count:
        sums = sums + exchange_odd(sums, shift)
        shift *= 2
    tail = seal(sums, exchange_odd(sums, shift), scale)
    sent = lax.dynamic_update_slice(sent, tail, (0, sent.shape[1] - TAIL, 0))
    arrived = lax.all_to_all(sent, "lon", split_axis=0, concat_axis=0, tiled=True)
    sums = tally(arrived)
    other = swap(sums, "lat", 0)
    pressure, residual, held = combine(sums, other, arrived, w, mw, w_edge, mw_edge)
    held = held.reshape((1, 1, lon_count, 2, held.shape[1] // 2, held.shape[2]))
    return (held, pressure, residual)


def solution(mesh):
    return jax.shard_map(
        on_device,
        mesh=mesh,
        in_specs=(
            P(None, None, "lat", "lon"),
            P(),
            P("lat", "lon"),
            P("lat", "lon"),
            P("lat", "lon"),
            P("lat", "lon"),
        ),
        out_specs=(P("lat", "lon", None, None, None, None), P("lat", "lon"), P("lat", "lon")),
        check_vma=False,
    )
```

```python
import jax
import jax.numpy as jnp
from jax import lax
from jax.experimental import pallas as pl
from jax.experimental.pallas import tpu as pltpu
from jax.sharding import PartitionSpec as P

STEPS = 4
RIM = STEPS + 1
ROWS = 8
LANES = 128
HALF = LANES // 2
QUARTER = LANES // 4
EAST = 48
SEAM = HALF + EAST
CHUNK = 32
FIELDS = 4
GROUPS = 6
PITCH = LANES // GROUPS
PIECES = 2
OUTER = 16
TAIL = 16
SUM_ROWS = 4
VMEM_BYTES = 16 * 1024 * 1024
WHOLE_BYTES = 56450000


def lanes_of(shape):
    return lax.broadcasted_iota(jnp.int32, shape, len(shape) - 1)


def turn(values, amount):
    amount = amount % values.shape[1]
    return pltpu.roll(values, amount, 1) if amount else values


def sides(near, far):
    place = lax.axis_index("lat")
    even = is_even("lat")
    last = lax.axis_size("lat") - 1
    north = jnp.where(place == 0, 0.0, jnp.where(even, far, near))
    south = jnp.where(place == last, 0.0, jnp.where(even, near, far))
    return north, south


def is_even(axis):
    return lax.rem(lax.axis_index(axis), 2) == 0


def pack_edges(ref, part):
    cols = ref.shape[2]
    packed = None
    for place in range(FIELDS):
        west = ref[place, part, :LANES]
        east = ref[place, part, cols - LANES :]
        if packed is None:
            lane = lanes_of(west.shape)
            packed = jnp.zeros(west.shape, jnp.float32)
        at = place * RIM
        packed = jnp.where((lane >= at) & (lane < at + RIM), turn(west, at), packed)
        at = HALF + place * RIM
        packed = jnp.where((lane >= at) & (lane < at + RIM), turn(east, at + RIM), packed)
    return packed


def integrate_bands(bands, thick_ref, count_ref, tend_ref, waits, finish):
    levels = tend_ref.shape[1]
    for place, (row, size) in enumerate(bands):
        part = slice(row, row + size)
        waits[place]()
        count = count_ref[part]
        first = jnp.zeros(count.shape, jnp.float32)
        second = jnp.zeros(count.shape, jnp.float32)
        depth = jnp.zeros(count.shape, jnp.float32)
        for level in range(levels):
            layer = jnp.where(count > level, thick_ref[level], 0.0)
            depth = depth + layer
            first = first + layer * tend_ref[0, level, part].astype(jnp.float32)
            second = second + layer * tend_ref[1, level, part].astype(jnp.float32)
        finish(place, part, (first, second, depth))


def outer_kernel(
    thick_hbm,
    count_hbm,
    inertia_hbm,
    tend_hbm,
    near_ref,
    far_ref,
    thick_ref,
    count_ref,
    tend_ref,
    thick_sem,
    sems,
):
    rows = count_hbm.shape[0]
    even = is_even("lat")
    starts = (0, rows - OUTER)
    bands = [(place * OUTER, OUTER) for place in range(2)]

    def pair(source, target, place, kind):
        there = pl.ds(starts[place], OUTER)
        here = pl.ds(place * OUTER, OUTER)
        if kind == 0:
            return pltpu.make_async_copy(
                source.at[:, :, there], target.at[:, :, here], sems.at[kind, place]
            )
        return pltpu.make_async_copy(source.at[there], target.at[here], sems.at[kind, place])

    tends = [pair(tend_hbm, tend_ref, place, 0) for place in range(2)]
    counts = [pair(count_hbm, count_ref, place, 1) for place in range(2)]
    thick = pltpu.make_async_copy(thick_hbm, thick_ref, thick_sem)
    last = rows - ROWS
    near_row = pl.multiple_of(jnp.where(even, last, 0), ROWS)
    far_row = pl.multiple_of(jnp.where(even, 0, last), ROWS)
    inertias = [
        pltpu.make_async_copy(
            inertia_hbm.at[pl.ds(row, ROWS)], ref.at[FIELDS - 1], sems.at[2, place]
        )
        for place, (row, ref) in enumerate(((near_row, near_ref), (far_row, far_ref)))
    ]
    for copy in (tends[0], counts[0], thick, tends[1], counts[1], inertias[0], inertias[1]):
        copy.start()
    thick.wait()
    results = []

    def wait(place):
        def run():
            counts[place].wait()
            tends[place].wait()

        return run

    integrate_bands(
        bands,
        thick_ref,
        count_ref,
        tend_ref,
        [wait(place) for place in range(2)],
        lambda place, part, values: results.append(values),
    )
    for field in range(FIELDS - 1):
        head = results[0][field][:ROWS]
        tail = results[1][field][-ROWS:]
        near_ref[field] = jnp.where(even, tail, head)
        far_ref[field] = jnp.where(even, head, tail)
    for copy in inertias:
        copy.wait()


def whole_kernel(
    thick_hbm,
    count_hbm,
    inertia_hbm,
    tend_hbm,
    fields_ref,
    side_ref,
    thick_ref,
    count_ref,
    tend_ref,
    sems,
    band_sems,
):
    rows = count_hbm.shape[0]
    bands = [(row, CHUNK) for row in range(0, rows, CHUNK)]
    tends = []
    for place, (row, size) in enumerate(bands):
        part = pl.ds(row, size)
        tends.append(
            pltpu.make_async_copy(
                tend_hbm.at[:, :, part], tend_ref.at[:, :, part], band_sems.at[place]
            )
        )
    count = pltpu.make_async_copy(count_hbm, count_ref, sems.at[0])
    thick = pltpu.make_async_copy(thick_hbm, thick_ref, sems.at[1])
    inertia = pltpu.make_async_copy(inertia_hbm, fields_ref.at[FIELDS - 1], sems.at[2])
    for copy in [tends[0], count, thick, inertia] + tends[1:]:
        copy.start()
    for copy in (count, thick, inertia):
        copy.wait()

    def finish(place, part, values):
        for field in range(FIELDS - 1):
            fields_ref[field, part] = values[field]
        side_ref[part] = pack_edges(fields_ref, part)

    integrate_bands(
        bands, thick_ref, count_ref, tend_ref, [copy.wait for copy in tends], finish
    )


def integrate_cost(tendency, rows):
    components, levels, _, cols = tendency.shape
    return pl.CostEstimate(
        flops=6 * components * levels * rows * cols,
        bytes_accessed=2 * components * levels * rows * cols,
        transcendentals=0,
    )


def integrate_outer(tendency, thickness, level_count, inertia):
    components, levels, _, cols = tendency.shape
    f32 = jnp.float32
    return pl.pallas_call(
        outer_kernel,
        in_specs=[pl.BlockSpec(memory_space=pltpu.HBM)] * 4,
        out_shape=[jax.ShapeDtypeStruct((FIELDS, ROWS, cols), f32)] * 2,
        scratch_shapes=[
            pltpu.SMEM(thickness.shape, f32),
            pltpu.VMEM((2 * OUTER, cols), jnp.int32),
            pltpu.VMEM((components, levels, 2 * OUTER, cols), tendency.dtype),
            pltpu.SemaphoreType.DMA,
            pltpu.SemaphoreType.DMA((3, 2)),
        ],
        cost_estimate=integrate_cost(tendency, 2 * OUTER),
        name="outer",
    )(thickness, level_count, inertia, tendency)


def integrate(tendency, thickness, level_count, inertia):
    rows, cols = level_count.shape
    f32 = jnp.float32
    return pl.pallas_call(
        whole_kernel,
        in_specs=[pl.BlockSpec(memory_space=pltpu.HBM)] * 4,
        out_shape=[
            jax.ShapeDtypeStruct((FIELDS, rows, cols), f32),
            jax.ShapeDtypeStruct((rows, LANES), f32),
        ],
        scratch_shapes=[
            pltpu.SMEM(thickness.shape, f32),
            pltpu.VMEM((rows, cols), jnp.int32),
            pltpu.VMEM(tendency.shape, tendency.dtype),
            pltpu.SemaphoreType.DMA((3,)),
            pltpu.SemaphoreType.DMA((rows // CHUNK,)),
        ],
        cost_estimate=integrate_cost(tendency, rows),
        compiler_params=pltpu.CompilerParams(vmem_limit_bytes=WHOLE_BYTES),
        name="whole",
    )(thickness, level_count, inertia, tendency)


def edges_kernel(side_ref, near_ref, far_ref, near_out_ref, far_out_ref):
    even_lon = is_even("lon")
    near = pack_edges(near_ref, slice(None))
    far = pack_edges(far_ref, slice(None))
    north, south = sides(near, far)
    packed = jnp.concatenate([north, side_ref[...], south], axis=0)
    size = near_out_ref.shape[0]
    lane = lanes_of(near_out_ref.shape)
    west = jnp.zeros(near_out_ref.shape, jnp.float32)
    east = jnp.zeros(near_out_ref.shape, jnp.float32)
    for group in range(GROUPS):
        rows = packed[group * size : (group + 1) * size]
        at = group * PITCH
        here = (lane >= at) & (lane < at + PITCH)
        west = jnp.where(here, turn(rows, at), west)
        east = jnp.where(here, turn(rows, at - HALF), east)
    near_out_ref[...] = jnp.where(even_lon, east, west)
    far_out_ref[...] = jnp.where(even_lon, west, east)


def edges(side, near, far):
    rows = side.shape[0] + 2 * ROWS
    message = jax.ShapeDtypeStruct((rows // GROUPS, LANES), jnp.float32)
    return pl.pallas_call(
        edges_kernel,
        out_shape=[message, message],
        compiler_params=pltpu.CompilerParams(vmem_limit_bytes=VMEM_BYTES),
        name="edges",
    )(side, near, far)


def smooth(field):
    rows, cols = field.shape
    tall = field + 0.5 * (pltpu.roll(field, 1, 0) + pltpu.roll(field, rows - 1, 0))
    return tall + 0.5 * (pltpu.roll(tall, 1, 1) + pltpu.roll(tall, cols - 1, 1))


def basis(first, second, depth, inertia):
    tall, wide = first.shape
    own = slice(ROWS, tall - ROWS)
    inside = inertia > 0.0
    east_west = pltpu.roll(first, wide - 1, 1) - pltpu.roll(first, 1, 1)
    north_south = pltpu.roll(second, tall - 1, 0) - pltpu.roll(second, 1, 0)
    scaled = jnp.where(depth > 0.0, 0.5 * (east_west + north_south), 0.0)
    diag = inertia + 2.0 * depth + smooth(depth)
    inverse = jnp.where(inside, 1.0 / jnp.where(inside, diag, 1.0), 0.0)
    mws = [scaled[own]]
    ws = []
    vector = scaled * inverse
    for step in range(STEPS):
        ws.append(vector[own])
        weighed = depth * vector
        scaled = depth * smooth(vector) + smooth(weighed) - 2.0 * weighed
        mws.append(scaled[own])
        if step + 1 < STEPS:
            vector = scaled * inverse
    return ws, mws


def moments(ws, mws, mask):
    ws = [jnp.where(mask, values, 0.0) for values in ws]
    images = [mws[place] - mws[place + 1] for place in range(STEPS)]
    pairs = [ws[place] * mws[0] for place in range(STEPS)]
    for low in range(STEPS):
        for high in range(low, STEPS):
            pairs.append(ws[low] * images[high])
    lines = []
    for product in pairs:
        line = jnp.sum(product, axis=0, keepdims=True)
        total = line[:, :LANES]
        for start in range(LANES, line.shape[1], LANES):
            total = total + line[:, start : start + LANES]
        total = total + turn(total, HALF)
        lines.append(total + turn(total, QUARTER))
    quarter = lanes_of((1, LANES)) // QUARTER
    packed = []
    for start in range(0, len(lines), 4):
        row = jnp.zeros((1, LANES), jnp.float32)
        for place, line in enumerate(lines[start : start + 4]):
            row = jnp.where(quarter == place, line, row)
        packed.append(row)
    packed.append(jnp.zeros((ROWS - len(packed), LANES), jnp.float32))
    return jnp.concatenate(packed, axis=0)


def interior_kernel(
    fields_ref,
    near_ref,
    far_ref,
    w_ref,
    mw_ref,
    strip_ref,
    sums_ref,
    forcing_ref,
):
    forcing_ref[...] = fields_ref[:2]
    cols = fields_ref.shape[2]
    lane = lanes_of((strip_ref.shape[1], LANES))
    padded = []
    for place in range(FIELDS):
        north, south = sides(near_ref[place], far_ref[place])
        values = jnp.concatenate([north, fields_ref[place], south], axis=0)
        east = turn(values[:, cols - LANES :], SEAM)
        strip_ref[place] = jnp.where(lane < HALF, values[:, :LANES], east)
        padded.append(values)
    ws, mws = basis(*padded)
    for place, values in enumerate(ws):
        w_ref[place] = values
    for place, values in enumerate(mws):
        mw_ref[place] = values
    lane = lanes_of(ws[0].shape)
    sums_ref[...] = moments(ws, mws, (lane >= RIM) & (lane < cols - RIM))


def interior(fields, near, far):
    _, rows, cols = fields.shape
    f32 = jnp.float32
    return pl.pallas_call(
        interior_kernel,
        out_shape=[
            jax.ShapeDtypeStruct((STEPS, rows, cols), f32),
            jax.ShapeDtypeStruct((STEPS + 1, rows, cols), f32),
            jax.ShapeDtypeStruct((FIELDS, rows + 2 * ROWS, LANES), f32),
            jax.ShapeDtypeStruct((ROWS, LANES), f32),
            jax.ShapeDtypeStruct((2, rows, cols), f32),
        ],
        compiler_params=pltpu.CompilerParams(vmem_limit_bytes=VMEM_BYTES),
        cost_estimate=pl.CostEstimate(
            flops=300 * rows * cols, bytes_accessed=64 * rows * cols, transcendentals=0
        ),
        name="interior",
    )(fields, near, far)


def strip_kernel(strip_in_ref, far_ref, near_ref, inner_ref, w_ref, mw_ref, sums_ref):
    even = is_even("lon")
    near = near_ref[...]
    far = far_ref[...]
    from_east = jnp.where(even, near, far)
    from_west = jnp.where(even, far, near)
    lane = lanes_of(near.shape)
    padded = []
    for place in range(FIELDS):
        halo = []
        for group in range(GROUPS):
            at = group * PITCH + place * RIM
            east = turn(from_east, SEAM - at)
            west = turn(from_west, LANES - RIM - at)
            west = jnp.where(lane >= LANES - RIM, west, 0.0)
            halo.append(jnp.where(lane < SEAM + RIM, east, west))
        halo = jnp.concatenate(halo, axis=0)
        padded.append(jnp.where(lanes_of(halo.shape) < SEAM, strip_in_ref[place], halo))
    ws, mws = basis(*padded)
    for place, values in enumerate(ws):
        w_ref[place] = values
    for place, values in enumerate(mws):
        mw_ref[place] = values
    lane = lanes_of(ws[0].shape)
    edge = (lane < RIM) | ((lane >= SEAM - RIM) & (lane < SEAM))
    sums_ref[...] = inner_ref[...] + moments(ws, mws, edge)


def strip(strip_in, near, far, inner):
    rows = strip_in.shape[1] - 2 * ROWS
    f32 = jnp.float32
    return pl.pallas_call(
        strip_kernel,
        out_shape=[
            jax.ShapeDtypeStruct((STEPS, rows, LANES), f32),
            jax.ShapeDtypeStruct((STEPS + 1, rows, LANES), f32),
            jax.ShapeDtypeStruct((ROWS, LANES), f32),
        ],
        compiler_params=pltpu.CompilerParams(vmem_limit_bytes=VMEM_BYTES),
        name="strip",
    )(strip_in, far, near, inner)


def power(exponent):
    size = jnp.abs(exponent)
    value = jnp.ones(exponent.shape, jnp.float32)
    for bit in range(7):
        up, down = 2.0 ** (1 << bit), 2.0 ** -(1 << bit)
        factor = jnp.where(exponent < 0, down, up)
        value = value * jnp.where((size >> bit) & 1 == 1, factor, 1.0)
    return value


def exponent_of(size):
    bits = jnp.ceil(jnp.log2(jnp.maximum(size, 2.0**-100)))
    return jnp.clip(bits, -100.0, 100.0).astype(jnp.int32)


def nearest(values):
    return jnp.floor(values + 0.5)


def place_kernel(owner_ref, fields_ref, sent_ref, scale_ref):
    count = owner_ref.shape[0]
    span = fields_ref.shape[1] // count
    sent_ref[...] = jnp.zeros(sent_ref.shape, jnp.int16)
    scale_ref[...] = jnp.zeros(scale_ref.shape, jnp.float32)
    for block in range(count):
        target = owner_ref[block]

        @pl.when(target >= 0)
        def _(block=block, target=target):
            rows = slice(block * span, (block + 1) * span)
            for half in range(fields_ref.shape[2] // LANES):
                cols = slice(half * LANES, (half + 1) * LANES)
                pieces = [fields_ref[0, rows, cols], fields_ref[1, rows, cols]]
                values = jnp.concatenate(pieces, axis=0)
                bits = exponent_of(jnp.max(jnp.abs(values), axis=0, keepdims=True))
                whole = jnp.clip(nearest(values * power(15 - bits)), -32767.0, 32767.0)
                there = slice(2 * span * half, 2 * span * (half + 1))
                sent_ref[target, there] = whole.astype(jnp.int32).astype(jnp.int16)
                scale_ref[target, half : half + 1] = bits.astype(jnp.float32)


def place(owner, fields, lon_count):
    _, rows, cols = fields.shape
    span = rows // owner.shape[0]
    return pl.pallas_call(
        place_kernel,
        in_specs=[
            pl.BlockSpec(memory_space=pltpu.SMEM),
            pl.BlockSpec(memory_space=pltpu.VMEM),
        ],
        out_shape=[
            jax.ShapeDtypeStruct((lon_count, cols // LANES * 2 * span + TAIL, LANES), jnp.int16),
            jax.ShapeDtypeStruct((lon_count, ROWS, LANES), jnp.float32),
        ],
        compiler_params=pltpu.CompilerParams(vmem_limit_bytes=VMEM_BYTES),
        cost_estimate=pl.CostEstimate(
            flops=60 * rows * cols, bytes_accessed=12 * rows * cols, transcendentals=0
        ),
        name="place",
    )(owner, fields)


def seal_kernel(sums_ref, other_ref, scale_ref, tail_ref):
    sums = sums_ref[:SUM_ROWS] + other_ref[:SUM_ROWS]
    bits = exponent_of(jnp.abs(sums))
    scaled = sums * power(-bits) * 2.0**14
    high = nearest(scaled)
    low = nearest((scaled - high) * 2.0**15)
    parts = jnp.concatenate([bits.astype(jnp.float32), high, low], axis=0)
    for slot in range(tail_ref.shape[0]):
        tile = jnp.concatenate([parts, scale_ref[slot, : TAIL - 3 * SUM_ROWS]], axis=0)
        tail_ref[slot] = tile.astype(jnp.int32).astype(jnp.int16)


def seal(sums, other, scale):
    return pl.pallas_call(
        seal_kernel,
        out_shape=jax.ShapeDtypeStruct((scale.shape[0], TAIL, LANES), jnp.int16),
        compiler_params=pltpu.CompilerParams(vmem_limit_bytes=VMEM_BYTES),
        name="seal",
    )(sums, other, scale)


def combine_kernel(
    arrived_ref,
    w_ref,
    mw_ref,
    w_edge_ref,
    mw_edge_ref,
    pressure_hbm,
    residual_hbm,
    held_hbm,
    pressure_ref,
    residual_ref,
    held_ref,
    held_sem,
    sems,
):
    rows = held_ref.shape[1]
    slots = held_ref.shape[0]
    tails = []
    for slot in range(slots):
        tails.append(arrived_ref[slot, arrived_ref.shape[1] - TAIL :].astype(jnp.int32))
    scales = jnp.concatenate([tail[3 * SUM_ROWS :] for tail in tails], axis=0)
    scales = power(scales - 15)
    exponents = jnp.concatenate([tail[:SUM_ROWS] for tail in tails], axis=0)
    high = jnp.concatenate([tail[SUM_ROWS : 2 * SUM_ROWS] for tail in tails], axis=0)
    low = jnp.concatenate([tail[2 * SUM_ROWS : 3 * SUM_ROWS] for tail in tails], axis=0)
    digits = high.astype(jnp.float32) + low.astype(jnp.float32) * 2.0**-15
    sums = digits * power(exponents - 14)
    packed = sums[:SUM_ROWS]
    for slot in range(1, slots):
        packed = packed + sums[slot * SUM_ROWS : (slot + 1) * SUM_ROWS]
    spare = TAIL - 3 * SUM_ROWS
    for slot in range(slots):
        for half in range(held_ref.shape[2] // LANES):
            at = slot * spare + half
            whole = arrived_ref[slot, half * rows : (half + 1) * rows].astype(jnp.int32)
            whole = whole.astype(jnp.float32) * scales[at : at + 1]
            held_ref[slot, :, half * LANES : (half + 1) * LANES] = whole
    held_copy = pltpu.make_async_copy(held_ref, held_hbm, held_sem)
    held_copy.start()
    quarter = lanes_of(packed.shape) // QUARTER
    totals = [
        jnp.sum(jnp.where(quarter == place, packed, 0.0), axis=1, keepdims=True)
        for place in range(4)
    ]
    entry = lambda place: totals[place % 4][place // 4 : place // 4 + 1, :]
    right = [entry(place) for place in range(STEPS)]
    matrix = {}
    place = STEPS
    for low in range(STEPS):
        for high in range(low, STEPS):
            matrix[low, high] = entry(place)
            place += 1
    for pivot in range(STEPS):
        inverse = 1.0 / matrix[pivot, pivot]
        for row in range(pivot + 1, STEPS):
            factor = matrix[pivot, row] * inverse
            for col in range(row, STEPS):
                matrix[row, col] = matrix[row, col] - factor * matrix[pivot, col]
            right[row] = right[row] - factor * right[pivot]
        matrix[pivot, pivot] = inverse
    for pivot in reversed(range(STEPS)):
        for col in range(pivot + 1, STEPS):
            right[pivot] = right[pivot] - matrix[pivot, col] * right[col]
        right[pivot] = right[pivot] * matrix[pivot, pivot]

    def results(w_ref, mw_ref, part):
        pressure = right[0] * w_ref[0, part]
        residual = mw_ref[0, part] - right[0] * (mw_ref[0, part] - mw_ref[1, part])
        for place in range(1, STEPS):
            pressure = pressure + right[place] * w_ref[place, part]
            image = mw_ref[place, part] - mw_ref[place + 1, part]
            residual = residual - right[place] * image
        return pressure, residual

    rows, cols = pressure_ref.shape
    copies = []
    for piece in range(PIECES):
        part = slice(piece * rows // PIECES, (piece + 1) * rows // PIECES)
        inner = results(w_ref, mw_ref, part)
        edge = results(w_edge_ref, mw_edge_ref, part)
        lane = lanes_of(edge[0].shape)
        for field, (out_ref, out_hbm, inside, border) in enumerate(
            zip((pressure_ref, residual_ref), (pressure_hbm, residual_hbm), inner, edge)
        ):
            out_ref[part, :LANES] = jnp.where(lane < RIM, border, inside[:, :LANES])
            if cols > 2 * LANES:
                out_ref[part, LANES : cols - LANES] = inside[:, LANES : cols - LANES]
            out_ref[part, cols - LANES :] = jnp.where(
                lane >= LANES - RIM, turn(border, -SEAM), inside[:, cols - LANES :]
            )
            there = pl.ds(piece * rows // PIECES, rows // PIECES)
            copy = pltpu.make_async_copy(
                out_ref.at[there], out_hbm.at[there], sems.at[field, piece]
            )
            copy.start()
            copies.append(copy)
    held_copy.wait()
    for copy in copies:
        copy.wait()


def combine(arrived, w, mw, w_edge, mw_edge):
    rows, cols = w.shape[1:]
    shape = jax.ShapeDtypeStruct((rows, cols), jnp.float32)
    held = (arrived.shape[0], (arrived.shape[1] - TAIL) * LANES // cols, cols)
    return pl.pallas_call(
        combine_kernel,
        out_shape=[shape, shape, jax.ShapeDtypeStruct(held, jnp.float32)],
        out_specs=[pl.BlockSpec(memory_space=pltpu.HBM)] * 3,
        scratch_shapes=[
            pltpu.VMEM((rows, cols), jnp.float32),
            pltpu.VMEM((rows, cols), jnp.float32),
            pltpu.VMEM(held, jnp.float32),
            pltpu.SemaphoreType.DMA,
            pltpu.SemaphoreType.DMA((2, PIECES)),
        ],
        compiler_params=pltpu.CompilerParams(vmem_limit_bytes=VMEM_BYTES),
        name="combine",
    )(arrived, w, mw, w_edge, mw_edge)


def exchange(values, axis, distance):
    pairs = [(place, place ^ distance) for place in range(lax.axis_size(axis))]
    return lax.ppermute(values, axis, pairs)


def swap(values, axis, first):
    count = lax.axis_size(axis)
    pairs = []
    for place in range(first, count, 2):
        beside = (place + 1) % count
        pairs += [(place, beside), (beside, place)]
    return lax.ppermute(values, axis, pairs)


def on_device(tendency, thickness, level_count, block_mask, owner, inertia):
    lat_count = lax.axis_size("lat")
    lon_count = lax.axis_size("lon")
    inputs = (tendency, thickness, level_count, inertia)
    near, far = integrate_outer(*inputs)
    fields, side = integrate(*inputs)
    near = swap(near, "lat", 0)
    far = swap(far, "lat", 1)
    near_edge, far_edge = edges(side, near, far)
    far_edge = swap(far_edge, "lon", 1)
    near_edge = swap(near_edge, "lon", 0)
    w, mw, strip_in, inner, forcing = interior(fields, near, far)
    w_edge, mw_edge, sums = strip(strip_in, near_edge, far_edge, inner)
    sent, scale = place(owner[:, 0], forcing, lon_count)
    shift = 1
    while 2 * shift < lat_count:
        sums = sums + exchange(sums, "lat", shift)
        shift *= 2
    tail = seal(sums, exchange(sums, "lat", shift), scale)
    sent = lax.dynamic_update_slice(sent, tail, (0, sent.shape[1] - TAIL, 0))
    arrived = lax.all_to_all(sent, "lon", split_axis=0, concat_axis=0, tiled=True)
    pressure, residual, held = combine(arrived, w, mw, w_edge, mw_edge)
    held = held.reshape((1, 1, lon_count, 2, held.shape[1] // 2, held.shape[2]))
    return (held, pressure, residual)


def solution(mesh):
    return jax.shard_map(
        on_device,
        mesh=mesh,
        in_specs=(
            P(None, None, "lat", "lon"),
            P(),
            P("lat", "lon"),
            P("lat", "lon"),
            P("lat", "lon"),
            P("lat", "lon"),
        ),
        out_specs=(P("lat", "lon", None, None, None, None), P("lat", "lon"), P("lat", "lon")),
        check_vma=False,
    )
```

```python
import functools

import jax
import jax.numpy as jnp
from jax import lax
from jax.experimental import pallas as pl
from jax.experimental.pallas import tpu as pltpu
from jax.sharding import PartitionSpec as P

STEPS = 4
RIM = STEPS + 1
ROWS = 8
LANES = 128
HALF = LANES // 2
QUARTER = LANES // 4
FOLD = 4
PITCH = LANES // FOLD
CHUNK = 32
FIELDS = 4
PIECES = 2
OUTER = 16
TAIL = 16
SUM_ROWS = 4
VMEM_BYTES = 16 * 1024 * 1024
WHOLE_BYTES = 56450000


def lanes_of(shape):
    return lax.broadcasted_iota(jnp.int32, shape, len(shape) - 1)


def turn(values, amount):
    amount = amount % values.shape[1]
    return pltpu.roll(values, amount, 1) if amount else values


def sides(near, far):
    place = lax.axis_index("lat")
    even = is_even("lat")
    last = lax.axis_size("lat") - 1
    north = jnp.where(place == 0, 0.0, jnp.where(even, far, near))
    south = jnp.where(place == last, 0.0, jnp.where(even, near, far))
    return north, south


def is_even(axis):
    return lax.rem(lax.axis_index(axis), 2) == 0


def pack_edges(ref, part):
    cols = ref.shape[2]
    packed = None
    for place in range(FIELDS):
        west = ref[place, part, :LANES]
        east = ref[place, part, cols - LANES :]
        if packed is None:
            lane = lanes_of(west.shape)
            packed = jnp.zeros(west.shape, jnp.float32)
        at = place * RIM
        packed = jnp.where((lane >= at) & (lane < at + RIM), turn(west, at), packed)
        at = HALF + place * RIM
        packed = jnp.where((lane >= at) & (lane < at + RIM), turn(east, at + RIM), packed)
    return packed


def integrate_bands(bands, thick_ref, count_ref, tend_ref, waits, finish):
    levels = tend_ref.shape[1]
    for place, (row, size) in enumerate(bands):
        part = slice(row, row + size)
        waits[place]()
        count = count_ref[part]
        first = jnp.zeros(count.shape, jnp.float32)
        second = jnp.zeros(count.shape, jnp.float32)
        depth = jnp.zeros(count.shape, jnp.float32)
        for level in range(levels):
            layer = jnp.where(count > level, thick_ref[level], 0.0)
            depth = depth + layer
            first = first + layer * tend_ref[0, level, part].astype(jnp.float32)
            second = second + layer * tend_ref[1, level, part].astype(jnp.float32)
        finish(place, part, (first, second, depth))


def outer_kernel(
    thick_hbm,
    count_hbm,
    inertia_hbm,
    tend_hbm,
    near_ref,
    far_ref,
    thick_ref,
    count_ref,
    tend_ref,
    thick_sem,
    sems,
):
    rows = count_hbm.shape[0]
    even = is_even("lat")
    starts = (0, rows - OUTER)
    bands = [(place * OUTER, OUTER) for place in range(2)]

    def pair(source, target, place, kind):
        there = pl.ds(starts[place], OUTER)
        here = pl.ds(place * OUTER, OUTER)
        if kind == 0:
            return pltpu.make_async_copy(
                source.at[:, :, there], target.at[:, :, here], sems.at[kind, place]
            )
        return pltpu.make_async_copy(source.at[there], target.at[here], sems.at[kind, place])

    tends = [pair(tend_hbm, tend_ref, place, 0) for place in range(2)]
    counts = [pair(count_hbm, count_ref, place, 1) for place in range(2)]
    thick = pltpu.make_async_copy(thick_hbm, thick_ref, thick_sem)
    last = rows - ROWS
    near_row = pl.multiple_of(jnp.where(even, last, 0), ROWS)
    far_row = pl.multiple_of(jnp.where(even, 0, last), ROWS)
    inertias = [
        pltpu.make_async_copy(
            inertia_hbm.at[pl.ds(row, ROWS)], ref.at[FIELDS - 1], sems.at[2, place]
        )
        for place, (row, ref) in enumerate(((near_row, near_ref), (far_row, far_ref)))
    ]
    for copy in (tends[0], counts[0], thick, tends[1], counts[1], inertias[0], inertias[1]):
        copy.start()
    thick.wait()
    results = []

    def wait(place):
        def run():
            counts[place].wait()
            tends[place].wait()

        return run

    integrate_bands(
        bands,
        thick_ref,
        count_ref,
        tend_ref,
        [wait(place) for place in range(2)],
        lambda place, part, values: results.append(values),
    )
    for field in range(FIELDS - 1):
        head = results[0][field][:ROWS]
        tail = results[1][field][-ROWS:]
        near_ref[field] = jnp.where(even, tail, head)
        far_ref[field] = jnp.where(even, head, tail)
    for copy in inertias:
        copy.wait()


def whole_kernel(
    thick_hbm,
    count_hbm,
    inertia_hbm,
    tend_hbm,
    fields_ref,
    side_ref,
    thick_ref,
    count_ref,
    tend_ref,
    sems,
    band_sems,
):
    rows = count_hbm.shape[0]
    bands = [(row, CHUNK) for row in range(0, rows, CHUNK)]
    tends = []
    for place, (row, size) in enumerate(bands):
        part = pl.ds(row, size)
        tends.append(
            pltpu.make_async_copy(
                tend_hbm.at[:, :, part], tend_ref.at[:, :, part], band_sems.at[place]
            )
        )
    count = pltpu.make_async_copy(count_hbm, count_ref, sems.at[0])
    thick = pltpu.make_async_copy(thick_hbm, thick_ref, sems.at[1])
    inertia = pltpu.make_async_copy(inertia_hbm, fields_ref.at[FIELDS - 1], sems.at[2])
    for copy in [tends[0], count, thick, inertia] + tends[1:]:
        copy.start()
    for copy in (count, thick, inertia):
        copy.wait()

    def finish(place, part, values):
        for field in range(FIELDS - 1):
            fields_ref[field, part] = values[field]
        side_ref[part] = pack_edges(fields_ref, part)

    integrate_bands(
        bands, thick_ref, count_ref, tend_ref, [copy.wait for copy in tends], finish
    )


def integrate_cost(tendency, rows):
    components, levels, _, cols = tendency.shape
    return pl.CostEstimate(
        flops=6 * components * levels * rows * cols,
        bytes_accessed=2 * components * levels * rows * cols,
        transcendentals=0,
    )


def integrate_outer(tendency, thickness, level_count, inertia):
    components, levels, _, cols = tendency.shape
    f32 = jnp.float32
    return pl.pallas_call(
        outer_kernel,
        in_specs=[pl.BlockSpec(memory_space=pltpu.HBM)] * 4,
        out_shape=[jax.ShapeDtypeStruct((FIELDS, ROWS, cols), f32)] * 2,
        scratch_shapes=[
            pltpu.SMEM(thickness.shape, f32),
            pltpu.VMEM((2 * OUTER, cols), jnp.int32),
            pltpu.VMEM((components, levels, 2 * OUTER, cols), tendency.dtype),
            pltpu.SemaphoreType.DMA,
            pltpu.SemaphoreType.DMA((3, 2)),
        ],
        cost_estimate=integrate_cost(tendency, 2 * OUTER),
        name="outer",
    )(thickness, level_count, inertia, tendency)


def integrate(tendency, thickness, level_count, inertia):
    rows, cols = level_count.shape
    f32 = jnp.float32
    return pl.pallas_call(
        whole_kernel,
        in_specs=[pl.BlockSpec(memory_space=pltpu.HBM)] * 4,
        out_shape=[
            jax.ShapeDtypeStruct((FIELDS, rows, cols), f32),
            jax.ShapeDtypeStruct((rows, LANES), f32),
        ],
        scratch_shapes=[
            pltpu.SMEM(thickness.shape, f32),
            pltpu.VMEM((rows, cols), jnp.int32),
            pltpu.VMEM(tendency.shape, tendency.dtype),
            pltpu.SemaphoreType.DMA((3,)),
            pltpu.SemaphoreType.DMA((rows // CHUNK,)),
        ],
        cost_estimate=integrate_cost(tendency, rows),
        compiler_params=pltpu.CompilerParams(vmem_limit_bytes=WHOLE_BYTES),
        name="whole",
    )(thickness, level_count, inertia, tendency)


def folded_rows(tall):
    return (tall - 2 * ROWS) // FOLD + 2 * ROWS


def fold(values, shift, first, last):
    size = folded_rows(values.shape[0])
    lane = lanes_of((size, LANES))
    folded = jnp.zeros((size, LANES), jnp.float32)
    for part in range(FOLD):
        start = part * (size - 2 * ROWS)
        rows = turn(values[start : start + size], part * PITCH + shift)
        here = (lane >= part * PITCH + first) & (lane < part * PITCH + last)
        folded = jnp.where(here, rows, folded)
    return folded


def edges_kernel(side_ref, near_ref, far_ref, near_out_ref, far_out_ref):
    even_lon = is_even("lon")
    near = pack_edges(near_ref, slice(None))
    far = pack_edges(far_ref, slice(None))
    north, south = sides(near, far)
    packed = jnp.concatenate([north, side_ref[...], south], axis=0)
    west = fold(packed, 0, 0, PITCH)
    east = fold(packed, -HALF, 0, PITCH)
    near_out_ref[...] = jnp.where(even_lon, east, west)
    far_out_ref[...] = jnp.where(even_lon, west, east)


def edges(side, near, far):
    rows = side.shape[0] + 2 * ROWS
    message = jax.ShapeDtypeStruct((folded_rows(rows), LANES), jnp.float32)
    return pl.pallas_call(
        edges_kernel,
        out_shape=[message, message],
        compiler_params=pltpu.CompilerParams(vmem_limit_bytes=VMEM_BYTES),
        name="edges",
    )(side, near, far)


def smooth(field):
    rows, cols = field.shape
    tall = field + 0.5 * (pltpu.roll(field, 1, 0) + pltpu.roll(field, rows - 1, 0))
    return tall + 0.5 * (pltpu.roll(tall, 1, 1) + pltpu.roll(tall, cols - 1, 1))


def basis(first, second, depth, inertia):
    tall, wide = first.shape
    own = slice(ROWS, tall - ROWS)
    inside = inertia > 0.0
    east_west = pltpu.roll(first, wide - 1, 1) - pltpu.roll(first, 1, 1)
    north_south = pltpu.roll(second, tall - 1, 0) - pltpu.roll(second, 1, 0)
    scaled = jnp.where(depth > 0.0, 0.5 * (east_west + north_south), 0.0)
    diag = inertia + 2.0 * depth + smooth(depth)
    inverse = jnp.where(inside, 1.0 / jnp.where(inside, diag, 1.0), 0.0)
    mws = [scaled[own]]
    ws = []
    vector = scaled * inverse
    for step in range(STEPS):
        ws.append(vector[own])
        weighed = depth * vector
        scaled = depth * smooth(vector) + smooth(weighed) - 2.0 * weighed
        mws.append(scaled[own])
        if step + 1 < STEPS:
            vector = scaled * inverse
    return ws, mws


def moments(ws, mws, mask):
    ws = [jnp.where(mask, values, 0.0) for values in ws]
    images = [mws[place] - mws[place + 1] for place in range(STEPS)]
    pairs = [ws[place] * mws[0] for place in range(STEPS)]
    for low in range(STEPS):
        for high in range(low, STEPS):
            pairs.append(ws[low] * images[high])
    lines = []
    for product in pairs:
        line = jnp.sum(product, axis=0, keepdims=True)
        total = line[:, :LANES]
        for start in range(LANES, line.shape[1], LANES):
            total = total + line[:, start : start + LANES]
        total = total + turn(total, HALF)
        lines.append(total + turn(total, QUARTER))
    quarter = lanes_of((1, LANES)) // QUARTER
    packed = []
    for start in range(0, len(lines), 4):
        row = jnp.zeros((1, LANES), jnp.float32)
        for place, line in enumerate(lines[start : start + 4]):
            row = jnp.where(quarter == place, line, row)
        packed.append(row)
    packed.append(jnp.zeros((ROWS - len(packed), LANES), jnp.float32))
    return jnp.concatenate(packed, axis=0)


def interior_kernel(
    fields_ref,
    near_ref,
    far_ref,
    w_ref,
    mw_ref,
    near_strip_ref,
    far_strip_ref,
    sums_ref,
    forcing_ref,
):
    forcing_ref[...] = fields_ref[:2]
    cols = fields_ref.shape[2]
    even = is_even("lon")
    padded = []
    for place in range(FIELDS):
        north, south = sides(near_ref[place], far_ref[place])
        values = jnp.concatenate([north, fields_ref[place], south], axis=0)
        west = fold(values[:, :LANES], RIM, RIM, 3 * RIM)
        east = fold(values[:, cols - LANES :], 2 * RIM, 0, 2 * RIM)
        near_strip_ref[place] = jnp.where(even, east, west)
        far_strip_ref[place] = jnp.where(even, west, east)
        padded.append(values)
    ws, mws = basis(*padded)
    for place, values in enumerate(ws):
        w_ref[place] = values
    for place, values in enumerate(mws):
        mw_ref[place] = values
    lane = lanes_of(ws[0].shape)
    sums_ref[...] = moments(ws, mws, (lane >= RIM) & (lane < cols - RIM))


def interior(fields, near, far):
    _, rows, cols = fields.shape
    f32 = jnp.float32
    return pl.pallas_call(
        interior_kernel,
        out_shape=[
            jax.ShapeDtypeStruct((STEPS, rows, cols), f32),
            jax.ShapeDtypeStruct((STEPS + 1, rows, cols), f32),
            jax.ShapeDtypeStruct((FIELDS, folded_rows(rows + 2 * ROWS), LANES), f32),
            jax.ShapeDtypeStruct((FIELDS, folded_rows(rows + 2 * ROWS), LANES), f32),
            jax.ShapeDtypeStruct((ROWS, LANES), f32),
            jax.ShapeDtypeStruct((2, rows, cols), f32),
        ],
        compiler_params=pltpu.CompilerParams(vmem_limit_bytes=VMEM_BYTES),
        cost_estimate=pl.CostEstimate(
            flops=300 * rows * cols, bytes_accessed=64 * rows * cols, transcendentals=0
        ),
        name="interior",
    )(fields, near, far)


def strip_kernel(near, strip_in_ref, message_ref, before_ref, w_ref, mw_ref, sums_ref):
    even = is_even("lon")
    eastern = even if near else jnp.logical_not(even)
    message = message_ref[...]
    column = lax.rem(lanes_of(message.shape), PITCH)
    first = jnp.where(eastern, 2 * RIM, 0)
    halo = (column >= first) & (column < first + RIM)
    padded = []
    for place in range(FIELDS):
        at = place * RIM
        beyond = jnp.where(eastern, turn(message, 2 * RIM - at), turn(message, -at))
        padded.append(jnp.where(halo, beyond, strip_in_ref[place]))
    ws, mws = basis(*padded)
    for place, values in enumerate(ws):
        w_ref[place] = values
    for place, values in enumerate(mws):
        mw_ref[place] = values
    column = lax.rem(lanes_of(ws[0].shape), PITCH)
    edge = (column >= RIM) & (column < 2 * RIM)
    sums_ref[...] = before_ref[...] + moments(ws, mws, edge)


def strip(near, strip_in, message, before):
    rows = strip_in.shape[1] - 2 * ROWS
    f32 = jnp.float32
    return pl.pallas_call(
        functools.partial(strip_kernel, near),
        out_shape=[
            jax.ShapeDtypeStruct((STEPS, rows, LANES), f32),
            jax.ShapeDtypeStruct((STEPS + 1, rows, LANES), f32),
            jax.ShapeDtypeStruct((ROWS, LANES), f32),
        ],
        compiler_params=pltpu.CompilerParams(vmem_limit_bytes=VMEM_BYTES),
        cost_estimate=pl.CostEstimate(
            flops=300 * rows * LANES, bytes_accessed=64 * rows * LANES, transcendentals=0
        ),
        name="near_strip" if near else "far_strip",
    )(strip_in, message, before)


def power(exponent):
    size = jnp.abs(exponent)
    value = jnp.ones(exponent.shape, jnp.float32)
    for bit in range(7):
        up, down = 2.0 ** (1 << bit), 2.0 ** -(1 << bit)
        factor = jnp.where(exponent < 0, down, up)
        value = value * jnp.where((size >> bit) & 1 == 1, factor, 1.0)
    return value


def exponent_of(size):
    bits = jnp.ceil(jnp.log2(jnp.maximum(size, 2.0**-100)))
    return jnp.clip(bits, -100.0, 100.0).astype(jnp.int32)


def nearest(values):
    return jnp.floor(values + 0.5)


def place_kernel(owner_ref, fields_ref, sent_ref, scale_ref):
    count = owner_ref.shape[0]
    span = fields_ref.shape[1] // count
    sent_ref[...] = jnp.zeros(sent_ref.shape, jnp.int16)
    scale_ref[...] = jnp.zeros(scale_ref.shape, jnp.float32)
    for block in range(count):
        target = owner_ref[block]

        @pl.when(target >= 0)
        def _(block=block, target=target):
            rows = slice(block * span, (block + 1) * span)
            for half in range(fields_ref.shape[2] // LANES):
                cols = slice(half * LANES, (half + 1) * LANES)
                pieces = [fields_ref[0, rows, cols], fields_ref[1, rows, cols]]
                values = jnp.concatenate(pieces, axis=0)
                bits = exponent_of(jnp.max(jnp.abs(values), axis=0, keepdims=True))
                whole = jnp.clip(nearest(values * power(15 - bits)), -32767.0, 32767.0)
                there = slice(2 * span * half, 2 * span * (half + 1))
                sent_ref[target, there] = whole.astype(jnp.int32).astype(jnp.int16)
                scale_ref[target, half : half + 1] = bits.astype(jnp.float32)


def place(owner, fields, lon_count):
    _, rows, cols = fields.shape
    span = rows // owner.shape[0]
    return pl.pallas_call(
        place_kernel,
        in_specs=[
            pl.BlockSpec(memory_space=pltpu.SMEM),
            pl.BlockSpec(memory_space=pltpu.VMEM),
        ],
        out_shape=[
            jax.ShapeDtypeStruct((lon_count, cols // LANES * 2 * span + TAIL, LANES), jnp.int16),
            jax.ShapeDtypeStruct((lon_count, ROWS, LANES), jnp.float32),
        ],
        compiler_params=pltpu.CompilerParams(vmem_limit_bytes=VMEM_BYTES),
        cost_estimate=pl.CostEstimate(
            flops=60 * rows * cols, bytes_accessed=12 * rows * cols, transcendentals=0
        ),
        name="place",
    )(owner, fields)


def seal_kernel(sums_ref, other_ref, scale_ref, tail_ref):
    sums = sums_ref[:SUM_ROWS] + other_ref[:SUM_ROWS]
    bits = exponent_of(jnp.abs(sums))
    scaled = sums * power(-bits) * 2.0**14
    high = nearest(scaled)
    low = nearest((scaled - high) * 2.0**15)
    parts = jnp.concatenate([bits.astype(jnp.float32), high, low], axis=0)
    for slot in range(tail_ref.shape[0]):
        tile = jnp.concatenate([parts, scale_ref[slot, : TAIL - 3 * SUM_ROWS]], axis=0)
        tail_ref[slot] = tile.astype(jnp.int32).astype(jnp.int16)


def seal(sums, other, scale):
    return pl.pallas_call(
        seal_kernel,
        out_shape=jax.ShapeDtypeStruct((scale.shape[0], TAIL, LANES), jnp.int16),
        compiler_params=pltpu.CompilerParams(vmem_limit_bytes=VMEM_BYTES),
        name="seal",
    )(sums, other, scale)


def combine_kernel(
    arrived_ref,
    w_ref,
    mw_ref,
    near_w_ref,
    near_mw_ref,
    far_w_ref,
    far_mw_ref,
    pressure_hbm,
    residual_hbm,
    held_hbm,
    pressure_ref,
    residual_ref,
    held_ref,
    held_sem,
    sems,
):
    rows = held_ref.shape[1]
    slots = held_ref.shape[0]
    tails = []
    for slot in range(slots):
        tails.append(arrived_ref[slot, arrived_ref.shape[1] - TAIL :].astype(jnp.int32))
    scales = jnp.concatenate([tail[3 * SUM_ROWS :] for tail in tails], axis=0)
    scales = power(scales - 15)
    exponents = jnp.concatenate([tail[:SUM_ROWS] for tail in tails], axis=0)
    high = jnp.concatenate([tail[SUM_ROWS : 2 * SUM_ROWS] for tail in tails], axis=0)
    low = jnp.concatenate([tail[2 * SUM_ROWS : 3 * SUM_ROWS] for tail in tails], axis=0)
    digits = high.astype(jnp.float32) + low.astype(jnp.float32) * 2.0**-15
    sums = digits * power(exponents - 14)
    packed = sums[:SUM_ROWS]
    for slot in range(1, slots):
        packed = packed + sums[slot * SUM_ROWS : (slot + 1) * SUM_ROWS]
    spare = TAIL - 3 * SUM_ROWS
    for slot in range(slots):
        for half in range(held_ref.shape[2] // LANES):
            at = slot * spare + half
            whole = arrived_ref[slot, half * rows : (half + 1) * rows].astype(jnp.int32)
            whole = whole.astype(jnp.float32) * scales[at : at + 1]
            held_ref[slot, :, half * LANES : (half + 1) * LANES] = whole
    held_copy = pltpu.make_async_copy(held_ref, held_hbm, held_sem)
    held_copy.start()
    quarter = lanes_of(packed.shape) // QUARTER
    totals = [
        jnp.sum(jnp.where(quarter == place, packed, 0.0), axis=1, keepdims=True)
        for place in range(4)
    ]
    entry = lambda place: totals[place % 4][place // 4 : place // 4 + 1, :]
    right = [entry(place) for place in range(STEPS)]
    matrix = {}
    place = STEPS
    for low in range(STEPS):
        for high in range(low, STEPS):
            matrix[low, high] = entry(place)
            place += 1
    for pivot in range(STEPS):
        inverse = 1.0 / matrix[pivot, pivot]
        for row in range(pivot + 1, STEPS):
            factor = matrix[pivot, row] * inverse
            for col in range(row, STEPS):
                matrix[row, col] = matrix[row, col] - factor * matrix[pivot, col]
            right[row] = right[row] - factor * right[pivot]
        matrix[pivot, pivot] = inverse
    for pivot in reversed(range(STEPS)):
        for col in range(pivot + 1, STEPS):
            right[pivot] = right[pivot] - matrix[pivot, col] * right[col]
        right[pivot] = right[pivot] * matrix[pivot, pivot]

    def results(w_ref, mw_ref, part):
        pressure = right[0] * w_ref[0, part]
        residual = mw_ref[0, part] - right[0] * (mw_ref[0, part] - mw_ref[1, part])
        for place in range(1, STEPS):
            pressure = pressure + right[place] * w_ref[place, part]
            image = mw_ref[place, part] - mw_ref[place + 1, part]
            residual = residual - right[place] * image
        return pressure, residual

    rows, cols = pressure_ref.shape
    even = is_even("lon")
    near = results(near_w_ref, near_mw_ref, slice(None))
    far = results(far_w_ref, far_mw_ref, slice(None))
    west = [jnp.where(even, b, a) for a, b in zip(near, far)]
    east = [jnp.where(even, a, b) for a, b in zip(near, far)]

    def unfold(values, parts, lane):
        return jnp.concatenate([turn(values, lane - RIM - part * PITCH) for part in parts], axis=0)

    copies = []
    for piece in range(PIECES):
        part = slice(piece * rows // PIECES, (piece + 1) * rows // PIECES)
        inner = results(w_ref, mw_ref, part)
        parts = range(piece * FOLD // PIECES, (piece + 1) * FOLD // PIECES)
        lane = lanes_of((rows // PIECES, LANES))
        for field, (out_ref, out_hbm, inside) in enumerate(
            zip((pressure_ref, residual_ref), (pressure_hbm, residual_hbm), inner)
        ):
            border = unfold(west[field], parts, 0)
            out_ref[part, :LANES] = jnp.where(lane < RIM, border, inside[:, :LANES])
            if cols > 2 * LANES:
                out_ref[part, LANES : cols - LANES] = inside[:, LANES : cols - LANES]
            border = unfold(east[field], parts, LANES - RIM)
            out_ref[part, cols - LANES :] = jnp.where(
                lane >= LANES - RIM, border, inside[:, cols - LANES :]
            )
            there = pl.ds(piece * rows // PIECES, rows // PIECES)
            copy = pltpu.make_async_copy(
                out_ref.at[there], out_hbm.at[there], sems.at[field, piece]
            )
            copy.start()
            copies.append(copy)
    held_copy.wait()
    for copy in copies:
        copy.wait()


def combine(arrived, w, mw, near, far):
    rows, cols = w.shape[1:]
    shape = jax.ShapeDtypeStruct((rows, cols), jnp.float32)
    held = (arrived.shape[0], (arrived.shape[1] - TAIL) * LANES // cols, cols)
    return pl.pallas_call(
        combine_kernel,
        out_shape=[shape, shape, jax.ShapeDtypeStruct(held, jnp.float32)],
        out_specs=[pl.BlockSpec(memory_space=pltpu.HBM)] * 3,
        scratch_shapes=[
            pltpu.VMEM((rows, cols), jnp.float32),
            pltpu.VMEM((rows, cols), jnp.float32),
            pltpu.VMEM(held, jnp.float32),
            pltpu.SemaphoreType.DMA,
            pltpu.SemaphoreType.DMA((2, PIECES)),
        ],
        compiler_params=pltpu.CompilerParams(vmem_limit_bytes=VMEM_BYTES),
        name="combine",
    )(arrived, w, mw, *near, *far)


def exchange(values, axis, distance):
    pairs = [(place, place ^ distance) for place in range(lax.axis_size(axis))]
    return lax.ppermute(values, axis, pairs)


def swap(values, axis, first):
    count = lax.axis_size(axis)
    pairs = []
    for place in range(first, count, 2):
        beside = (place + 1) % count
        pairs += [(place, beside), (beside, place)]
    return lax.ppermute(values, axis, pairs)


def on_device(tendency, thickness, level_count, block_mask, owner, inertia):
    lat_count = lax.axis_size("lat")
    lon_count = lax.axis_size("lon")
    inputs = (tendency, thickness, level_count, inertia)
    near, far = integrate_outer(*inputs)
    fields, side = integrate(*inputs)
    near = swap(near, "lat", 0)
    far = swap(far, "lat", 1)
    near_edge, far_edge = edges(side, near, far)
    far_edge = swap(far_edge, "lon", 1)
    near_edge = swap(near_edge, "lon", 0)
    w, mw, near_strip, far_strip, sums, forcing = interior(fields, near, far)
    *near_results, sums = strip(True, near_strip, near_edge, sums)
    *far_results, sums = strip(False, far_strip, far_edge, sums)
    sent, scale = place(owner[:, 0], forcing, lon_count)
    shift = 1
    while 2 * shift < lat_count:
        sums = sums + exchange(sums, "lat", shift)
        shift *= 2
    tail = seal(sums, exchange(sums, "lat", shift), scale)
    sent = lax.dynamic_update_slice(sent, tail, (0, sent.shape[1] - TAIL, 0))
    arrived = lax.all_to_all(sent, "lon", split_axis=0, concat_axis=0, tiled=True)
    pressure, residual, held = combine(arrived, w, mw, near_results, far_results)
    held = held.reshape((1, 1, lon_count, 2, held.shape[1] // 2, held.shape[2]))
    return (held, pressure, residual)


def solution(mesh):
    return jax.shard_map(
        on_device,
        mesh=mesh,
        in_specs=(
            P(None, None, "lat", "lon"),
            P(),
            P("lat", "lon"),
            P("lat", "lon"),
            P("lat", "lon"),
            P("lat", "lon"),
        ),
        out_specs=(P("lat", "lon", None, None, None, None), P("lat", "lon"), P("lat", "lon")),
        check_vma=False,
    )
```

```python
import functools

import jax
import jax.numpy as jnp
from jax import lax
from jax.experimental import pallas as pl
from jax.experimental.pallas import tpu as pltpu
from jax.sharding import PartitionSpec as P

STEPS = 4
RIM = STEPS + 1
ROWS = 8
LANES = 128
HALF = LANES // 2
QUARTER = LANES // 4
FOLD = 4
PITCH = LANES // FOLD
CHUNK = 32
FIELDS = 4
PIECES = 2
OUTER = 16
TAIL = 16
SUM_ROWS = 4
VMEM_BYTES = 16 * 1024 * 1024
WHOLE_BYTES = 56450000


def lanes_of(shape):
    return lax.broadcasted_iota(jnp.int32, shape, len(shape) - 1)


def turn(values, amount):
    amount = amount % values.shape[1]
    return pltpu.roll(values, amount, 1) if amount else values


def sides(near, far):
    place = lax.axis_index("lat")
    even = is_even("lat")
    last = lax.axis_size("lat") - 1
    north = jnp.where(place == 0, 0.0, jnp.where(even, far, near))
    south = jnp.where(place == last, 0.0, jnp.where(even, near, far))
    return north, south


def is_even(axis):
    return lax.rem(lax.axis_index(axis), 2) == 0


def pack_edges(ref, part):
    cols = ref.shape[2]
    packed = None
    for place in range(FIELDS):
        west = ref[place, part, :LANES]
        east = ref[place, part, cols - LANES :]
        if packed is None:
            lane = lanes_of(west.shape)
            packed = jnp.zeros(west.shape, jnp.float32)
        at = place * RIM
        packed = jnp.where((lane >= at) & (lane < at + RIM), turn(west, at), packed)
        at = HALF + place * RIM
        packed = jnp.where((lane >= at) & (lane < at + RIM), turn(east, at + RIM), packed)
    return packed


def integrate_bands(bands, thick_ref, count_ref, tend_ref, waits, finish):
    levels = tend_ref.shape[1]
    for place, (row, size) in enumerate(bands):
        part = slice(row, row + size)
        waits[place]()
        count = count_ref[part]
        first = jnp.zeros(count.shape, jnp.float32)
        second = jnp.zeros(count.shape, jnp.float32)
        depth = jnp.zeros(count.shape, jnp.float32)
        for level in range(levels):
            layer = jnp.where(count > level, thick_ref[level], 0.0)
            depth = depth + layer
            first = first + layer * tend_ref[0, level, part].astype(jnp.float32)
            second = second + layer * tend_ref[1, level, part].astype(jnp.float32)
        finish(place, part, (first, second, depth))


def outer_kernel(
    thick_hbm,
    count_hbm,
    inertia_hbm,
    tend_hbm,
    near_ref,
    far_ref,
    thick_ref,
    count_ref,
    tend_ref,
    thick_sem,
    sems,
):
    rows = count_hbm.shape[0]
    even = is_even("lat")
    starts = (0, rows - OUTER)
    bands = [(place * OUTER, OUTER) for place in range(2)]

    def pair(source, target, place, kind):
        there = pl.ds(starts[place], OUTER)
        here = pl.ds(place * OUTER, OUTER)
        if kind == 0:
            return pltpu.make_async_copy(
                source.at[:, :, there], target.at[:, :, here], sems.at[kind, place]
            )
        return pltpu.make_async_copy(source.at[there], target.at[here], sems.at[kind, place])

    tends = [pair(tend_hbm, tend_ref, place, 0) for place in range(2)]
    counts = [pair(count_hbm, count_ref, place, 1) for place in range(2)]
    thick = pltpu.make_async_copy(thick_hbm, thick_ref, thick_sem)
    last = rows - ROWS
    near_row = pl.multiple_of(jnp.where(even, last, 0), ROWS)
    far_row = pl.multiple_of(jnp.where(even, 0, last), ROWS)
    inertias = [
        pltpu.make_async_copy(
            inertia_hbm.at[pl.ds(row, ROWS)], ref.at[FIELDS - 1], sems.at[2, place]
        )
        for place, (row, ref) in enumerate(((near_row, near_ref), (far_row, far_ref)))
    ]
    for copy in (tends[0], counts[0], thick, tends[1], counts[1], inertias[0], inertias[1]):
        copy.start()
    thick.wait()
    results = []

    def wait(place):
        def run():
            counts[place].wait()
            tends[place].wait()

        return run

    integrate_bands(
        bands,
        thick_ref,
        count_ref,
        tend_ref,
        [wait(place) for place in range(2)],
        lambda place, part, values: results.append(values),
    )
    for field in range(FIELDS - 1):
        head = results[0][field][:ROWS]
        tail = results[1][field][-ROWS:]
        near_ref[field] = jnp.where(even, tail, head)
        far_ref[field] = jnp.where(even, head, tail)
    for copy in inertias:
        copy.wait()


def whole_kernel(
    thick_hbm,
    count_hbm,
    inertia_hbm,
    tend_hbm,
    fields_ref,
    side_ref,
    thick_ref,
    count_ref,
    tend_ref,
    sems,
    band_sems,
):
    rows = count_hbm.shape[0]
    bands = [(row, CHUNK) for row in range(0, rows, CHUNK)]
    tends = []
    for place, (row, size) in enumerate(bands):
        part = pl.ds(row, size)
        tends.append(
            pltpu.make_async_copy(
                tend_hbm.at[:, :, part], tend_ref.at[:, :, part], band_sems.at[place]
            )
        )
    count = pltpu.make_async_copy(count_hbm, count_ref, sems.at[0])
    thick = pltpu.make_async_copy(thick_hbm, thick_ref, sems.at[1])
    inertia = pltpu.make_async_copy(inertia_hbm, fields_ref.at[FIELDS - 1], sems.at[2])
    for copy in [tends[0], count, thick, inertia] + tends[1:]:
        copy.start()
    for copy in (count, thick, inertia):
        copy.wait()

    def finish(place, part, values):
        for field in range(FIELDS - 1):
            fields_ref[field, part] = values[field]
        side_ref[part] = pack_edges(fields_ref, part)

    integrate_bands(
        bands, thick_ref, count_ref, tend_ref, [copy.wait for copy in tends], finish
    )


def integrate_cost(tendency, rows):
    components, levels, _, cols = tendency.shape
    return pl.CostEstimate(
        flops=6 * components * levels * rows * cols,
        bytes_accessed=2 * components * levels * rows * cols,
        transcendentals=0,
    )


def integrate_outer(tendency, thickness, level_count, inertia):
    components, levels, _, cols = tendency.shape
    f32 = jnp.float32
    return pl.pallas_call(
        outer_kernel,
        in_specs=[pl.BlockSpec(memory_space=pltpu.HBM)] * 4,
        out_shape=[jax.ShapeDtypeStruct((FIELDS, ROWS, cols), f32)] * 2,
        scratch_shapes=[
            pltpu.SMEM(thickness.shape, f32),
            pltpu.VMEM((2 * OUTER, cols), jnp.int32),
            pltpu.VMEM((components, levels, 2 * OUTER, cols), tendency.dtype),
            pltpu.SemaphoreType.DMA,
            pltpu.SemaphoreType.DMA((3, 2)),
        ],
        cost_estimate=integrate_cost(tendency, 2 * OUTER),
        name="outer",
    )(thickness, level_count, inertia, tendency)


def integrate(tendency, thickness, level_count, inertia):
    rows, cols = level_count.shape
    f32 = jnp.float32
    return pl.pallas_call(
        whole_kernel,
        in_specs=[pl.BlockSpec(memory_space=pltpu.HBM)] * 4,
        out_shape=[
            jax.ShapeDtypeStruct((FIELDS, rows, cols), f32),
            jax.ShapeDtypeStruct((rows, LANES), f32),
        ],
        scratch_shapes=[
            pltpu.SMEM(thickness.shape, f32),
            pltpu.VMEM((rows, cols), jnp.int32),
            pltpu.VMEM(tendency.shape, tendency.dtype),
            pltpu.SemaphoreType.DMA((3,)),
            pltpu.SemaphoreType.DMA((rows // CHUNK,)),
        ],
        cost_estimate=integrate_cost(tendency, rows),
        compiler_params=pltpu.CompilerParams(vmem_limit_bytes=WHOLE_BYTES),
        name="whole",
    )(thickness, level_count, inertia, tendency)


def folded_rows(tall):
    return (tall - 2 * ROWS) // FOLD + 2 * ROWS


def fold(values, shift, first, last):
    size = folded_rows(values.shape[0])
    lane = lanes_of((size, LANES))
    folded = jnp.zeros((size, LANES), jnp.float32)
    for part in range(FOLD):
        start = part * (size - 2 * ROWS)
        rows = turn(values[start : start + size], part * PITCH + shift)
        here = (lane >= part * PITCH + first) & (lane < part * PITCH + last)
        folded = jnp.where(here, rows, folded)
    return folded


def edges_kernel(side_ref, near_ref, far_ref, near_out_ref, far_out_ref):
    even_lon = is_even("lon")
    near = pack_edges(near_ref, slice(None))
    far = pack_edges(far_ref, slice(None))
    north, south = sides(near, far)
    packed = jnp.concatenate([north, side_ref[...], south], axis=0)
    west = fold(packed, 0, 0, PITCH)
    east = fold(packed, -HALF, 0, PITCH)
    near_out_ref[...] = jnp.where(even_lon, east, west)
    far_out_ref[...] = jnp.where(even_lon, west, east)


def edges(side, near, far):
    rows = side.shape[0] + 2 * ROWS
    message = jax.ShapeDtypeStruct((folded_rows(rows), LANES), jnp.float32)
    return pl.pallas_call(
        edges_kernel,
        out_shape=[message, message],
        compiler_params=pltpu.CompilerParams(vmem_limit_bytes=VMEM_BYTES),
        name="edges",
    )(side, near, far)


def smooth(field):
    rows, cols = field.shape
    tall = field + 0.5 * (pltpu.roll(field, 1, 0) + pltpu.roll(field, rows - 1, 0))
    return tall + 0.5 * (pltpu.roll(tall, 1, 1) + pltpu.roll(tall, cols - 1, 1))


def basis(first, second, depth, inertia):
    tall, wide = first.shape
    own = slice(ROWS, tall - ROWS)
    inside = inertia > 0.0
    east_west = pltpu.roll(first, wide - 1, 1) - pltpu.roll(first, 1, 1)
    north_south = pltpu.roll(second, tall - 1, 0) - pltpu.roll(second, 1, 0)
    scaled = jnp.where(depth > 0.0, 0.5 * (east_west + north_south), 0.0)
    diag = inertia + 2.0 * depth + smooth(depth)
    inverse = jnp.where(inside, 1.0 / jnp.where(inside, diag, 1.0), 0.0)
    mws = [scaled[own]]
    ws = []
    vector = scaled * inverse
    for step in range(STEPS):
        ws.append(vector[own])
        weighed = depth * vector
        scaled = depth * smooth(vector) + smooth(weighed) - 2.0 * weighed
        mws.append(scaled[own])
        if step + 1 < STEPS:
            vector = scaled * inverse
    return ws, mws


def moments(ws, mws, mask):
    ws = [jnp.where(mask, values, 0.0) for values in ws]
    images = [mws[place] - mws[place + 1] for place in range(STEPS)]
    pairs = [ws[place] * mws[0] for place in range(STEPS)]
    for low in range(STEPS):
        for high in range(low, STEPS):
            pairs.append(ws[low] * images[high])
    lines = []
    for product in pairs:
        line = jnp.sum(product, axis=0, keepdims=True)
        total = line[:, :LANES]
        for start in range(LANES, line.shape[1], LANES):
            total = total + line[:, start : start + LANES]
        total = total + turn(total, HALF)
        lines.append(total + turn(total, QUARTER))
    quarter = lanes_of((1, LANES)) // QUARTER
    packed = []
    for start in range(0, len(lines), 4):
        row = jnp.zeros((1, LANES), jnp.float32)
        for place, line in enumerate(lines[start : start + 4]):
            row = jnp.where(quarter == place, line, row)
        packed.append(row)
    packed.append(jnp.zeros((ROWS - len(packed), LANES), jnp.float32))
    return jnp.concatenate(packed, axis=0)


def interior_kernel(
    fields_ref,
    near_ref,
    far_ref,
    w_ref,
    mw_ref,
    near_strip_ref,
    far_strip_ref,
    sums_ref,
    forcing_ref,
):
    forcing_ref[...] = fields_ref[:2]
    cols = fields_ref.shape[2]
    even = is_even("lon")
    padded = []
    for place in range(FIELDS):
        north, south = sides(near_ref[place], far_ref[place])
        values = jnp.concatenate([north, fields_ref[place], south], axis=0)
        west = fold(values[:, :LANES], RIM, RIM, 3 * RIM)
        east = fold(values[:, cols - LANES :], 2 * RIM, 0, 2 * RIM)
        near_strip_ref[place] = jnp.where(even, east, west)
        far_strip_ref[place] = jnp.where(even, west, east)
        padded.append(values)
    ws, mws = basis(*padded)
    for place, values in enumerate(ws):
        w_ref[place] = values
    for place, values in enumerate(mws):
        mw_ref[place] = values
    lane = lanes_of(ws[0].shape)
    sums_ref[...] = moments(ws, mws, (lane >= RIM) & (lane < cols - RIM))


def interior(fields, near, far):
    _, rows, cols = fields.shape
    f32 = jnp.float32
    return pl.pallas_call(
        interior_kernel,
        out_shape=[
            jax.ShapeDtypeStruct((STEPS, rows, cols), f32),
            jax.ShapeDtypeStruct((STEPS + 1, rows, cols), f32),
            jax.ShapeDtypeStruct((FIELDS, folded_rows(rows + 2 * ROWS), LANES), f32),
            jax.ShapeDtypeStruct((FIELDS, folded_rows(rows + 2 * ROWS), LANES), f32),
            jax.ShapeDtypeStruct((ROWS, LANES), f32),
            jax.ShapeDtypeStruct((2, rows, cols), f32),
        ],
        compiler_params=pltpu.CompilerParams(vmem_limit_bytes=VMEM_BYTES),
        cost_estimate=pl.CostEstimate(
            flops=300000 * rows * cols, bytes_accessed=64 * rows * cols, transcendentals=0
        ),
        name="interior",
    )(fields, near, far)


def strip_kernel(near, strip_in_ref, message_ref, before_ref, w_ref, mw_ref, sums_ref):
    even = is_even("lon")
    eastern = even if near else jnp.logical_not(even)
    message = message_ref[...]
    column = lax.rem(lanes_of(message.shape), PITCH)
    first = jnp.where(eastern, 2 * RIM, 0)
    halo = (column >= first) & (column < first + RIM)
    padded = []
    for place in range(FIELDS):
        at = place * RIM
        beyond = jnp.where(eastern, turn(message, 2 * RIM - at), turn(message, -at))
        padded.append(jnp.where(halo, beyond, strip_in_ref[place]))
    ws, mws = basis(*padded)
    for place, values in enumerate(ws):
        w_ref[place] = values
    for place, values in enumerate(mws):
        mw_ref[place] = values
    column = lax.rem(lanes_of(ws[0].shape), PITCH)
    edge = (column >= RIM) & (column < 2 * RIM)
    sums_ref[...] = before_ref[...] + moments(ws, mws, edge)


def strip(near, strip_in, message, before):
    rows = strip_in.shape[1] - 2 * ROWS
    f32 = jnp.float32
    return pl.pallas_call(
        functools.partial(strip_kernel, near),
        out_shape=[
            jax.ShapeDtypeStruct((STEPS, rows, LANES), f32),
            jax.ShapeDtypeStruct((STEPS + 1, rows, LANES), f32),
            jax.ShapeDtypeStruct((ROWS, LANES), f32),
        ],
        compiler_params=pltpu.CompilerParams(vmem_limit_bytes=VMEM_BYTES),
        cost_estimate=pl.CostEstimate(
            flops=300 * rows * LANES, bytes_accessed=64 * rows * LANES, transcendentals=0
        ),
        name="near_strip" if near else "far_strip",
    )(strip_in, message, before)


def power(exponent):
    size = jnp.abs(exponent)
    value = jnp.ones(exponent.shape, jnp.float32)
    for bit in range(7):
        up, down = 2.0 ** (1 << bit), 2.0 ** -(1 << bit)
        factor = jnp.where(exponent < 0, down, up)
        value = value * jnp.where((size >> bit) & 1 == 1, factor, 1.0)
    return value


def exponent_of(size):
    bits = jnp.ceil(jnp.log2(jnp.maximum(size, 2.0**-100)))
    return jnp.clip(bits, -100.0, 100.0).astype(jnp.int32)


def nearest(values):
    return jnp.floor(values + 0.5)


def place_kernel(owner_ref, fields_ref, sent_ref, scale_ref):
    count = owner_ref.shape[0]
    span = fields_ref.shape[1] // count
    sent_ref[...] = jnp.zeros(sent_ref.shape, jnp.int16)
    scale_ref[...] = jnp.zeros(scale_ref.shape, jnp.float32)
    for block in range(count):
        target = owner_ref[block]

        @pl.when(target >= 0)
        def _(block=block, target=target):
            rows = slice(block * span, (block + 1) * span)
            for half in range(fields_ref.shape[2] // LANES):
                cols = slice(half * LANES, (half + 1) * LANES)
                pieces = [fields_ref[0, rows, cols], fields_ref[1, rows, cols]]
                values = jnp.concatenate(pieces, axis=0)
                bits = exponent_of(jnp.max(jnp.abs(values), axis=0, keepdims=True))
                whole = jnp.clip(nearest(values * power(15 - bits)), -32767.0, 32767.0)
                there = slice(2 * span * half, 2 * span * (half + 1))
                sent_ref[target, there] = whole.astype(jnp.int32).astype(jnp.int16)
                scale_ref[target, half : half + 1] = bits.astype(jnp.float32)


def place(owner, fields, lon_count):
    _, rows, cols = fields.shape
    span = rows // owner.shape[0]
    return pl.pallas_call(
        place_kernel,
        in_specs=[
            pl.BlockSpec(memory_space=pltpu.SMEM),
            pl.BlockSpec(memory_space=pltpu.VMEM),
        ],
        out_shape=[
            jax.ShapeDtypeStruct((lon_count, cols // LANES * 2 * span + TAIL, LANES), jnp.int16),
            jax.ShapeDtypeStruct((lon_count, ROWS, LANES), jnp.float32),
        ],
        compiler_params=pltpu.CompilerParams(vmem_limit_bytes=VMEM_BYTES),
        cost_estimate=pl.CostEstimate(
            flops=60 * rows * cols, bytes_accessed=12 * rows * cols, transcendentals=0
        ),
        name="place",
    )(owner, fields)


def seal_kernel(sums_ref, other_ref, scale_ref, tail_ref):
    sums = sums_ref[:SUM_ROWS] + other_ref[:SUM_ROWS]
    bits = exponent_of(jnp.abs(sums))
    scaled = sums * power(-bits) * 2.0**14
    high = nearest(scaled)
    low = nearest((scaled - high) * 2.0**15)
    parts = jnp.concatenate([bits.astype(jnp.float32), high, low], axis=0)
    for slot in range(tail_ref.shape[0]):
        tile = jnp.concatenate([parts, scale_ref[slot, : TAIL - 3 * SUM_ROWS]], axis=0)
        tail_ref[slot] = tile.astype(jnp.int32).astype(jnp.int16)


def seal(sums, other, scale):
    return pl.pallas_call(
        seal_kernel,
        out_shape=jax.ShapeDtypeStruct((scale.shape[0], TAIL, LANES), jnp.int16),
        compiler_params=pltpu.CompilerParams(vmem_limit_bytes=VMEM_BYTES),
        name="seal",
    )(sums, other, scale)


def combine_kernel(
    arrived_ref,
    w_ref,
    mw_ref,
    near_w_ref,
    near_mw_ref,
    far_w_ref,
    far_mw_ref,
    pressure_hbm,
    residual_hbm,
    held_hbm,
    pressure_ref,
    residual_ref,
    held_ref,
    held_sem,
    sems,
):
    rows = held_ref.shape[1]
    slots = held_ref.shape[0]
    tails = []
    for slot in range(slots):
        tails.append(arrived_ref[slot, arrived_ref.shape[1] - TAIL :].astype(jnp.int32))
    scales = jnp.concatenate([tail[3 * SUM_ROWS :] for tail in tails], axis=0)
    scales = power(scales - 15)
    exponents = jnp.concatenate([tail[:SUM_ROWS] for tail in tails], axis=0)
    high = jnp.concatenate([tail[SUM_ROWS : 2 * SUM_ROWS] for tail in tails], axis=0)
    low = jnp.concatenate([tail[2 * SUM_ROWS : 3 * SUM_ROWS] for tail in tails], axis=0)
    digits = high.astype(jnp.float32) + low.astype(jnp.float32) * 2.0**-15
    sums = digits * power(exponents - 14)
    packed = sums[:SUM_ROWS]
    for slot in range(1, slots):
        packed = packed + sums[slot * SUM_ROWS : (slot + 1) * SUM_ROWS]
    spare = TAIL - 3 * SUM_ROWS
    for slot in range(slots):
        for half in range(held_ref.shape[2] // LANES):
            at = slot * spare + half
            whole = arrived_ref[slot, half * rows : (half + 1) * rows].astype(jnp.int32)
            whole = whole.astype(jnp.float32) * scales[at : at + 1]
            held_ref[slot, :, half * LANES : (half + 1) * LANES] = whole
    held_copy = pltpu.make_async_copy(held_ref, held_hbm, held_sem)
    held_copy.start()
    quarter = lanes_of(packed.shape) // QUARTER
    totals = [
        jnp.sum(jnp.where(quarter == place, packed, 0.0), axis=1, keepdims=True)
        for place in range(4)
    ]
    entry = lambda place: totals[place % 4][place // 4 : place // 4 + 1, :]
    right = [entry(place) for place in range(STEPS)]
    matrix = {}
    place = STEPS
    for low in range(STEPS):
        for high in range(low, STEPS):
            matrix[low, high] = entry(place)
            place += 1
    for pivot in range(STEPS):
        inverse = 1.0 / matrix[pivot, pivot]
        for row in range(pivot + 1, STEPS):
            factor = matrix[pivot, row] * inverse
            for col in range(row, STEPS):
                matrix[row, col] = matrix[row, col] - factor * matrix[pivot, col]
            right[row] = right[row] - factor * right[pivot]
        matrix[pivot, pivot] = inverse
    for pivot in reversed(range(STEPS)):
        for col in range(pivot + 1, STEPS):
            right[pivot] = right[pivot] - matrix[pivot, col] * right[col]
        right[pivot] = right[pivot] * matrix[pivot, pivot]

    def results(w_ref, mw_ref, part):
        pressure = right[0] * w_ref[0, part]
        residual = mw_ref[0, part] - right[0] * (mw_ref[0, part] - mw_ref[1, part])
        for place in range(1, STEPS):
            pressure = pressure + right[place] * w_ref[place, part]
            image = mw_ref[place, part] - mw_ref[place + 1, part]
            residual = residual - right[place] * image
        return pressure, residual

    rows, cols = pressure_ref.shape
    even = is_even("lon")
    near = results(near_w_ref, near_mw_ref, slice(None))
    far = results(far_w_ref, far_mw_ref, slice(None))
    west = [jnp.where(even, b, a) for a, b in zip(near, far)]
    east = [jnp.where(even, a, b) for a, b in zip(near, far)]

    def unfold(values, parts, lane):
        return jnp.concatenate([turn(values, lane - RIM - part * PITCH) for part in parts], axis=0)

    copies = []
    for piece in range(PIECES):
        part = slice(piece * rows // PIECES, (piece + 1) * rows // PIECES)
        inner = results(w_ref, mw_ref, part)
        parts = range(piece * FOLD // PIECES, (piece + 1) * FOLD // PIECES)
        lane = lanes_of((rows // PIECES, LANES))
        for field, (out_ref, out_hbm, inside) in enumerate(
            zip((pressure_ref, residual_ref), (pressure_hbm, residual_hbm), inner)
        ):
            border = unfold(west[field], parts, 0)
            out_ref[part, :LANES] = jnp.where(lane < RIM, border, inside[:, :LANES])
            if cols > 2 * LANES:
                out_ref[part, LANES : cols - LANES] = inside[:, LANES : cols - LANES]
            border = unfold(east[field], parts, LANES - RIM)
            out_ref[part, cols - LANES :] = jnp.where(
                lane >= LANES - RIM, border, inside[:, cols - LANES :]
            )
            there = pl.ds(piece * rows // PIECES, rows // PIECES)
            copy = pltpu.make_async_copy(
                out_ref.at[there], out_hbm.at[there], sems.at[field, piece]
            )
            copy.start()
            copies.append(copy)
    held_copy.wait()
    for copy in copies:
        copy.wait()


def combine(arrived, w, mw, near, far):
    rows, cols = w.shape[1:]
    shape = jax.ShapeDtypeStruct((rows, cols), jnp.float32)
    held = (arrived.shape[0], (arrived.shape[1] - TAIL) * LANES // cols, cols)
    return pl.pallas_call(
        combine_kernel,
        out_shape=[shape, shape, jax.ShapeDtypeStruct(held, jnp.float32)],
        out_specs=[pl.BlockSpec(memory_space=pltpu.HBM)] * 3,
        scratch_shapes=[
            pltpu.VMEM((rows, cols), jnp.float32),
            pltpu.VMEM((rows, cols), jnp.float32),
            pltpu.VMEM(held, jnp.float32),
            pltpu.SemaphoreType.DMA,
            pltpu.SemaphoreType.DMA((2, PIECES)),
        ],
        compiler_params=pltpu.CompilerParams(vmem_limit_bytes=VMEM_BYTES),
        name="combine",
    )(arrived, w, mw, *near, *far)


def exchange(values, axis, distance):
    pairs = [(place, place ^ distance) for place in range(lax.axis_size(axis))]
    return lax.ppermute(values, axis, pairs)


def swap(values, axis, first):
    count = lax.axis_size(axis)
    pairs = []
    for place in range(first, count, 2):
        beside = (place + 1) % count
        pairs += [(place, beside), (beside, place)]
    return lax.ppermute(values, axis, pairs)


def on_device(tendency, thickness, level_count, block_mask, owner, inertia):
    lat_count = lax.axis_size("lat")
    lon_count = lax.axis_size("lon")
    inputs = (tendency, thickness, level_count, inertia)
    near, far = integrate_outer(*inputs)
    fields, side = integrate(*inputs)
    near = swap(near, "lat", 0)
    far = swap(far, "lat", 1)
    near_edge, far_edge = edges(side, near, far)
    far_edge = swap(far_edge, "lon", 1)
    near_edge = swap(near_edge, "lon", 0)
    w, mw, near_strip, far_strip, sums, forcing = interior(fields, near, far)
    *near_results, sums = strip(True, near_strip, near_edge, sums)
    *far_results, sums = strip(False, far_strip, far_edge, sums)
    sent, scale = place(owner[:, 0], forcing, lon_count)
    shift = 1
    while 2 * shift < lat_count:
        sums = sums + exchange(sums, "lat", shift)
        shift *= 2
    tail = seal(sums, exchange(sums, "lat", shift), scale)
    sent = lax.dynamic_update_slice(sent, tail, (0, sent.shape[1] - TAIL, 0))
    arrived = lax.all_to_all(sent, "lon", split_axis=0, concat_axis=0, tiled=True)
    pressure, residual, held = combine(arrived, w, mw, near_results, far_results)
    held = held.reshape((1, 1, lon_count, 2, held.shape[1] // 2, held.shape[2]))
    return (held, pressure, residual)


def solution(mesh):
    return jax.shard_map(
        on_device,
        mesh=mesh,
        in_specs=(
            P(None, None, "lat", "lon"),
            P(),
            P("lat", "lon"),
            P("lat", "lon"),
            P("lat", "lon"),
            P("lat", "lon"),
        ),
        out_specs=(P("lat", "lon", None, None, None, None), P("lat", "lon"), P("lat", "lon")),
        check_vma=False,
    )
```

```python
import functools

import jax
import jax.numpy as jnp
from jax import lax
from jax.experimental import pallas as pl
from jax.experimental.pallas import tpu as pltpu
from jax.sharding import PartitionSpec as P

STEPS = 4
RIM = STEPS + 1
ROWS = 8
LANES = 128
HALF = LANES // 2
QUARTER = LANES // 4
FOLD = 4
PITCH = LANES // FOLD
CHUNK = 32
FIELDS = 4
PIECES = 2
OUTER = 16
TAIL = 16
SUM_ROWS = 4
VMEM_BYTES = 16 * 1024 * 1024
WHOLE_BYTES = 56450000


def lanes_of(shape):
    return lax.broadcasted_iota(jnp.int32, shape, len(shape) - 1)


def turn(values, amount):
    amount = amount % values.shape[1]
    return pltpu.roll(values, amount, 1) if amount else values


def sides(near, far):
    place = lax.axis_index("lat")
    even = is_even("lat")
    last = lax.axis_size("lat") - 1
    north = jnp.where(place == 0, 0.0, jnp.where(even, far, near))
    south = jnp.where(place == last, 0.0, jnp.where(even, near, far))
    return north, south


def is_even(axis):
    return lax.rem(lax.axis_index(axis), 2) == 0


def pack_edges(ref, part):
    cols = ref.shape[2]
    packed = None
    for place in range(FIELDS):
        west = ref[place, part, :LANES]
        east = ref[place, part, cols - LANES :]
        if packed is None:
            lane = lanes_of(west.shape)
            packed = jnp.zeros(west.shape, jnp.float32)
        at = place * RIM
        packed = jnp.where((lane >= at) & (lane < at + RIM), turn(west, at), packed)
        at = HALF + place * RIM
        packed = jnp.where((lane >= at) & (lane < at + RIM), turn(east, at + RIM), packed)
    return packed


def integrate_bands(bands, thick_ref, count_ref, tend_ref, waits, finish):
    levels = tend_ref.shape[1]
    for place, (row, size) in enumerate(bands):
        part = slice(row, row + size)
        waits[place]()
        count = count_ref[part]
        first = jnp.zeros(count.shape, jnp.float32)
        second = jnp.zeros(count.shape, jnp.float32)
        depth = jnp.zeros(count.shape, jnp.float32)
        for level in range(levels):
            layer = jnp.where(count > level, thick_ref[level], 0.0)
            depth = depth + layer
            first = first + layer * tend_ref[0, level, part].astype(jnp.float32)
            second = second + layer * tend_ref[1, level, part].astype(jnp.float32)
        finish(place, part, (first, second, depth))


def outer_kernel(
    thick_hbm,
    count_hbm,
    inertia_hbm,
    tend_hbm,
    near_ref,
    far_ref,
    thick_ref,
    count_ref,
    tend_ref,
    thick_sem,
    sems,
):
    rows = count_hbm.shape[0]
    even = is_even("lat")
    starts = (0, rows - OUTER)
    bands = [(place * OUTER, OUTER) for place in range(2)]

    def pair(source, target, place, kind):
        there = pl.ds(starts[place], OUTER)
        here = pl.ds(place * OUTER, OUTER)
        if kind == 0:
            return pltpu.make_async_copy(
                source.at[:, :, there], target.at[:, :, here], sems.at[kind, place]
            )
        return pltpu.make_async_copy(source.at[there], target.at[here], sems.at[kind, place])

    tends = [pair(tend_hbm, tend_ref, place, 0) for place in range(2)]
    counts = [pair(count_hbm, count_ref, place, 1) for place in range(2)]
    thick = pltpu.make_async_copy(thick_hbm, thick_ref, thick_sem)
    last = rows - ROWS
    near_row = pl.multiple_of(jnp.where(even, last, 0), ROWS)
    far_row = pl.multiple_of(jnp.where(even, 0, last), ROWS)
    inertias = [
        pltpu.make_async_copy(
            inertia_hbm.at[pl.ds(row, ROWS)], ref.at[FIELDS - 1], sems.at[2, place]
        )
        for place, (row, ref) in enumerate(((near_row, near_ref), (far_row, far_ref)))
    ]
    for copy in (tends[0], counts[0], thick, tends[1], counts[1], inertias[0], inertias[1]):
        copy.start()
    thick.wait()
    results = []

    def wait(place):
        def run():
            counts[place].wait()
            tends[place].wait()

        return run

    integrate_bands(
        bands,
        thick_ref,
        count_ref,
        tend_ref,
        [wait(place) for place in range(2)],
        lambda place, part, values: results.append(values),
    )
    for field in range(FIELDS - 1):
        head = results[0][field][:ROWS]
        tail = results[1][field][-ROWS:]
        near_ref[field] = jnp.where(even, tail, head)
        far_ref[field] = jnp.where(even, head, tail)
    for copy in inertias:
        copy.wait()


def whole_kernel(
    thick_hbm,
    count_hbm,
    inertia_hbm,
    tend_hbm,
    fields_ref,
    side_ref,
    thick_ref,
    count_ref,
    tend_ref,
    sems,
    band_sems,
):
    rows = count_hbm.shape[0]
    bands = [(row, CHUNK) for row in range(0, rows, CHUNK)]
    tends = []
    for place, (row, size) in enumerate(bands):
        part = pl.ds(row, size)
        tends.append(
            pltpu.make_async_copy(
                tend_hbm.at[:, :, part], tend_ref.at[:, :, part], band_sems.at[place]
            )
        )
    count = pltpu.make_async_copy(count_hbm, count_ref, sems.at[0])
    thick = pltpu.make_async_copy(thick_hbm, thick_ref, sems.at[1])
    inertia = pltpu.make_async_copy(inertia_hbm, fields_ref.at[FIELDS - 1], sems.at[2])
    for copy in [tends[0], count, thick, inertia] + tends[1:]:
        copy.start()
    for copy in (count, thick, inertia):
        copy.wait()

    def finish(place, part, values):
        for field in range(FIELDS - 1):
            fields_ref[field, part] = values[field]
        side_ref[part] = pack_edges(fields_ref, part)

    integrate_bands(
        bands, thick_ref, count_ref, tend_ref, [copy.wait for copy in tends], finish
    )


def integrate_cost(tendency, rows):
    components, levels, _, cols = tendency.shape
    return pl.CostEstimate(
        flops=6 * components * levels * rows * cols,
        bytes_accessed=2 * components * levels * rows * cols,
        transcendentals=0,
    )


def integrate_outer(tendency, thickness, level_count, inertia):
    components, levels, _, cols = tendency.shape
    f32 = jnp.float32
    return pl.pallas_call(
        outer_kernel,
        in_specs=[pl.BlockSpec(memory_space=pltpu.HBM)] * 4,
        out_shape=[jax.ShapeDtypeStruct((FIELDS, ROWS, cols), f32)] * 2,
        scratch_shapes=[
            pltpu.SMEM(thickness.shape, f32),
            pltpu.VMEM((2 * OUTER, cols), jnp.int32),
            pltpu.VMEM((components, levels, 2 * OUTER, cols), tendency.dtype),
            pltpu.SemaphoreType.DMA,
            pltpu.SemaphoreType.DMA((3, 2)),
        ],
        cost_estimate=integrate_cost(tendency, 2 * OUTER),
        name="outer",
    )(thickness, level_count, inertia, tendency)


def integrate(tendency, thickness, level_count, inertia):
    rows, cols = level_count.shape
    f32 = jnp.float32
    return pl.pallas_call(
        whole_kernel,
        in_specs=[pl.BlockSpec(memory_space=pltpu.HBM)] * 4,
        out_shape=[
            jax.ShapeDtypeStruct((FIELDS, rows, cols), f32),
            jax.ShapeDtypeStruct((rows, LANES), f32),
        ],
        scratch_shapes=[
            pltpu.SMEM(thickness.shape, f32),
            pltpu.VMEM((rows, cols), jnp.int32),
            pltpu.VMEM(tendency.shape, tendency.dtype),
            pltpu.SemaphoreType.DMA((3,)),
            pltpu.SemaphoreType.DMA((rows // CHUNK,)),
        ],
        cost_estimate=integrate_cost(tendency, rows),
        compiler_params=pltpu.CompilerParams(vmem_limit_bytes=WHOLE_BYTES),
        name="whole",
    )(thickness, level_count, inertia, tendency)


def folded_rows(tall):
    return (tall - 2 * ROWS) // FOLD + 2 * ROWS


def fold(values, shift, first, last):
    size = folded_rows(values.shape[0])
    lane = lanes_of((size, LANES))
    folded = jnp.zeros((size, LANES), jnp.float32)
    for part in range(FOLD):
        start = part * (size - 2 * ROWS)
        rows = turn(values[start : start + size], part * PITCH + shift)
        here = (lane >= part * PITCH + first) & (lane < part * PITCH + last)
        folded = jnp.where(here, rows, folded)
    return folded


def edges_kernel(side_ref, near_ref, far_ref, near_out_ref, far_out_ref):
    even_lon = is_even("lon")
    near = pack_edges(near_ref, slice(None))
    far = pack_edges(far_ref, slice(None))
    north, south = sides(near, far)
    packed = jnp.concatenate([north, side_ref[...], south], axis=0)
    west = fold(packed, 0, 0, PITCH)
    east = fold(packed, -HALF, 0, PITCH)
    near_out_ref[...] = jnp.where(even_lon, east, west)
    far_out_ref[...] = jnp.where(even_lon, west, east)


def edges(side, near, far):
    rows = side.shape[0] + 2 * ROWS
    message = jax.ShapeDtypeStruct((folded_rows(rows), LANES), jnp.float32)
    return pl.pallas_call(
        edges_kernel,
        out_shape=[message, message],
        compiler_params=pltpu.CompilerParams(vmem_limit_bytes=VMEM_BYTES),
        name="edges",
    )(side, near, far)


def smooth(field):
    rows, cols = field.shape
    tall = field + 0.5 * (pltpu.roll(field, 1, 0) + pltpu.roll(field, rows - 1, 0))
    return tall + 0.5 * (pltpu.roll(tall, 1, 1) + pltpu.roll(tall, cols - 1, 1))


def basis(first, second, depth, inertia):
    tall, wide = first.shape
    own = slice(ROWS, tall - ROWS)
    inside = inertia > 0.0
    east_west = pltpu.roll(first, wide - 1, 1) - pltpu.roll(first, 1, 1)
    north_south = pltpu.roll(second, tall - 1, 0) - pltpu.roll(second, 1, 0)
    scaled = jnp.where(depth > 0.0, 0.5 * (east_west + north_south), 0.0)
    diag = inertia + 2.0 * depth + smooth(depth)
    inverse = jnp.where(inside, 1.0 / jnp.where(inside, diag, 1.0), 0.0)
    mws = [scaled[own]]
    ws = []
    vector = scaled * inverse
    ws.append(vector[own])
    for step in range(STEPS):
        weighed = depth * vector
        scaled = depth * smooth(vector) + smooth(weighed) - 2.0 * weighed
        mws.append(scaled[own])
        vector = scaled * inverse
        ws.append(vector[own])
    return ws, mws, diag[own]


def moments(ws, mws, mask):
    ws = [jnp.where(mask, values, 0.0) for values in ws[:STEPS]]
    images = [mws[place] - mws[place + 1] for place in range(STEPS)]
    pairs = [ws[place] * mws[0] for place in range(STEPS)]
    for low in range(STEPS):
        for high in range(low, STEPS):
            pairs.append(ws[low] * images[high])
    lines = []
    for product in pairs:
        line = jnp.sum(product, axis=0, keepdims=True)
        total = line[:, :LANES]
        for start in range(LANES, line.shape[1], LANES):
            total = total + line[:, start : start + LANES]
        total = total + turn(total, HALF)
        lines.append(total + turn(total, QUARTER))
    quarter = lanes_of((1, LANES)) // QUARTER
    packed = []
    for start in range(0, len(lines), 4):
        row = jnp.zeros((1, LANES), jnp.float32)
        for place, line in enumerate(lines[start : start + 4]):
            row = jnp.where(quarter == place, line, row)
        packed.append(row)
    packed.append(jnp.zeros((ROWS - len(packed), LANES), jnp.float32))
    return jnp.concatenate(packed, axis=0)


def interior_kernel(
    fields_ref,
    near_ref,
    far_ref,
    w_ref,
    diag_ref,
    near_strip_ref,
    far_strip_ref,
    sums_ref,
    forcing_ref,
):
    forcing_ref[...] = fields_ref[:2]
    cols = fields_ref.shape[2]
    even = is_even("lon")
    padded = []
    for place in range(FIELDS):
        north, south = sides(near_ref[place], far_ref[place])
        values = jnp.concatenate([north, fields_ref[place], south], axis=0)
        west = fold(values[:, :LANES], RIM, RIM, 3 * RIM)
        east = fold(values[:, cols - LANES :], 2 * RIM, 0, 2 * RIM)
        near_strip_ref[place] = jnp.where(even, east, west)
        far_strip_ref[place] = jnp.where(even, west, east)
        padded.append(values)
    ws, mws, diag = basis(*padded)
    for place, values in enumerate(ws):
        w_ref[place] = values
    diag_ref[...] = diag
    lane = lanes_of(ws[0].shape)
    sums_ref[...] = moments(ws, mws, (lane >= RIM) & (lane < cols - RIM))


def interior(fields, near, far):
    _, rows, cols = fields.shape
    f32 = jnp.float32
    return pl.pallas_call(
        interior_kernel,
        out_shape=[
            jax.ShapeDtypeStruct((STEPS + 1, rows, cols), f32),
            jax.ShapeDtypeStruct((rows, cols), f32),
            jax.ShapeDtypeStruct((FIELDS, folded_rows(rows + 2 * ROWS), LANES), f32),
            jax.ShapeDtypeStruct((FIELDS, folded_rows(rows + 2 * ROWS), LANES), f32),
            jax.ShapeDtypeStruct((ROWS, LANES), f32),
            jax.ShapeDtypeStruct((2, rows, cols), f32),
        ],
        compiler_params=pltpu.CompilerParams(vmem_limit_bytes=VMEM_BYTES),
        cost_estimate=pl.CostEstimate(
            flops=300000 * rows * cols, bytes_accessed=64 * rows * cols, transcendentals=0
        ),
        name="interior",
    )(fields, near, far)


def strip_kernel(near, strip_in_ref, message_ref, before_ref, w_ref, diag_ref, sums_ref):
    even = is_even("lon")
    eastern = even if near else jnp.logical_not(even)
    message = message_ref[...]
    column = lax.rem(lanes_of(message.shape), PITCH)
    first = jnp.where(eastern, 2 * RIM, 0)
    halo = (column >= first) & (column < first + RIM)
    padded = []
    for place in range(FIELDS):
        at = place * RIM
        beyond = jnp.where(eastern, turn(message, 2 * RIM - at), turn(message, -at))
        padded.append(jnp.where(halo, beyond, strip_in_ref[place]))
    ws, mws, diag = basis(*padded)
    for place, values in enumerate(ws):
        w_ref[place] = values
    diag_ref[...] = diag
    column = lax.rem(lanes_of(ws[0].shape), PITCH)
    edge = (column >= RIM) & (column < 2 * RIM)
    sums_ref[...] = before_ref[...] + moments(ws, mws, edge)


def strip(near, strip_in, message, before):
    rows = strip_in.shape[1] - 2 * ROWS
    f32 = jnp.float32
    return pl.pallas_call(
        functools.partial(strip_kernel, near),
        out_shape=[
            jax.ShapeDtypeStruct((STEPS + 1, rows, LANES), f32),
            jax.ShapeDtypeStruct((rows, LANES), f32),
            jax.ShapeDtypeStruct((ROWS, LANES), f32),
        ],
        compiler_params=pltpu.CompilerParams(vmem_limit_bytes=VMEM_BYTES),
        cost_estimate=pl.CostEstimate(
            flops=300 * rows * LANES, bytes_accessed=64 * rows * LANES, transcendentals=0
        ),
        name="near_strip" if near else "far_strip",
    )(strip_in, message, before)


def power(exponent):
    size = jnp.abs(exponent)
    value = jnp.ones(exponent.shape, jnp.float32)
    for bit in range(7):
        up, down = 2.0 ** (1 << bit), 2.0 ** -(1 << bit)
        factor = jnp.where(exponent < 0, down, up)
        value = value * jnp.where((size >> bit) & 1 == 1, factor, 1.0)
    return value


def exponent_of(size):
    bits = jnp.ceil(jnp.log2(jnp.maximum(size, 2.0**-100)))
    return jnp.clip(bits, -100.0, 100.0).astype(jnp.int32)


def nearest(values):
    return jnp.floor(values + 0.5)


def place_kernel(owner_ref, fields_ref, sent_ref, scale_ref):
    count = owner_ref.shape[0]
    span = fields_ref.shape[1] // count
    sent_ref[...] = jnp.zeros(sent_ref.shape, jnp.int16)
    scale_ref[...] = jnp.zeros(scale_ref.shape, jnp.float32)
    for block in range(count):
        target = owner_ref[block]

        @pl.when(target >= 0)
        def _(block=block, target=target):
            rows = slice(block * span, (block + 1) * span)
            for half in range(fields_ref.shape[2] // LANES):
                cols = slice(half * LANES, (half + 1) * LANES)
                pieces = [fields_ref[0, rows, cols], fields_ref[1, rows, cols]]
                values = jnp.concatenate(pieces, axis=0)
                bits = exponent_of(jnp.max(jnp.abs(values), axis=0, keepdims=True))
                whole = jnp.clip(nearest(values * power(15 - bits)), -32767.0, 32767.0)
                there = slice(2 * span * half, 2 * span * (half + 1))
                sent_ref[target, there] = whole.astype(jnp.int32).astype(jnp.int16)
                scale_ref[target, half : half + 1] = bits.astype(jnp.float32)


def place(owner, fields, lon_count):
    _, rows, cols = fields.shape
    span = rows // owner.shape[0]
    return pl.pallas_call(
        place_kernel,
        in_specs=[
            pl.BlockSpec(memory_space=pltpu.SMEM),
            pl.BlockSpec(memory_space=pltpu.VMEM),
        ],
        out_shape=[
            jax.ShapeDtypeStruct((lon_count, cols // LANES * 2 * span + TAIL, LANES), jnp.int16),
            jax.ShapeDtypeStruct((lon_count, ROWS, LANES), jnp.float32),
        ],
        compiler_params=pltpu.CompilerParams(vmem_limit_bytes=VMEM_BYTES),
        cost_estimate=pl.CostEstimate(
            flops=60 * rows * cols, bytes_accessed=12 * rows * cols, transcendentals=0
        ),
        name="place",
    )(owner, fields)


def seal_kernel(sums_ref, other_ref, scale_ref, tail_ref):
    sums = sums_ref[:SUM_ROWS] + other_ref[:SUM_ROWS]
    bits = exponent_of(jnp.abs(sums))
    scaled = sums * power(-bits) * 2.0**14
    high = nearest(scaled)
    low = nearest((scaled - high) * 2.0**15)
    parts = jnp.concatenate([bits.astype(jnp.float32), high, low], axis=0)
    for slot in range(tail_ref.shape[0]):
        tile = jnp.concatenate([parts, scale_ref[slot, : TAIL - 3 * SUM_ROWS]], axis=0)
        tail_ref[slot] = tile.astype(jnp.int32).astype(jnp.int16)


def seal(sums, other, scale):
    return pl.pallas_call(
        seal_kernel,
        out_shape=jax.ShapeDtypeStruct((scale.shape[0], TAIL, LANES), jnp.int16),
        compiler_params=pltpu.CompilerParams(vmem_limit_bytes=VMEM_BYTES),
        name="seal",
    )(sums, other, scale)


def combine_kernel(
    arrived_ref,
    w_ref,
    diag_ref,
    near_w_ref,
    near_diag_ref,
    far_w_ref,
    far_diag_ref,
    pressure_hbm,
    residual_hbm,
    held_hbm,
    pressure_ref,
    residual_ref,
    held_ref,
    held_sem,
    sems,
):
    rows = held_ref.shape[1]
    slots = held_ref.shape[0]
    tails = []
    for slot in range(slots):
        tails.append(arrived_ref[slot, arrived_ref.shape[1] - TAIL :].astype(jnp.int32))
    scales = jnp.concatenate([tail[3 * SUM_ROWS :] for tail in tails], axis=0)
    scales = power(scales - 15)
    exponents = jnp.concatenate([tail[:SUM_ROWS] for tail in tails], axis=0)
    high = jnp.concatenate([tail[SUM_ROWS : 2 * SUM_ROWS] for tail in tails], axis=0)
    low = jnp.concatenate([tail[2 * SUM_ROWS : 3 * SUM_ROWS] for tail in tails], axis=0)
    digits = high.astype(jnp.float32) + low.astype(jnp.float32) * 2.0**-15
    sums = digits * power(exponents - 14)
    packed = sums[:SUM_ROWS]
    for slot in range(1, slots):
        packed = packed + sums[slot * SUM_ROWS : (slot + 1) * SUM_ROWS]
    spare = TAIL - 3 * SUM_ROWS
    for slot in range(slots):
        for half in range(held_ref.shape[2] // LANES):
            at = slot * spare + half
            whole = arrived_ref[slot, half * rows : (half + 1) * rows].astype(jnp.int32)
            whole = whole.astype(jnp.float32) * scales[at : at + 1]
            held_ref[slot, :, half * LANES : (half + 1) * LANES] = whole
    held_copy = pltpu.make_async_copy(held_ref, held_hbm, held_sem)
    held_copy.start()
    quarter = lanes_of(packed.shape) // QUARTER
    totals = [
        jnp.sum(jnp.where(quarter == place, packed, 0.0), axis=1, keepdims=True)
        for place in range(4)
    ]
    entry = lambda place: totals[place % 4][place // 4 : place // 4 + 1, :]
    right = [entry(place) for place in range(STEPS)]
    matrix = {}
    place = STEPS
    for low in range(STEPS):
        for high in range(low, STEPS):
            matrix[low, high] = entry(place)
            place += 1
    for pivot in range(STEPS):
        inverse = 1.0 / matrix[pivot, pivot]
        for row in range(pivot + 1, STEPS):
            factor = matrix[pivot, row] * inverse
            for col in range(row, STEPS):
                matrix[row, col] = matrix[row, col] - factor * matrix[pivot, col]
            right[row] = right[row] - factor * right[pivot]
        matrix[pivot, pivot] = inverse
    for pivot in reversed(range(STEPS)):
        for col in range(pivot + 1, STEPS):
            right[pivot] = right[pivot] - matrix[pivot, col] * right[col]
        right[pivot] = right[pivot] * matrix[pivot, pivot]

    left = [1.0 - right[0]]
    for place in range(1, STEPS):
        left.append(right[place - 1] - right[place])
    left.append(right[STEPS - 1])

    def results(w_ref, diag_ref, part):
        vector = w_ref[0, part]
        pressure = right[0] * vector
        residual = left[0] * vector
        for place in range(1, STEPS):
            vector = w_ref[place, part]
            pressure = pressure + right[place] * vector
            residual = residual + left[place] * vector
        residual = residual + left[STEPS] * w_ref[STEPS, part]
        return pressure, diag_ref[part] * residual

    rows, cols = pressure_ref.shape
    even = is_even("lon")
    near = results(near_w_ref, near_diag_ref, slice(None))
    far = results(far_w_ref, far_diag_ref, slice(None))
    west = [jnp.where(even, b, a) for a, b in zip(near, far)]
    east = [jnp.where(even, a, b) for a, b in zip(near, far)]

    def unfold(values, parts, lane):
        return jnp.concatenate([turn(values, lane - RIM - part * PITCH) for part in parts], axis=0)

    copies = []
    for piece in range(PIECES):
        part = slice(piece * rows // PIECES, (piece + 1) * rows // PIECES)
        inner = results(w_ref, diag_ref, part)
        parts = range(piece * FOLD // PIECES, (piece + 1) * FOLD // PIECES)
        lane = lanes_of((rows // PIECES, LANES))
        for field, (out_ref, out_hbm, inside) in enumerate(
            zip((pressure_ref, residual_ref), (pressure_hbm, residual_hbm), inner)
        ):
            border = unfold(west[field], parts, 0)
            out_ref[part, :LANES] = jnp.where(lane < RIM, border, inside[:, :LANES])
            if cols > 2 * LANES:
                out_ref[part, LANES : cols - LANES] = inside[:, LANES : cols - LANES]
            border = unfold(east[field], parts, LANES - RIM)
            out_ref[part, cols - LANES :] = jnp.where(
                lane >= LANES - RIM, border, inside[:, cols - LANES :]
            )
            there = pl.ds(piece * rows // PIECES, rows // PIECES)
            copy = pltpu.make_async_copy(
                out_ref.at[there], out_hbm.at[there], sems.at[field, piece]
            )
            copy.start()
            copies.append(copy)
    held_copy.wait()
    for copy in copies:
        copy.wait()


def combine(arrived, w, diag, near, far):
    rows, cols = w.shape[1:]
    shape = jax.ShapeDtypeStruct((rows, cols), jnp.float32)
    held = (arrived.shape[0], (arrived.shape[1] - TAIL) * LANES // cols, cols)
    return pl.pallas_call(
        combine_kernel,
        out_shape=[shape, shape, jax.ShapeDtypeStruct(held, jnp.float32)],
        out_specs=[pl.BlockSpec(memory_space=pltpu.HBM)] * 3,
        scratch_shapes=[
            pltpu.VMEM((rows, cols), jnp.float32),
            pltpu.VMEM((rows, cols), jnp.float32),
            pltpu.VMEM(held, jnp.float32),
            pltpu.SemaphoreType.DMA,
            pltpu.SemaphoreType.DMA((2, PIECES)),
        ],
        compiler_params=pltpu.CompilerParams(vmem_limit_bytes=VMEM_BYTES),
        name="combine",
    )(arrived, w, diag, *near, *far)


def exchange(values, axis, distance):
    pairs = [(place, place ^ distance) for place in range(lax.axis_size(axis))]
    return lax.ppermute(values, axis, pairs)


def swap(values, axis, first):
    count = lax.axis_size(axis)
    pairs = []
    for place in range(first, count, 2):
        beside = (place + 1) % count
        pairs += [(place, beside), (beside, place)]
    return lax.ppermute(values, axis, pairs)


def on_device(tendency, thickness, level_count, block_mask, owner, inertia):
    lat_count = lax.axis_size("lat")
    lon_count = lax.axis_size("lon")
    inputs = (tendency, thickness, level_count, inertia)
    near, far = integrate_outer(*inputs)
    fields, side = integrate(*inputs)
    near = swap(near, "lat", 0)
    far = swap(far, "lat", 1)
    near_edge, far_edge = edges(side, near, far)
    far_edge = swap(far_edge, "lon", 1)
    near_edge = swap(near_edge, "lon", 0)
    w, diag, near_strip, far_strip, sums, forcing = interior(fields, near, far)
    *near_results, sums = strip(True, near_strip, near_edge, sums)
    *far_results, sums = strip(False, far_strip, far_edge, sums)
    sent, scale = place(owner[:, 0], forcing, lon_count)
    shift = 1
    while 2 * shift < lat_count:
        sums = sums + exchange(sums, "lat", shift)
        shift *= 2
    tail = seal(sums, exchange(sums, "lat", shift), scale)
    sent = lax.dynamic_update_slice(sent, tail, (0, sent.shape[1] - TAIL, 0))
    arrived = lax.all_to_all(sent, "lon", split_axis=0, concat_axis=0, tiled=True)
    pressure, residual, held = combine(arrived, w, diag, near_results, far_results)
    held = held.reshape((1, 1, lon_count, 2, held.shape[1] // 2, held.shape[2]))
    return (held, pressure, residual)


def solution(mesh):
    return jax.shard_map(
        on_device,
        mesh=mesh,
        in_specs=(
            P(None, None, "lat", "lon"),
            P(),
            P("lat", "lon"),
            P("lat", "lon"),
            P("lat", "lon"),
            P("lat", "lon"),
        ),
        out_specs=(P("lat", "lon", None, None, None, None), P("lat", "lon"), P("lat", "lon")),
        check_vma=False,
    )
```

```python
import functools

import jax
import jax.numpy as jnp
from jax import lax
from jax.experimental import pallas as pl
from jax.experimental.pallas import tpu as pltpu
from jax.sharding import PartitionSpec as P

STEPS = 4
RIM = STEPS + 1
ROWS = 8
LANES = 128
HALF = LANES // 2
QUARTER = LANES // 4
FOLD = 4
PITCH = LANES // FOLD
CHUNK = 32
FIELDS = 4
PIECES = 2
OUTER = 16
TAIL = 16
SUM_ROWS = 4
VMEM_BYTES = 16 * 1024 * 1024
WHOLE_BYTES = 56450000


def lanes_of(shape):
    return lax.broadcasted_iota(jnp.int32, shape, len(shape) - 1)


def turn(values, amount):
    amount = amount % values.shape[1]
    return pltpu.roll(values, amount, 1) if amount else values


def sides(near, far):
    place = lax.axis_index("lat")
    even = is_even("lat")
    last = lax.axis_size("lat") - 1
    north = jnp.where(place == 0, 0.0, jnp.where(even, far, near))
    south = jnp.where(place == last, 0.0, jnp.where(even, near, far))
    return north, south


def is_even(axis):
    return lax.rem(lax.axis_index(axis), 2) == 0


def pack_edges(ref, part):
    cols = ref.shape[2]
    packed = None
    for place in range(FIELDS):
        west = ref[place, part, :LANES]
        east = ref[place, part, cols - LANES :]
        if packed is None:
            lane = lanes_of(west.shape)
            packed = jnp.zeros(west.shape, jnp.float32)
        at = place * RIM
        packed = jnp.where((lane >= at) & (lane < at + RIM), turn(west, at), packed)
        at = HALF + place * RIM
        packed = jnp.where((lane >= at) & (lane < at + RIM), turn(east, at + RIM), packed)
    return packed


def integrate_bands(bands, thick_ref, count_ref, tend_ref, waits, finish):
    levels = tend_ref.shape[1]
    for place, (row, size) in enumerate(bands):
        part = slice(row, row + size)
        waits[place]()
        count = count_ref[part]
        first = jnp.zeros(count.shape, jnp.float32)
        second = jnp.zeros(count.shape, jnp.float32)
        depth = jnp.zeros(count.shape, jnp.float32)
        for level in range(levels):
            layer = jnp.where(count > level, thick_ref[level], 0.0)
            depth = depth + layer
            first = first + layer * tend_ref[0, level, part].astype(jnp.float32)
            second = second + layer * tend_ref[1, level, part].astype(jnp.float32)
        finish(place, part, (first, second, depth))


def outer_kernel(
    thick_hbm,
    count_hbm,
    inertia_hbm,
    tend_hbm,
    near_ref,
    far_ref,
    thick_ref,
    count_ref,
    tend_ref,
    thick_sem,
    sems,
):
    rows = count_hbm.shape[0]
    even = is_even("lat")
    starts = (0, rows - OUTER)
    bands = [(place * OUTER, OUTER) for place in range(2)]

    def pair(source, target, place, kind):
        there = pl.ds(starts[place], OUTER)
        here = pl.ds(place * OUTER, OUTER)
        if kind == 0:
            return pltpu.make_async_copy(
                source.at[:, :, there], target.at[:, :, here], sems.at[kind, place]
            )
        return pltpu.make_async_copy(source.at[there], target.at[here], sems.at[kind, place])

    tends = [pair(tend_hbm, tend_ref, place, 0) for place in range(2)]
    counts = [pair(count_hbm, count_ref, place, 1) for place in range(2)]
    thick = pltpu.make_async_copy(thick_hbm, thick_ref, thick_sem)
    last = rows - ROWS
    near_row = pl.multiple_of(jnp.where(even, last, 0), ROWS)
    far_row = pl.multiple_of(jnp.where(even, 0, last), ROWS)
    inertias = [
        pltpu.make_async_copy(
            inertia_hbm.at[pl.ds(row, ROWS)], ref.at[FIELDS - 1], sems.at[2, place]
        )
        for place, (row, ref) in enumerate(((near_row, near_ref), (far_row, far_ref)))
    ]
    for copy in (tends[0], counts[0], thick, tends[1], counts[1], inertias[0], inertias[1]):
        copy.start()
    thick.wait()
    results = []

    def wait(place):
        def run():
            counts[place].wait()
            tends[place].wait()

        return run

    integrate_bands(
        bands,
        thick_ref,
        count_ref,
        tend_ref,
        [wait(place) for place in range(2)],
        lambda place, part, values: results.append(values),
    )
    for field in range(FIELDS - 1):
        head = results[0][field][:ROWS]
        tail = results[1][field][-ROWS:]
        near_ref[field] = jnp.where(even, tail, head)
        far_ref[field] = jnp.where(even, head, tail)
    for copy in inertias:
        copy.wait()


def whole_kernel(
    thick_hbm,
    count_hbm,
    inertia_hbm,
    tend_hbm,
    fields_ref,
    side_ref,
    thick_ref,
    count_ref,
    tend_ref,
    sems,
    band_sems,
    count_sems,
):
    rows = count_hbm.shape[0]
    bands = [(row, CHUNK) for row in range(0, rows, CHUNK)]
    tends = []
    counts = []
    for place, (row, size) in enumerate(bands):
        part = pl.ds(row, size)
        counts.append(
            pltpu.make_async_copy(count_hbm.at[part], count_ref.at[part], count_sems.at[place])
        )
        tends.append(
            pltpu.make_async_copy(
                tend_hbm.at[:, :, part], tend_ref.at[:, :, part], band_sems.at[place]
            )
        )
    thick = pltpu.make_async_copy(thick_hbm, thick_ref, sems.at[0])
    inertia = pltpu.make_async_copy(inertia_hbm, fields_ref.at[FIELDS - 1], sems.at[1])
    order = [tends[0], counts[0], thick, tends[1], counts[1], inertia]
    for place in range(2, len(bands)):
        order += [tends[place], counts[place]]
    for copy in order:
        copy.start()
    thick.wait()

    def wait(place):
        def run():
            counts[place].wait()
            tends[place].wait()

        return run

    def finish(place, part, values):
        if place == 0:
            inertia.wait()
        for field in range(FIELDS - 1):
            fields_ref[field, part] = values[field]
        side_ref[part] = pack_edges(fields_ref, part)

    waits = [wait(place) for place in range(len(bands))]
    integrate_bands(bands, thick_ref, count_ref, tend_ref, waits, finish)


def integrate_cost(tendency, rows):
    components, levels, _, cols = tendency.shape
    return pl.CostEstimate(
        flops=6 * components * levels * rows * cols,
        bytes_accessed=2 * components * levels * rows * cols,
        transcendentals=0,
    )


def integrate_outer(tendency, thickness, level_count, inertia):
    components, levels, _, cols = tendency.shape
    f32 = jnp.float32
    return pl.pallas_call(
        outer_kernel,
        in_specs=[pl.BlockSpec(memory_space=pltpu.HBM)] * 4,
        out_shape=[jax.ShapeDtypeStruct((FIELDS, ROWS, cols), f32)] * 2,
        scratch_shapes=[
            pltpu.SMEM(thickness.shape, f32),
            pltpu.VMEM((2 * OUTER, cols), jnp.int32),
            pltpu.VMEM((components, levels, 2 * OUTER, cols), tendency.dtype),
            pltpu.SemaphoreType.DMA,
            pltpu.SemaphoreType.DMA((3, 2)),
        ],
        cost_estimate=integrate_cost(tendency, 2 * OUTER),
        name="outer",
    )(thickness, level_count, inertia, tendency)


def integrate(tendency, thickness, level_count, inertia):
    rows, cols = level_count.shape
    f32 = jnp.float32
    return pl.pallas_call(
        whole_kernel,
        in_specs=[pl.BlockSpec(memory_space=pltpu.HBM)] * 4,
        out_shape=[
            jax.ShapeDtypeStruct((FIELDS, rows, cols), f32),
            jax.ShapeDtypeStruct((rows, LANES), f32),
        ],
        scratch_shapes=[
            pltpu.SMEM(thickness.shape, f32),
            pltpu.VMEM((rows, cols), jnp.int32),
            pltpu.VMEM(tendency.shape, tendency.dtype),
            pltpu.SemaphoreType.DMA((2,)),
            pltpu.SemaphoreType.DMA((rows // CHUNK,)),
            pltpu.SemaphoreType.DMA((rows // CHUNK,)),
        ],
        cost_estimate=integrate_cost(tendency, rows),
        compiler_params=pltpu.CompilerParams(vmem_limit_bytes=WHOLE_BYTES),
        name="whole",
    )(thickness, level_count, inertia, tendency)


def folded_rows(tall):
    return (tall - 2 * ROWS) // FOLD + 2 * ROWS


def fold(values, shift, first, last):
    size = folded_rows(values.shape[0])
    lane = lanes_of((size, LANES))
    folded = jnp.zeros((size, LANES), jnp.float32)
    for part in range(FOLD):
        start = part * (size - 2 * ROWS)
        rows = turn(values[start : start + size], part * PITCH + shift)
        here = (lane >= part * PITCH + first) & (lane < part * PITCH + last)
        folded = jnp.where(here, rows, folded)
    return folded


def edges_kernel(side_ref, near_ref, far_ref, near_out_ref, far_out_ref):
    even_lon = is_even("lon")
    near = pack_edges(near_ref, slice(None))
    far = pack_edges(far_ref, slice(None))
    north, south = sides(near, far)
    packed = jnp.concatenate([north, side_ref[...], south], axis=0)
    west = fold(packed, 0, 0, PITCH)
    east = fold(packed, -HALF, 0, PITCH)
    near_out_ref[...] = jnp.where(even_lon, east, west)
    far_out_ref[...] = jnp.where(even_lon, west, east)


def edges(side, near, far):
    rows = side.shape[0] + 2 * ROWS
    message = jax.ShapeDtypeStruct((folded_rows(rows), LANES), jnp.float32)
    return pl.pallas_call(
        edges_kernel,
        out_shape=[message, message],
        compiler_params=pltpu.CompilerParams(vmem_limit_bytes=VMEM_BYTES),
        name="edges",
    )(side, near, far)


def smooth(field):
    rows, cols = field.shape
    tall = field + 0.5 * (pltpu.roll(field, 1, 0) + pltpu.roll(field, rows - 1, 0))
    return tall + 0.5 * (pltpu.roll(tall, 1, 1) + pltpu.roll(tall, cols - 1, 1))


def basis(first, second, depth, inertia):
    tall, wide = first.shape
    own = slice(ROWS, tall - ROWS)
    inside = inertia > 0.0
    east_west = pltpu.roll(first, wide - 1, 1) - pltpu.roll(first, 1, 1)
    north_south = pltpu.roll(second, tall - 1, 0) - pltpu.roll(second, 1, 0)
    scaled = jnp.where(depth > 0.0, 0.5 * (east_west + north_south), 0.0)
    diag = inertia + 2.0 * depth + smooth(depth)
    inverse = jnp.where(inside, 1.0 / jnp.where(inside, diag, 1.0), 0.0)
    mws = [scaled[own]]
    ws = []
    vector = scaled * inverse
    for step in range(STEPS):
        ws.append(vector[own])
        weighed = depth * vector
        scaled = depth * smooth(vector) + smooth(weighed) - 2.0 * weighed
        mws.append(scaled[own])
        if step + 1 < STEPS:
            vector = scaled * inverse
    return ws, mws


def moments(ws, mws, mask):
    ws = [jnp.where(mask, values, 0.0) for values in ws]
    images = [mws[place] - mws[place + 1] for place in range(STEPS)]
    pairs = [ws[place] * mws[0] for place in range(STEPS)]
    for low in range(STEPS):
        for high in range(low, STEPS):
            pairs.append(ws[low] * images[high])
    lines = []
    for product in pairs:
        line = jnp.sum(product, axis=0, keepdims=True)
        total = line[:, :LANES]
        for start in range(LANES, line.shape[1], LANES):
            total = total + line[:, start : start + LANES]
        total = total + turn(total, HALF)
        lines.append(total + turn(total, QUARTER))
    quarter = lanes_of((1, LANES)) // QUARTER
    packed = []
    for start in range(0, len(lines), 4):
        row = jnp.zeros((1, LANES), jnp.float32)
        for place, line in enumerate(lines[start : start + 4]):
            row = jnp.where(quarter == place, line, row)
        packed.append(row)
    packed.append(jnp.zeros((ROWS - len(packed), LANES), jnp.float32))
    return jnp.concatenate(packed, axis=0)


def interior_kernel(
    fields_ref,
    near_ref,
    far_ref,
    w_ref,
    mw_ref,
    near_strip_ref,
    far_strip_ref,
    sums_ref,
    forcing_ref,
):
    forcing_ref[...] = fields_ref[:2]
    cols = fields_ref.shape[2]
    even = is_even("lon")
    padded = []
    for place in range(FIELDS):
        north, south = sides(near_ref[place], far_ref[place])
        values = jnp.concatenate([north, fields_ref[place], south], axis=0)
        west = fold(values[:, :LANES], RIM, RIM, 3 * RIM)
        east = fold(values[:, cols - LANES :], 2 * RIM, 0, 2 * RIM)
        near_strip_ref[place] = jnp.where(even, east, west)
        far_strip_ref[place] = jnp.where(even, west, east)
        padded.append(values)
    ws, mws = basis(*padded)
    for place, values in enumerate(ws):
        w_ref[place] = values
    for place, values in enumerate(mws):
        mw_ref[place] = values
    lane = lanes_of(ws[0].shape)
    sums_ref[...] = moments(ws, mws, (lane >= RIM) & (lane < cols - RIM))


def interior(fields, near, far):
    _, rows, cols = fields.shape
    f32 = jnp.float32
    return pl.pallas_call(
        interior_kernel,
        out_shape=[
            jax.ShapeDtypeStruct((STEPS, rows, cols), f32),
            jax.ShapeDtypeStruct((STEPS + 1, rows, cols), f32),
            jax.ShapeDtypeStruct((FIELDS, folded_rows(rows + 2 * ROWS), LANES), f32),
            jax.ShapeDtypeStruct((FIELDS, folded_rows(rows + 2 * ROWS), LANES), f32),
            jax.ShapeDtypeStruct((ROWS, LANES), f32),
            jax.ShapeDtypeStruct((2, rows, cols), f32),
        ],
        compiler_params=pltpu.CompilerParams(vmem_limit_bytes=VMEM_BYTES),
        cost_estimate=pl.CostEstimate(
            flops=300000 * rows * cols, bytes_accessed=64 * rows * cols, transcendentals=0
        ),
        name="interior",
    )(fields, near, far)


def strip_kernel(near, strip_in_ref, message_ref, before_ref, w_ref, mw_ref, sums_ref):
    even = is_even("lon")
    eastern = even if near else jnp.logical_not(even)
    message = message_ref[...]
    column = lax.rem(lanes_of(message.shape), PITCH)
    first = jnp.where(eastern, 2 * RIM, 0)
    halo = (column >= first) & (column < first + RIM)
    padded = []
    for place in range(FIELDS):
        at = place * RIM
        beyond = jnp.where(eastern, turn(message, 2 * RIM - at), turn(message, -at))
        padded.append(jnp.where(halo, beyond, strip_in_ref[place]))
    ws, mws = basis(*padded)
    for place, values in enumerate(ws):
        w_ref[place] = values
    for place, values in enumerate(mws):
        mw_ref[place] = values
    column = lax.rem(lanes_of(ws[0].shape), PITCH)
    edge = (column >= RIM) & (column < 2 * RIM)
    sums_ref[...] = before_ref[...] + moments(ws, mws, edge)


def strip(near, strip_in, message, before):
    rows = strip_in.shape[1] - 2 * ROWS
    f32 = jnp.float32
    return pl.pallas_call(
        functools.partial(strip_kernel, near),
        out_shape=[
            jax.ShapeDtypeStruct((STEPS, rows, LANES), f32),
            jax.ShapeDtypeStruct((STEPS + 1, rows, LANES), f32),
            jax.ShapeDtypeStruct((ROWS, LANES), f32),
        ],
        compiler_params=pltpu.CompilerParams(vmem_limit_bytes=VMEM_BYTES),
        cost_estimate=pl.CostEstimate(
            flops=300 * rows * LANES, bytes_accessed=64 * rows * LANES, transcendentals=0
        ),
        name="near_strip" if near else "far_strip",
    )(strip_in, message, before)


def power(exponent):
    size = jnp.abs(exponent)
    value = jnp.ones(exponent.shape, jnp.float32)
    for bit in range(7):
        up, down = 2.0 ** (1 << bit), 2.0 ** -(1 << bit)
        factor = jnp.where(exponent < 0, down, up)
        value = value * jnp.where((size >> bit) & 1 == 1, factor, 1.0)
    return value


def exponent_of(size):
    bits = jnp.ceil(jnp.log2(jnp.maximum(size, 2.0**-100)))
    return jnp.clip(bits, -100.0, 100.0).astype(jnp.int32)


def nearest(values):
    return jnp.floor(values + 0.5)


def place_kernel(owner_ref, fields_ref, sent_ref, scale_ref):
    count = owner_ref.shape[0]
    span = fields_ref.shape[1] // count
    sent_ref[...] = jnp.zeros(sent_ref.shape, jnp.int16)
    scale_ref[...] = jnp.zeros(scale_ref.shape, jnp.float32)
    for block in range(count):
        target = owner_ref[block]

        @pl.when(target >= 0)
        def _(block=block, target=target):
            rows = slice(block * span, (block + 1) * span)
            for half in range(fields_ref.shape[2] // LANES):
                cols = slice(half * LANES, (half + 1) * LANES)
                pieces = [fields_ref[0, rows, cols], fields_ref[1, rows, cols]]
                values = jnp.concatenate(pieces, axis=0)
                bits = exponent_of(jnp.max(jnp.abs(values), axis=0, keepdims=True))
                whole = jnp.clip(nearest(values * power(15 - bits)), -32767.0, 32767.0)
                there = slice(2 * span * half, 2 * span * (half + 1))
                sent_ref[target, there] = whole.astype(jnp.int32).astype(jnp.int16)
                scale_ref[target, half : half + 1] = bits.astype(jnp.float32)


def place(owner, fields, lon_count):
    _, rows, cols = fields.shape
    span = rows // owner.shape[0]
    return pl.pallas_call(
        place_kernel,
        in_specs=[
            pl.BlockSpec(memory_space=pltpu.SMEM),
            pl.BlockSpec(memory_space=pltpu.VMEM),
        ],
        out_shape=[
            jax.ShapeDtypeStruct((lon_count, cols // LANES * 2 * span + TAIL, LANES), jnp.int16),
            jax.ShapeDtypeStruct((lon_count, ROWS, LANES), jnp.float32),
        ],
        compiler_params=pltpu.CompilerParams(vmem_limit_bytes=VMEM_BYTES),
        cost_estimate=pl.CostEstimate(
            flops=60 * rows * cols, bytes_accessed=12 * rows * cols, transcendentals=0
        ),
        name="place",
    )(owner, fields)


def seal_kernel(sums_ref, other_ref, scale_ref, tail_ref):
    sums = sums_ref[:SUM_ROWS] + other_ref[:SUM_ROWS]
    bits = exponent_of(jnp.abs(sums))
    scaled = sums * power(-bits) * 2.0**14
    high = nearest(scaled)
    low = nearest((scaled - high) * 2.0**15)
    parts = jnp.concatenate([bits.astype(jnp.float32), high, low], axis=0)
    for slot in range(tail_ref.shape[0]):
        tile = jnp.concatenate([parts, scale_ref[slot, : TAIL - 3 * SUM_ROWS]], axis=0)
        tail_ref[slot] = tile.astype(jnp.int32).astype(jnp.int16)


def seal(sums, other, scale):
    return pl.pallas_call(
        seal_kernel,
        out_shape=jax.ShapeDtypeStruct((scale.shape[0], TAIL, LANES), jnp.int16),
        compiler_params=pltpu.CompilerParams(vmem_limit_bytes=VMEM_BYTES),
        name="seal",
    )(sums, other, scale)


def combine_kernel(
    arrived_ref,
    w_ref,
    mw_ref,
    near_w_ref,
    near_mw_ref,
    far_w_ref,
    far_mw_ref,
    pressure_hbm,
    residual_hbm,
    held_hbm,
    pressure_ref,
    residual_ref,
    held_ref,
    held_sem,
    sems,
):
    rows = held_ref.shape[1]
    slots = held_ref.shape[0]
    tails = []
    for slot in range(slots):
        tails.append(arrived_ref[slot, arrived_ref.shape[1] - TAIL :].astype(jnp.int32))
    scales = jnp.concatenate([tail[3 * SUM_ROWS :] for tail in tails], axis=0)
    scales = power(scales - 15)
    exponents = jnp.concatenate([tail[:SUM_ROWS] for tail in tails], axis=0)
    high = jnp.concatenate([tail[SUM_ROWS : 2 * SUM_ROWS] for tail in tails], axis=0)
    low = jnp.concatenate([tail[2 * SUM_ROWS : 3 * SUM_ROWS] for tail in tails], axis=0)
    digits = high.astype(jnp.float32) + low.astype(jnp.float32) * 2.0**-15
    sums = digits * power(exponents - 14)
    packed = sums[:SUM_ROWS]
    for slot in range(1, slots):
        packed = packed + sums[slot * SUM_ROWS : (slot + 1) * SUM_ROWS]
    spare = TAIL - 3 * SUM_ROWS
    for slot in range(slots):
        for half in range(held_ref.shape[2] // LANES):
            at = slot * spare + half
            whole = arrived_ref[slot, half * rows : (half + 1) * rows].astype(jnp.int32)
            whole = whole.astype(jnp.float32) * scales[at : at + 1]
            held_ref[slot, :, half * LANES : (half + 1) * LANES] = whole
    held_copy = pltpu.make_async_copy(held_ref, held_hbm, held_sem)
    held_copy.start()
    quarter = lanes_of(packed.shape) // QUARTER
    totals = [
        jnp.sum(jnp.where(quarter == place, packed, 0.0), axis=1, keepdims=True)
        for place in range(4)
    ]
    entry = lambda place: totals[place % 4][place // 4 : place // 4 + 1, :]
    right = [entry(place) for place in range(STEPS)]
    matrix = {}
    place = STEPS
    for low in range(STEPS):
        for high in range(low, STEPS):
            matrix[low, high] = entry(place)
            place += 1
    for pivot in range(STEPS):
        inverse = 1.0 / matrix[pivot, pivot]
        for row in range(pivot + 1, STEPS):
            factor = matrix[pivot, row] * inverse
            for col in range(row, STEPS):
                matrix[row, col] = matrix[row, col] - factor * matrix[pivot, col]
            right[row] = right[row] - factor * right[pivot]
        matrix[pivot, pivot] = inverse
    for pivot in reversed(range(STEPS)):
        for col in range(pivot + 1, STEPS):
            right[pivot] = right[pivot] - matrix[pivot, col] * right[col]
        right[pivot] = right[pivot] * matrix[pivot, pivot]

    def results(w_ref, mw_ref, part):
        pressure = right[0] * w_ref[0, part]
        residual = mw_ref[0, part] - right[0] * (mw_ref[0, part] - mw_ref[1, part])
        for place in range(1, STEPS):
            pressure = pressure + right[place] * w_ref[place, part]
            image = mw_ref[place, part] - mw_ref[place + 1, part]
            residual = residual - right[place] * image
        return pressure, residual

    rows, cols = pressure_ref.shape
    even = is_even("lon")
    near = results(near_w_ref, near_mw_ref, slice(None))
    far = results(far_w_ref, far_mw_ref, slice(None))
    west = [jnp.where(even, b, a) for a, b in zip(near, far)]
    east = [jnp.where(even, a, b) for a, b in zip(near, far)]

    def unfold(values, parts, lane):
        return jnp.concatenate([turn(values, lane - RIM - part * PITCH) for part in parts], axis=0)

    copies = []
    for piece in range(PIECES):
        part = slice(piece * rows // PIECES, (piece + 1) * rows // PIECES)
        inner = results(w_ref, mw_ref, part)
        parts = range(piece * FOLD // PIECES, (piece + 1) * FOLD // PIECES)
        lane = lanes_of((rows // PIECES, LANES))
        for field, (out_ref, out_hbm, inside) in enumerate(
            zip((pressure_ref, residual_ref), (pressure_hbm, residual_hbm), inner)
        ):
            border = unfold(west[field], parts, 0)
            out_ref[part, :LANES] = jnp.where(lane < RIM, border, inside[:, :LANES])
            if cols > 2 * LANES:
                out_ref[part, LANES : cols - LANES] = inside[:, LANES : cols - LANES]
            border = unfold(east[field], parts, LANES - RIM)
            out_ref[part, cols - LANES :] = jnp.where(
                lane >= LANES - RIM, border, inside[:, cols - LANES :]
            )
            there = pl.ds(piece * rows // PIECES, rows // PIECES)
            copy = pltpu.make_async_copy(
                out_ref.at[there], out_hbm.at[there], sems.at[field, piece]
            )
            copy.start()
            copies.append(copy)
    held_copy.wait()
    for copy in copies:
        copy.wait()


def combine(arrived, w, mw, near, far):
    rows, cols = w.shape[1:]
    shape = jax.ShapeDtypeStruct((rows, cols), jnp.float32)
    held = (arrived.shape[0], (arrived.shape[1] - TAIL) * LANES // cols, cols)
    return pl.pallas_call(
        combine_kernel,
        out_shape=[shape, shape, jax.ShapeDtypeStruct(held, jnp.float32)],
        out_specs=[pl.BlockSpec(memory_space=pltpu.HBM)] * 3,
        scratch_shapes=[
            pltpu.VMEM((rows, cols), jnp.float32),
            pltpu.VMEM((rows, cols), jnp.float32),
            pltpu.VMEM(held, jnp.float32),
            pltpu.SemaphoreType.DMA,
            pltpu.SemaphoreType.DMA((2, PIECES)),
        ],
        compiler_params=pltpu.CompilerParams(vmem_limit_bytes=VMEM_BYTES),
        name="combine",
    )(arrived, w, mw, *near, *far)


def exchange(values, axis, distance):
    pairs = [(place, place ^ distance) for place in range(lax.axis_size(axis))]
    return lax.ppermute(values, axis, pairs)


def swap(values, axis, first):
    count = lax.axis_size(axis)
    pairs = []
    for place in range(first, count, 2):
        beside = (place + 1) % count
        pairs += [(place, beside), (beside, place)]
    return lax.ppermute(values, axis, pairs)


def on_device(tendency, thickness, level_count, block_mask, owner, inertia):
    lat_count = lax.axis_size("lat")
    lon_count = lax.axis_size("lon")
    inputs = (tendency, thickness, level_count, inertia)
    near, far = integrate_outer(*inputs)
    fields, side = integrate(*inputs)
    near = swap(near, "lat", 0)
    far = swap(far, "lat", 1)
    near_edge, far_edge = edges(side, near, far)
    far_edge = swap(far_edge, "lon", 1)
    near_edge = swap(near_edge, "lon", 0)
    w, mw, near_strip, far_strip, sums, forcing = interior(fields, near, far)
    *near_results, sums = strip(True, near_strip, near_edge, sums)
    *far_results, sums = strip(False, far_strip, far_edge, sums)
    sent, scale = place(owner[:, 0], forcing, lon_count)
    shift = 1
    while 2 * shift < lat_count:
        sums = sums + exchange(sums, "lat", shift)
        shift *= 2
    tail = seal(sums, exchange(sums, "lat", shift), scale)
    sent = lax.dynamic_update_slice(sent, tail, (0, sent.shape[1] - TAIL, 0))
    arrived = lax.all_to_all(sent, "lon", split_axis=0, concat_axis=0, tiled=True)
    pressure, residual, held = combine(arrived, w, mw, near_results, far_results)
    held = held.reshape((1, 1, lon_count, 2, held.shape[1] // 2, held.shape[2]))
    return (held, pressure, residual)


def solution(mesh):
    return jax.shard_map(
        on_device,
        mesh=mesh,
        in_specs=(
            P(None, None, "lat", "lon"),
            P(),
            P("lat", "lon"),
            P("lat", "lon"),
            P("lat", "lon"),
            P("lat", "lon"),
        ),
        out_specs=(P("lat", "lon", None, None, None, None), P("lat", "lon"), P("lat", "lon")),
        check_vma=False,
    )
```
